32 devices in a mesh: dp: 4 (over z), context: 4 (over y, x), tensor: 2 (over core).
Axes of the slice: x: 2, y: 2, z: 4, core: 2. Of those that a mesh axis runs over, the one named last changes fastest.
Arguments:
- inputs: bfloat16 [8192, 5376], P(('dp', 'context')), may hold values from -8 to 8
- queries: bfloat16 [8192, 2048], P(('dp', 'context'), 'tensor'), may hold values from -8 to 8
- key_states: bfloat16 [8192, 1024], P(('dp', 'context'), 'tensor'), may hold values from -8 to 8
- value_states: bfloat16 [8192, 1024], P(('dp', 'context'), 'tensor'), may hold values from -6 to 6
- out_grad: bfloat16 [8192, 5376], P(('dp', 'context')), may hold values from -8 to 8
- positions: int32 [8192], P(('dp', 'context')), may hold values from 0 to 10239, as said below
- w_query: bfloat16 [5376, 2048], P(None, 'tensor'), may hold values from -0.078125 to 0.078125
- w_key: bfloat16 [5376, 1024], P(None, 'tensor'), may hold values from -0.078125 to 0.078125
- w_value: bfloat16 [5376, 1024], P(None, 'tensor'), may hold values from -0.078125 to 0.078125
- w_output: bfloat16 [5376, 2048], P(None, 'tensor'), may hold values from -0.125 to 0.125
Outputs:
- input_grad: bfloat16 [8192, 5376], P(('dp', 'context', 'tensor'))
- grad_query: float32 [5376, 2048], P(('dp', 'context'), 'tensor')
- grad_key: float32 [5376, 1024], P(('dp', 'context'), 'tensor')
- grad_value: float32 [5376, 1024], P(('dp', 'context'), 'tensor')
- grad_output: float32 [5376, 2048], P(('dp', 'context'), 'tensor')
The draws below stay inside these ranges and needn't reach their ends.
Inputs may be any that keep to these rules, and one draw needn't show every extreme that they name: Within a document positions rise by one from token to token; a position of 0 starts a new document; the first document of each replica's 2048 tokens may have begun before them.
All inputs are finite; a program needn't handle non-finite values.
Results may differ from the reference program's by a relative error of at most 0.02.
Values may be sent and summed in bfloat16 or wider, within the bound.
No kernel may reach another device: no remote copies, remote signals or barrier semaphores. Data moves between devices by JAX's collectives and lax.ppermute only.
A program may use at most 192 MiB of HBM per device.

```python
import jax
import jax.numpy as jnp
from jax import lax

D = 5376
H = 16
KVH = 8
HD = 128
W = 1024
QSCALAR = 168
SEG = 2048
TOKENS = 8192


def build_positions(key):
    base = jax.random.fold_in(key, 7)
    replicas = TOKENS // SEG
    replica_index = jnp.arange(replicas, dtype=jnp.int32)[:, None]
    index = jnp.broadcast_to(jnp.arange(SEG, dtype=jnp.int32)[None, :], (replicas, SEG))
    breaks = jax.random.randint(jax.random.fold_in(base, 1), (replicas, SEG), 0, W) == 0
    breaks = breaks & (replica_index >= 1)
    forced = (replica_index == replicas - 1) & (index == SEG // 2)
    breaks = breaks | forced
    offsets = jax.random.randint(jax.random.fold_in(base, 2), (replicas,), 0, 8 * W)
    offsets = offsets.at[0].set(8 * W)
    marker = jnp.where(breaks, index, -16 * W)
    opening = jnp.where(breaks[:, 0], 0, -offsets).astype(jnp.int32)
    marker = marker.at[:, 0].set(opening)
    latest = lax.cummax(marker, axis=1)
    return (index - latest).reshape(TOKENS).astype(jnp.int32)


def draw_positions(key, part):
    return build_positions(key)


def draw_key_states(key, part):
    base = jax.random.normal(jax.random.fold_in(key, 21), (TOKENS, KVH * HD), jnp.float32)
    return jnp.clip(base, -6.0, 6.0).astype(jnp.bfloat16)


def draw_queries(key, part):
    base = jax.random.normal(jax.random.fold_in(key, 31), (TOKENS, H * HD), jnp.float32)
    return jnp.clip(base, -6.0, 6.0).astype(jnp.bfloat16)


def spiked(values, key, source, target, blocks, factor):
    def block_of(axis_at):
        return (jnp.arange(values.shape[axis_at]) // (values.shape[axis_at] // blocks)).reshape((-1,) + (1,) * (values.ndim - 1 - axis_at))

    first = jax.random.permutation(key, blocks)[block_of(target)]
    far = (block_of(target) + blocks // 2) % blocks
    return jnp.where((block_of(source) == first) | (block_of(source) == far), factor * values, values)


def block_scale(stream_key, extent, cuts, low, high):
    factor_of = 1.0
    for dim, blocks in cuts:
        draws = jax.random.uniform(jax.random.fold_in(jax.random.fold_in(stream_key, 6), dim), (blocks,), jnp.float32, low / len(cuts), high / len(cuts))
        factor_of = factor_of * jnp.repeat(jnp.exp(draws), extent[dim] // blocks).reshape((-1,) + (1,) * (len(extent) - 1 - dim))
    return factor_of


def normal_values(key, dims, scale, reach, cuts=(), kind=jnp.bfloat16):
    result = jax.random.normal(key, dims, jnp.float32) * scale
    if len(cuts) > 0:
        result = block_scale(key, dims, cuts, -0.22, 0.18) * result
    return jnp.clip(result, min=-reach, max=reach).astype(kind)


def bell_draw_with(own_key, shape, scale, reach, shards, heavy, kind=jnp.bfloat16):
    values = scale * jax.random.normal(own_key, shape, jnp.float32)
    if shards:
        values = values * block_scale(own_key, shape, shards, -0.22, 0.18)
    return jnp.clip(spiked(values, jax.random.fold_in(own_key, 3), *heavy), -reach, reach).astype(kind)


def setup_inputs(seed: int = 0) -> dict:
    arg_keys = jax.random.split(jax.random.key(seed), 11)
    inputs = bell_draw_with(arg_keys[0], (TOKENS, D), 1.0, 8.0, ((0, 16),), (0, 1, 16, 2.0))
    queries = draw_queries(jax.random.fold_in(arg_keys[10], 71), 0)
    key_states = draw_key_states(jax.random.fold_in(arg_keys[10], 71), 0)
    value_states = normal_values(arg_keys[3], (TOKENS, KVH * HD), 1.0, 6.0, ((0, 16), (1, 2)))
    out_grad = bell_draw_with(arg_keys[4], (TOKENS, D), 1.0, 8.0, ((0, 16),), (0, 1, 16, 2.0))
    positions = draw_positions(jax.random.fold_in(arg_keys[10], 71), 0)
    w_query = normal_values(arg_keys[6], (D, H * HD), D ** -0.5, 0.078125, ((1, 2),))
    w_key = normal_values(arg_keys[7], (D, KVH * HD), D ** -0.5, 0.078125, ((1, 2),))
    w_value = normal_values(arg_keys[8], (D, KVH * HD), D ** -0.5, 0.078125, ((1, 2),))
    w_output = normal_values(arg_keys[9], (D, H * HD), (H * HD) ** -0.5, 0.125, ((1, 2),))
    return dict(inputs=inputs, queries=queries, key_states=key_states, value_states=value_states, out_grad=out_grad, positions=positions, w_query=w_query, w_key=w_key, w_value=w_value, w_output=w_output)


def rotate_back(grads, places):
    count = grads.shape[0]
    half = HD // 2
    index = jnp.arange(half, dtype=jnp.float32)
    freq = jnp.power(jnp.float32(10000.0), index * (-2.0 / HD))
    angle = places.astype(jnp.float32)[:, None] * freq[None, :]
    cosine = jnp.cos(angle)[:, None, :]
    sine = jnp.sin(angle)[:, None, :]
    split = grads.reshape(count, -1, 2, half)
    first = split[:, :, 0, :]
    second = split[:, :, 1, :]
    upper = first * cosine + second * sine
    lower = second * cosine - first * sine
    return jnp.stack([upper, lower], axis=2).reshape(count, -1)


def group_backward(query_group, key_group, value_group, dattn_group, allowed):
    scale = QSCALAR ** -0.5
    query_wide = query_group.astype(jnp.float32)
    key_wide = key_group.astype(jnp.float32)
    value_wide = value_group.astype(jnp.float32)
    dattn_wide = dattn_group.astype(jnp.float32)
    scores = jnp.einsum("gqd,kd->gqk", query_wide, key_wide) * scale
    scores = jnp.where(allowed[None], scores, -1e30)
    top = jnp.max(scores, axis=-1, keepdims=True)
    weights = jnp.exp(scores - top)
    probs = weights / jnp.sum(weights, axis=-1, keepdims=True)
    probs_half = probs.astype(jnp.bfloat16)
    attn = jnp.einsum("gqk,kd->gqd", probs_half.astype(jnp.float32), value_wide).astype(jnp.bfloat16)
    dprobs = jnp.einsum("gqd,kd->gqk", dattn_wide, value_wide)
    delta = jnp.sum(dattn_wide * attn.astype(jnp.float32), axis=-1, keepdims=True)
    dscores = (probs * (dprobs - delta) * scale).astype(jnp.bfloat16)
    dscores_wide = dscores.astype(jnp.float32)
    query_grad = jnp.einsum("gqk,kd->gqd", dscores_wide, key_wide)
    key_grad = jnp.einsum("gqk,gqd->kd", dscores_wide, query_wide)
    value_grad = jnp.einsum("gqk,gqd->kd", probs_half.astype(jnp.float32), dattn_wide)
    return attn, query_grad, key_grad, value_grad


def reference(inputs, queries, key_states, value_states, out_grad, positions, w_query, w_key, w_value, w_output):
    group = H // KVH
    index = jnp.arange(SEG, dtype=jnp.int32)
    input_parts = []
    grad_sums = None
    for replica in range(TOKENS // SEG):
        first_row = replica * SEG
        input_rows = inputs[first_row:first_row + SEG]
        query_rows = queries[first_row:first_row + SEG]
        key_rows = key_states[first_row:first_row + SEG]
        value_rows = value_states[first_row:first_row + SEG]
        grad_rows = out_grad[first_row:first_row + SEG]
        places = positions[first_row:first_row + SEG]
        starts = index - places
        allowed = (index[None, :] <= index[:, None]) & (index[:, None] - index[None, :] < W) & (index[None, :] >= starts[:, None])
        dattn = jnp.dot(grad_rows, w_output, preferred_element_type=jnp.float32).astype(jnp.bfloat16)
        query_heads = query_rows.reshape(SEG, KVH, group, HD).transpose(1, 2, 0, 3)
        dattn_heads = dattn.reshape(SEG, KVH, group, HD).transpose(1, 2, 0, 3)
        key_heads = key_rows.reshape(SEG, KVH, HD).transpose(1, 0, 2)
        value_heads = value_rows.reshape(SEG, KVH, HD).transpose(1, 0, 2)

        def one_group(parts):
            return group_backward(parts[0], parts[1], parts[2], parts[3], allowed)

        attn, query_grad, key_grad, value_grad = lax.map(one_group, (query_heads, key_heads, value_heads, dattn_heads))
        attn_flat = attn.transpose(2, 0, 1, 3).reshape(SEG, H * HD)
        query_flat = query_grad.transpose(2, 0, 1, 3).reshape(SEG, H * HD)
        key_flat = key_grad.transpose(1, 0, 2).reshape(SEG, KVH * HD)
        value_flat = value_grad.transpose(1, 0, 2).reshape(SEG, KVH * HD)
        query_lin = rotate_back(query_flat, places).astype(jnp.bfloat16)
        key_lin = rotate_back(key_flat, places).astype(jnp.bfloat16)
        value_half = value_flat.astype(jnp.bfloat16)
        input_grad = jnp.dot(query_lin, w_query.T, preferred_element_type=jnp.float32)
        input_grad = input_grad + jnp.dot(key_lin, w_key.T, preferred_element_type=jnp.float32)
        input_grad = input_grad + jnp.dot(value_half, w_value.T, preferred_element_type=jnp.float32)
        input_parts.append(input_grad.astype(jnp.bfloat16))
        terms = (jnp.dot(input_rows.T, query_lin, preferred_element_type=jnp.float32),
                 jnp.dot(input_rows.T, key_lin, preferred_element_type=jnp.float32),
                 jnp.dot(input_rows.T, value_half, preferred_element_type=jnp.float32),
                 jnp.dot(grad_rows.T, attn_flat, preferred_element_type=jnp.float32))
        if grad_sums is None:
            grad_sums = terms
        else:
            grad_sums = tuple(old + new for old, new in zip(grad_sums, terms))
    return (jnp.concatenate(input_parts, axis=0), grad_sums[0], grad_sums[1], grad_sums[2], grad_sums[3])
```

```python
import functools

import jax
import jax.numpy as jnp
from jax import lax
from jax.experimental import pallas as pl
from jax.experimental.pallas import tpu as pltpu
from jax.sharding import PartitionSpec as P

HD = 128
W = 1024
QSCALAR = 168


def shifted(x, axis, by):
    count = lax.axis_size(axis)
    pairs = [(i, i + by) for i in range(count) if 0 <= i + by < count]
    return lax.ppermute(x, axis, pairs)


def rotate_back(grads, places):
    count = grads.shape[0]
    half = HD // 2
    index = jnp.arange(half, dtype=jnp.float32)
    freq = jnp.power(jnp.float32(10000.0), index * (-2.0 / HD))
    angle = places.astype(jnp.float32)[:, None] * freq[None, :]
    cosine = jnp.cos(angle)[:, None, :]
    sine = jnp.sin(angle)[:, None, :]
    split = grads.reshape(count, -1, 2, half)
    first = split[:, :, 0, :]
    second = split[:, :, 1, :]
    upper = first * cosine + second * sine
    lower = second * cosine - first * sine
    return jnp.stack([upper, lower], axis=2).reshape(count, -1)


def contract_rows(left, right):
    return lax.dot_general(
        left, right, (((0,), (0,)), ((), ())), preferred_element_type=jnp.float32
    )


def contract_cols(left, right):
    return lax.dot_general(
        left, right, (((1,), (1,)), ((), ())), preferred_element_type=jnp.float32
    )


def banded(
    inputs,
    queries,
    key_states,
    value_states,
    out_grad,
    positions,
    w_query,
    w_key,
    w_value,
    w_output,
):
    count = queries.shape[0]
    head_cols = queries.shape[1]
    kv_cols = key_states.shape[1]
    kv_here = kv_cols // HD
    group = head_cols // kv_cols
    scale = QSCALAR ** (-0.5)
    block = lax.axis_index("context")
    blocks = lax.axis_size("context")
    reach = min((W + count - 2) // count, blocks - 1)
    span = (reach + 1) * count
    key_pieces = []
    value_pieces = []
    for back in range(reach, 0, -1):
        earlier_keys, earlier_values = shifted((key_states, value_states), "context", back)
        key_pieces.append(earlier_keys)
        value_pieces.append(earlier_values)
    band_keys = jnp.concatenate(key_pieces + [key_states], axis=0)
    band_values = jnp.concatenate(value_pieces + [value_states], axis=0)
    query_index = block * count + jnp.arange(count, dtype=jnp.int32)
    key_index = (block - reach) * count + jnp.arange(span, dtype=jnp.int32)
    doc_start = query_index - positions
    allowed = (key_index[None, :] <= query_index[:, None]) & (
        query_index[:, None] - key_index[None, :] < W
    )
    allowed = allowed & (key_index[None, :] >= doc_start[:, None]) & (key_index[None, :] >= 0)
    query_heads = queries.reshape(count, kv_here, group, HD)
    key_heads = band_keys.reshape(span, kv_here, HD)
    value_heads = band_values.reshape(span, kv_here, HD)
    scores = (
        jnp.einsum("qhgd,khd->hgqk", query_heads, key_heads, preferred_element_type=jnp.float32)
        * scale
    )
    scores = jnp.where(allowed, scores, -1e30)
    top = jnp.max(scores, axis=-1, keepdims=True)
    weights = jnp.exp(scores - top)
    probs = weights / jnp.sum(weights, axis=-1, keepdims=True)
    probs_half = probs.astype(jnp.bfloat16)
    attn = jnp.einsum(
        "hgqk,khd->qhgd", probs_half, value_heads, preferred_element_type=jnp.float32
    ).astype(jnp.bfloat16)
    attn_flat = attn.reshape(count, head_cols)
    dattn = jnp.dot(out_grad, w_output, preferred_element_type=jnp.float32).astype(jnp.bfloat16)
    dattn_heads = dattn.reshape(count, kv_here, group, HD)
    dprobs = jnp.einsum(
        "qhgd,khd->hgqk", dattn_heads, value_heads, preferred_element_type=jnp.float32
    )
    delta = jnp.sum(dattn_heads.astype(jnp.float32) * attn.astype(jnp.float32), axis=-1)
    delta = jnp.transpose(delta, (1, 2, 0))[..., None]
    dscores = (probs * (dprobs - delta) * scale).astype(jnp.bfloat16)
    query_grad = jnp.einsum(
        "hgqk,khd->qhgd", dscores, key_heads, preferred_element_type=jnp.float32
    ).reshape(count, head_cols)
    band_key_grad = jnp.einsum(
        "hgqk,qhgd->khd", dscores, query_heads, preferred_element_type=jnp.float32
    ).reshape(span, kv_cols)
    band_value_grad = jnp.einsum(
        "hgqk,qhgd->khd", probs_half, dattn_heads, preferred_element_type=jnp.float32
    ).reshape(span, kv_cols)
    key_grad = band_key_grad[reach * count :]
    value_grad = band_value_grad[reach * count :]
    for back in range(1, reach + 1):
        first_row = (reach - back) * count
        sent_keys, sent_values = shifted(
            (
                band_key_grad[first_row : first_row + count],
                band_value_grad[first_row : first_row + count],
            ),
            "context",
            -back,
        )
        key_grad = key_grad + sent_keys
        value_grad = value_grad + sent_values
    query_lin = rotate_back(query_grad, positions).astype(jnp.bfloat16)
    key_lin = rotate_back(key_grad, positions).astype(jnp.bfloat16)
    value_half = value_grad.astype(jnp.bfloat16)
    total = contract_cols(query_lin, w_query)
    total = total + contract_cols(key_lin, w_key)
    total = total + contract_cols(value_half, w_value)
    input_grad = lax.psum_scatter(total, "tensor", scatter_dimension=0, tiled=True).astype(
        jnp.bfloat16
    )
    terms = (
        contract_rows(inputs, query_lin),
        contract_rows(inputs, key_lin),
        contract_rows(inputs, value_half),
        contract_rows(out_grad, attn_flat),
    )
    summed = (
        lax.psum_scatter(
            terms[0].astype(jnp.bfloat16), ("dp", "context"), scatter_dimension=0, tiled=True
        ).astype(jnp.float32),
        lax.psum_scatter(
            terms[1].astype(jnp.bfloat16), ("dp", "context"), scatter_dimension=0, tiled=True
        ).astype(jnp.float32),
        lax.psum_scatter(
            terms[2].astype(jnp.bfloat16), ("dp", "context"), scatter_dimension=0, tiled=True
        ).astype(jnp.float32),
        lax.psum_scatter(
            terms[3].astype(jnp.bfloat16), ("dp", "context"), scatter_dimension=0, tiled=True
        ).astype(jnp.float32),
    )
    return (input_grad, summed[0], summed[1], summed[2], summed[3])


TILE = 256
NEGATIVE = -1e30
LOG2E = 1.4426950408889634


def dot_nt(left, right):
    return lax.dot_general(
        left, right, (((1,), (1,)), ((), ())), preferred_element_type=jnp.float32
    )


def dot_nn(left, right):
    return lax.dot_general(
        left, right, (((1,), (0,)), ((), ())), preferred_element_type=jnp.float32
    )


def attention_kernel(blocks, count, heads, group, *refs):
    block_ref = refs[0]
    packs = refs[1 : 1 + blocks]
    dpacks = refs[1 + blocks : 1 + 2 * blocks]
    low_ref, cos_ref, sin_ref = refs[1 + 2 * blocks : 4 + 2 * blocks]
    attn_ref, query_ref, key_ref, value_ref = refs[4 + 2 * blocks : 8 + 2 * blocks]
    q_s, k_s, v_s, kt_s, vt_s, d_s, dt_s, dk_s, dv_s = refs[8 + 2 * blocks :]
    scale = QSCALAR ** (-0.5)
    factor = scale * LOG2E
    span = blocks * count
    wide = group * HD
    reach = -(-(W - 1) // TILE)
    here = block_ref[0]
    for part in range(blocks):
        start = pl.multiple_of((here ^ part) * count, count)
        rows = pl.ds(start, count)
        pack = packs[part]
        q_s[rows, :] = pack[:, : heads * wide]
        keys = pack[:, heads * wide : heads * (wide + HD)]
        values = pack[:, heads * (wide + HD) :]
        k_s[rows, :] = keys
        v_s[rows, :] = values
        kt_s[:, rows] = keys.T
        vt_s[:, rows] = values.T
        d_s[rows, :] = dpacks[part][...]
        dt_s[:, rows] = dpacks[part][...].T
    dk_s[...] = jnp.zeros_like(dk_s)
    dv_s[...] = jnp.zeros_like(dv_s)

    def rotated(grad, rows, times=1):
        cosine = cos_ref[rows, :]
        sine = sin_ref[rows, :]
        return grad * cosine + pltpu.roll(grad, HD // 2, 1) * sine

    for head in range(heads):
        kv = slice(head * HD, (head + 1) * HD)

        def tile(first_query, first_key, width):
            q_rows = pl.ds(first_query, TILE)
            k_rows = pl.ds(first_key, width)
            columns = [slice(head * wide + g * HD, head * wide + (g + 1) * HD) for g in range(group)]
            query = jnp.concatenate([q_s[q_rows, c] for c in columns], axis=0)
            dattn = jnp.concatenate([d_s[q_rows, c] for c in columns], axis=0)
            dattn_t = jnp.concatenate([dt_s[c, q_rows] for c in columns], axis=1)
            scores = dot_nt(k_s[k_rows, kv], query)
            low = jnp.concatenate([low_ref[:, q_rows]] * group, axis=1)
            at = first_key + lax.broadcasted_iota(jnp.int32, (width, group * TILE), 0)
            own = first_query + lax.rem(
                lax.broadcasted_iota(jnp.int32, (1, group * TILE), 1), jnp.int32(TILE)
            )
            scores = jnp.where((at >= low) & (at <= own), scores, NEGATIVE)
            top = jnp.max(scores, axis=0, keepdims=True)
            weights = jnp.exp2(scores * factor - top * factor)
            inverse = 1.0 / jnp.sum(weights, axis=0, keepdims=True)
            probs = weights * inverse
            half = probs.astype(jnp.bfloat16)
            attn = dot_nn(vt_s[kv, k_rows], half).astype(jnp.bfloat16)
            dprobs = dot_nt(v_s[k_rows, kv], dattn)
            attn_wide = attn.astype(jnp.float32)
            delta = jnp.sum(dattn_t.astype(jnp.float32) * attn_wide, axis=0, keepdims=True)
            dscores = (probs * (dprobs - delta)).astype(jnp.bfloat16)
            query_grad = (dot_nn(kt_s[kv, k_rows], dscores) * scale).T
            attn_rows = attn_wide.T
            dk_s[k_rows, kv] += dot_nn(dscores, query)
            dv_s[k_rows, kv] += dot_nn(half, dattn)
            for g, c in enumerate(columns):
                part = slice(g * TILE, (g + 1) * TILE)
                query_ref[q_rows, c] = rotated(query_grad[part], q_rows).astype(jnp.bfloat16)
                attn_ref[q_rows, c] = attn_rows[part].astype(jnp.bfloat16)

        tiles = span // TILE
        for index in range(min(reach, tiles)):
            tile(index * TILE, 0, (index + 1) * TILE)

        def steady(index, carry):
            first = pl.multiple_of(index * TILE, TILE)
            tile(first, pl.multiple_of(first - reach * TILE, TILE), (reach + 1) * TILE)
            return carry

        if tiles > reach:
            lax.fori_loop(reach, tiles, steady, 0)
        for index in range(tiles):
            rows = pl.ds(index * TILE, TILE)
            key_ref[rows, kv] = rotated(dk_s[rows, kv] * scale, rows).astype(jnp.bfloat16)
            value_ref[rows, kv] = dv_s[rows, kv].astype(jnp.bfloat16)


def attention(block, packs, dpacks, low, cosine, sine, heads, group):
    blocks = len(packs)
    count = packs[0].shape[0]
    span = blocks * count
    wide = heads * group * HD
    narrow = heads * HD
    vmem = pl.BlockSpec(memory_space=pltpu.VMEM)
    half = jnp.bfloat16
    pairs = heads * group * span * (W + TILE)
    return pl.pallas_call(
        functools.partial(attention_kernel, blocks, count, heads, group),
        out_shape=(
            jax.ShapeDtypeStruct((span, wide), half),
            jax.ShapeDtypeStruct((span, wide), half),
            jax.ShapeDtypeStruct((span, narrow), half),
            jax.ShapeDtypeStruct((span, narrow), half),
        ),
        in_specs=[pl.BlockSpec(memory_space=pltpu.SMEM)] + [vmem] * (2 * blocks + 3),
        out_specs=(vmem,) * 4,
        scratch_shapes=[
            pltpu.VMEM((span, wide), half),
            pltpu.VMEM((span, narrow), half),
            pltpu.VMEM((span, narrow), half),
            pltpu.VMEM((narrow, span), half),
            pltpu.VMEM((narrow, span), half),
            pltpu.VMEM((span, wide), half),
            pltpu.VMEM((wide, span), half),
            pltpu.VMEM((span, narrow), jnp.float32),
            pltpu.VMEM((span, narrow), jnp.float32),
        ],
        compiler_params=pltpu.CompilerParams(vmem_limit_bytes=48 * 1024 * 1024),
        cost_estimate=pl.CostEstimate(
            flops=10 * pairs * HD, bytes_accessed=span * wide * 12, transcendentals=pairs
        ),
        name="attention_backward",
    )(block, *packs, *dpacks, low, cosine, sine)


def swap(x, axis, by):
    count = lax.axis_size(axis)
    return lax.ppermute(x, axis, [(i, i ^ by) for i in range(count)])


def rotation_tables(places):
    half = HD // 2
    index = jnp.arange(half, dtype=jnp.float32)
    freq = jnp.power(jnp.float32(10000.0), index * (-2.0 / HD))
    angle = places.astype(jnp.float32)[:, None] * freq[None, :]
    cosine = jnp.cos(angle)
    sine = jnp.sin(angle)
    return jnp.concatenate([cosine, cosine], axis=1), jnp.concatenate([sine, -sine], axis=1)


def spread_rows(x, replicas, blocks, me, side):
    count, width = x.shape
    rows = width // (replicas * blocks)
    packed = x.reshape(count, replicas, blocks, rows)
    packed = jnp.transpose(packed, (2, 0, 1, 3)).reshape(blocks, count, replicas * rows)
    half = count // 2
    share = replicas * rows
    whole = jnp.zeros((blocks * count, share), x.dtype)
    own = lax.dynamic_slice(packed, (me, 0, 0), (1, count, share))[0]
    whole = lax.dynamic_update_slice(whole, own, (me * count, 0))
    for part in range(1, blocks):
        there = me ^ part
        sent = lax.dynamic_slice(packed, (there, side * half, 0), (1, half, share))[0]
        came = swap(sent, "context", part)
        other = swap(came, "tensor", 1)
        whole = lax.dynamic_update_slice(whole, came, (there * count + side * half, 0))
        whole = lax.dynamic_update_slice(whole, other, (there * count + (1 - side) * half, 0))
    return whole


def on_device(
    inputs,
    queries,
    key_states,
    value_states,
    out_grad,
    positions,
    w_query,
    w_key,
    w_value,
    w_output,
):
    count = queries.shape[0]
    head_cols = queries.shape[1]
    kv_cols = key_states.shape[1]
    kv_here = kv_cols // HD
    group = head_cols // kv_cols
    blocks = lax.axis_size("context")
    replicas = lax.axis_size("dp")
    cores = lax.axis_size("tensor")
    fits = (
        blocks & (blocks - 1) == 0
        and kv_here % blocks == 0
        and cores == 2
        and count % TILE == 0
        and W % TILE == 0
    )
    if not fits:
        return banded(
            inputs, queries, key_states, value_states, out_grad, positions,
            w_query, w_key, w_value, w_output,
        )
    me = lax.axis_index("context")
    side = lax.axis_index("tensor")
    heads = kv_here // blocks
    span = blocks * count
    wide = heads * group * HD
    narrow = heads * HD

    def columns(x, at, width):
        return lax.dynamic_slice(x, (0, at * width), (x.shape[0], width))

    packs = []
    for part in range(blocks):
        there = me ^ part
        pack = jnp.concatenate(
            [
                columns(queries, there, wide),
                columns(key_states, there, narrow),
                columns(value_states, there, narrow),
            ],
            axis=1,
        )
        packs.append(pack if part == 0 else swap(pack, "context", part))
    places = lax.all_gather(positions, "context", tiled=True)
    dattn = jnp.dot(out_grad, w_output, preferred_element_type=jnp.float32).astype(jnp.bfloat16)
    dpacks = []
    for part in range(blocks):
        pack = columns(dattn, me ^ part, wide)
        dpacks.append(pack if part == 0 else swap(pack, "context", part))
    index = jnp.arange(span, dtype=jnp.int32)
    low = jnp.maximum(index - places, index - (W - 1))[None, :]
    cosine, sine = rotation_tables(places)
    attn, query_lin, key_lin, value_half = attention(
        me.reshape(1), packs, dpacks, low, cosine, sine, heads, group
    )
    grad_rows = spread_rows(out_grad, replicas, blocks, me, side)
    input_rows = spread_rows(inputs, replicas, blocks, me, side)

    def gathered(x):
        return lax.all_gather(x, "context", axis=1, tiled=True)

    def reduced(left, right):
        term = contract_rows(left, right).astype(jnp.bfloat16)
        return lax.psum_scatter(term, "dp", scatter_dimension=0, tiled=True).astype(jnp.float32)

    attn_all = gathered(attn)
    grad_output = reduced(grad_rows, attn_all)
    value_all = gathered(value_half)
    grad_value = reduced(input_rows, value_all)
    key_all = gathered(key_lin)
    grad_key = reduced(input_rows, key_all)
    query_all = gathered(query_lin)
    grad_query = reduced(input_rows, query_all)

    def own_rows(x):
        return lax.dynamic_slice(x, (me * count, 0), (count, x.shape[1]))

    half = count // 2

    def input_part(which):
        def rows(x):
            return lax.dynamic_slice(x, (me * count + which * half, 0), (half, x.shape[1]))

        total = contract_cols(rows(query_all), w_query)
        total = total + contract_cols(rows(key_all), w_key)
        return total + contract_cols(rows(value_all), w_value)

    sent = swap(input_part(1 - side).astype(jnp.bfloat16), "tensor", 1)
    input_grad = (input_part(side) + sent.astype(jnp.float32)).astype(jnp.bfloat16)
    return (input_grad, grad_query, grad_key, grad_value, grad_output)


def solution(mesh):
    return jax.shard_map(
        on_device,
        mesh=mesh,
        in_specs=(
            P(("dp", "context"), None),
            P(("dp", "context"), "tensor"),
            P(("dp", "context"), "tensor"),
            P(("dp", "context"), "tensor"),
            P(("dp", "context"), None),
            P(("dp", "context")),
            P(None, "tensor"),
            P(None, "tensor"),
            P(None, "tensor"),
            P(None, "tensor"),
        ),
        out_specs=(
            P(("dp", "context", "tensor"), None),
            P(("dp", "context"), "tensor"),
            P(("dp", "context"), "tensor"),
            P(("dp", "context"), "tensor"),
            P(("dp", "context"), "tensor"),
        ),
        check_vma=False,
    )
```

```python
import functools

import jax
import jax.numpy as jnp
from jax import lax
from jax.experimental import pallas as pl
from jax.experimental.pallas import tpu as pltpu
from jax.sharding import PartitionSpec as P

HD = 128
W = 1024
QSCALAR = 168


def shifted(x, axis, by):
    count = lax.axis_size(axis)
    pairs = [(i, i + by) for i in range(count) if 0 <= i + by < count]
    return lax.ppermute(x, axis, pairs)


def rotate_back(grads, places):
    count = grads.shape[0]
    half = HD // 2
    index = jnp.arange(half, dtype=jnp.float32)
    freq = jnp.power(jnp.float32(10000.0), index * (-2.0 / HD))
    angle = places.astype(jnp.float32)[:, None] * freq[None, :]
    cosine = jnp.cos(angle)[:, None, :]
    sine = jnp.sin(angle)[:, None, :]
    split = grads.reshape(count, -1, 2, half)
    first = split[:, :, 0, :]
    second = split[:, :, 1, :]
    upper = first * cosine + second * sine
    lower = second * cosine - first * sine
    return jnp.stack([upper, lower], axis=2).reshape(count, -1)


def contract_rows(left, right):
    return lax.dot_general(
        left, right, (((0,), (0,)), ((), ())), preferred_element_type=jnp.float32
    )


def contract_cols(left, right):
    return lax.dot_general(
        left, right, (((1,), (1,)), ((), ())), preferred_element_type=jnp.float32
    )


def banded(
    inputs,
    queries,
    key_states,
    value_states,
    out_grad,
    positions,
    w_query,
    w_key,
    w_value,
    w_output,
):
    count = queries.shape[0]
    head_cols = queries.shape[1]
    kv_cols = key_states.shape[1]
    kv_here = kv_cols // HD
    group = head_cols // kv_cols
    scale = QSCALAR ** (-0.5)
    block = lax.axis_index("context")
    blocks = lax.axis_size("context")
    reach = min((W + count - 2) // count, blocks - 1)
    span = (reach + 1) * count
    key_pieces = []
    value_pieces = []
    for back in range(reach, 0, -1):
        earlier_keys, earlier_values = shifted((key_states, value_states), "context", back)
        key_pieces.append(earlier_keys)
        value_pieces.append(earlier_values)
    band_keys = jnp.concatenate(key_pieces + [key_states], axis=0)
    band_values = jnp.concatenate(value_pieces + [value_states], axis=0)
    query_index = block * count + jnp.arange(count, dtype=jnp.int32)
    key_index = (block - reach) * count + jnp.arange(span, dtype=jnp.int32)
    doc_start = query_index - positions
    allowed = (key_index[None, :] <= query_index[:, None]) & (
        query_index[:, None] - key_index[None, :] < W
    )
    allowed = allowed & (key_index[None, :] >= doc_start[:, None]) & (key_index[None, :] >= 0)
    query_heads = queries.reshape(count, kv_here, group, HD)
    key_heads = band_keys.reshape(span, kv_here, HD)
    value_heads = band_values.reshape(span, kv_here, HD)
    scores = (
        jnp.einsum("qhgd,khd->hgqk", query_heads, key_heads, preferred_element_type=jnp.float32)
        * scale
    )
    scores = jnp.where(allowed, scores, -1e30)
    top = jnp.max(scores, axis=-1, keepdims=True)
    weights = jnp.exp(scores - top)
    probs = weights / jnp.sum(weights, axis=-1, keepdims=True)
    probs_half = probs.astype(jnp.bfloat16)
    attn = jnp.einsum(
        "hgqk,khd->qhgd", probs_half, value_heads, preferred_element_type=jnp.float32
    ).astype(jnp.bfloat16)
    attn_flat = attn.reshape(count, head_cols)
    dattn = jnp.dot(out_grad, w_output, preferred_element_type=jnp.float32).astype(jnp.bfloat16)
    dattn_heads = dattn.reshape(count, kv_here, group, HD)
    dprobs = jnp.einsum(
        "qhgd,khd->hgqk", dattn_heads, value_heads, preferred_element_type=jnp.float32
    )
    delta = jnp.sum(dattn_heads.astype(jnp.float32) * attn.astype(jnp.float32), axis=-1)
    delta = jnp.transpose(delta, (1, 2, 0))[..., None]
    dscores = (probs * (dprobs - delta) * scale).astype(jnp.bfloat16)
    query_grad = jnp.einsum(
        "hgqk,khd->qhgd", dscores, key_heads, preferred_element_type=jnp.float32
    ).reshape(count, head_cols)
    band_key_grad = jnp.einsum(
        "hgqk,qhgd->khd", dscores, query_heads, preferred_element_type=jnp.float32
    ).reshape(span, kv_cols)
    band_value_grad = jnp.einsum(
        "hgqk,qhgd->khd", probs_half, dattn_heads, preferred_element_type=jnp.float32
    ).reshape(span, kv_cols)
    key_grad = band_key_grad[reach * count :]
    value_grad = band_value_grad[reach * count :]
    for back in range(1, reach + 1):
        first_row = (reach - back) * count
        sent_keys, sent_values = shifted(
            (
                band_key_grad[first_row : first_row + count],
                band_value_grad[first_row : first_row + count],
            ),
            "context",
            -back,
        )
        key_grad = key_grad + sent_keys
        value_grad = value_grad + sent_values
    query_lin = rotate_back(query_grad, positions).astype(jnp.bfloat16)
    key_lin = rotate_back(key_grad, positions).astype(jnp.bfloat16)
    value_half = value_grad.astype(jnp.bfloat16)
    total = contract_cols(query_lin, w_query)
    total = total + contract_cols(key_lin, w_key)
    total = total + contract_cols(value_half, w_value)
    input_grad = lax.psum_scatter(total, "tensor", scatter_dimension=0, tiled=True).astype(
        jnp.bfloat16
    )
    terms = (
        contract_rows(inputs, query_lin),
        contract_rows(inputs, key_lin),
        contract_rows(inputs, value_half),
        contract_rows(out_grad, attn_flat),
    )
    summed = (
        lax.psum_scatter(
            terms[0].astype(jnp.bfloat16), ("dp", "context"), scatter_dimension=0, tiled=True
        ).astype(jnp.float32),
        lax.psum_scatter(
            terms[1].astype(jnp.bfloat16), ("dp", "context"), scatter_dimension=0, tiled=True
        ).astype(jnp.float32),
        lax.psum_scatter(
            terms[2].astype(jnp.bfloat16), ("dp", "context"), scatter_dimension=0, tiled=True
        ).astype(jnp.float32),
        lax.psum_scatter(
            terms[3].astype(jnp.bfloat16), ("dp", "context"), scatter_dimension=0, tiled=True
        ).astype(jnp.float32),
    )
    return (input_grad, summed[0], summed[1], summed[2], summed[3])


TILE = 256
EXTRA = 16
RADIX = 128
NEGATIVE = -1e30
LOG2E = 1.4426950408889634
VMEM_LIMIT = 48 * 1024 * 1024


def dot_nt(left, right):
    return lax.dot_general(
        left, right, (((1,), (1,)), ((), ())), preferred_element_type=jnp.float32
    )


def dot_nn(left, right):
    return lax.dot_general(
        left, right, (((1,), (0,)), ((), ())), preferred_element_type=jnp.float32
    )


def whole():
    return pl.BlockSpec(memory_space=pltpu.VMEM)


def scalars():
    return pl.BlockSpec(memory_space=pltpu.SMEM)


def params():
    return pltpu.CompilerParams(vmem_limit_bytes=VMEM_LIMIT)


def aligned(index, size):
    return pl.ds(pl.multiple_of(index * size, size), size)


def pack_heads_kernel(blocks, wide, narrow, at_ref, q_ref, k_ref, v_ref, extra_ref, *outs):
    me = at_ref[0]
    count = q_ref.shape[0]
    for part in range(blocks):
        there = me ^ part
        out = outs[part]
        out[:count, :wide] = q_ref[:, aligned(there, wide)]
        out[:count, wide : wide + narrow] = k_ref[:, aligned(there, narrow)]
        out[:count, wide + narrow :] = v_ref[:, aligned(there, narrow)]
        out[count:, :] = extra_ref[...]


def pack_heads(at, queries, key_states, value_states, extra, blocks, wide, narrow):
    count = queries.shape[0]
    shape = jax.ShapeDtypeStruct((count + EXTRA, wide + 2 * narrow), queries.dtype)
    return pl.pallas_call(
        functools.partial(pack_heads_kernel, blocks, wide, narrow),
        out_shape=(shape,) * blocks,
        in_specs=[scalars()] + [whole()] * 4,
        out_specs=(whole(),) * blocks,
        compiler_params=params(),
        cost_estimate=pl.CostEstimate(
            flops=0, bytes_accessed=4 * blocks * count * (wide + 2 * narrow), transcendentals=0
        ),
        name="pack_heads",
    )(at, queries, key_states, value_states, extra)


def pack_rows_kernel(blocks, replicas, rows, at_ref, x_ref, own_ref, *rest):
    outs, turned = rest[:-1], rest[-1]
    me, side = at_ref[0], at_ref[1]
    count, width = x_ref.shape
    half = count // 2

    def turn(index, carry):
        cols = aligned(index, HD)
        turned[cols, :] = x_ref[:, cols].T
        return carry

    lax.fori_loop(0, width // HD, turn, 0)
    for replica in range(replicas):
        into = pl.ds(replica * rows, rows)
        own_ref[into, :] = turned[aligned(replica * blocks + me, rows), :]
        for part in range(1, blocks):
            taken = aligned(replica * blocks + (me ^ part), rows)
            outs[part - 1][into, :] = turned[taken, aligned(side, half)]


def pack_rows(at, x, blocks, replicas):
    count, width = x.shape
    rows = width // (replicas * blocks)
    share = replicas * rows
    own = jax.ShapeDtypeStruct((share, count), x.dtype)
    sent = jax.ShapeDtypeStruct((share, count // 2), x.dtype)
    return pl.pallas_call(
        functools.partial(pack_rows_kernel, blocks, replicas, rows),
        out_shape=(own,) + (sent,) * (blocks - 1),
        in_specs=[scalars(), whole()],
        out_specs=(whole(),) * blocks,
        scratch_shapes=[pltpu.VMEM((width, count), x.dtype)],
        compiler_params=params(),
        cost_estimate=pl.CostEstimate(
            flops=0, bytes_accessed=6 * count * width, transcendentals=0
        ),
        name="pack_rows",
    )(at, x)


def attention_kernel(blocks, count, heads, group, *refs):
    at_ref = refs[0]
    packs = refs[1 : 1 + blocks]
    dpacks = refs[1 + blocks : 1 + 2 * blocks]
    low_ref, cos_ref, sin_ref = refs[1 + 2 * blocks : 4 + 2 * blocks]
    first_ref, second_ref = refs[4 + 2 * blocks : 6 + 2 * blocks]
    q_s, k_s, v_s, kt_s, vt_s, d_s, dt_s, dk_s, dv_s = refs[6 + 2 * blocks :]
    scale = QSCALAR ** (-0.5)
    factor = scale * LOG2E
    span = blocks * count
    wide = heads * group * HD
    narrow = heads * HD
    per_block = count // TILE
    reach = -(-(W - 1) // TILE)
    me = at_ref[0]
    for part in range(blocks):
        rows = aligned(me ^ part, count)
        pack = packs[part]
        q_s[rows, :] = pack[:count, :wide]
        keys = pack[:count, wide : wide + narrow]
        values = pack[:count, wide + narrow :]
        k_s[rows, :] = keys
        v_s[rows, :] = values
        kt_s[:, rows] = keys.T
        vt_s[:, rows] = values.T
        d_s[rows, :] = dpacks[part][...]
        dt_s[:, rows] = dpacks[part][...].T
    dk_s[...] = jnp.zeros_like(dk_s)
    dv_s[...] = jnp.zeros_like(dv_s)

    def stored(index):
        return aligned(((index // per_block) ^ me) * per_block + lax.rem(index, per_block), TILE)

    def rotated(grad, rows):
        return grad * cos_ref[rows, :] + pltpu.roll(grad, HD // 2, 1) * sin_ref[rows, :]

    for head in range(heads):
        kv = slice(head * HD, (head + 1) * HD)

        def tile(index, first_key, width):
            index = jnp.int32(index)
            q_rows = aligned(index, TILE)
            t_rows = stored(index)
            k_rows = pl.ds(first_key, width)
            columns = [slice(head * group * HD + g * HD, head * group * HD + (g + 1) * HD) for g in range(group)]
            query = jnp.concatenate([q_s[q_rows, c] for c in columns], axis=0)
            dattn = jnp.concatenate([d_s[q_rows, c] for c in columns], axis=0)
            dattn_t = jnp.concatenate([dt_s[c, q_rows] for c in columns], axis=1)
            scores = dot_nt(k_s[k_rows, kv], query)
            low = jnp.concatenate([low_ref[:, t_rows]] * group, axis=1)
            at = first_key + lax.broadcasted_iota(jnp.int32, (width, group * TILE), 0)
            own = index * TILE + lax.rem(
                lax.broadcasted_iota(jnp.int32, (1, group * TILE), 1), jnp.int32(TILE)
            )
            scores = jnp.where((at >= low) & (at <= own), scores, NEGATIVE)
            top = jnp.max(scores, axis=0, keepdims=True)
            weights = jnp.exp2(scores * factor - top * factor)
            inverse = 1.0 / jnp.sum(weights, axis=0, keepdims=True)
            probs = weights * inverse
            half = probs.astype(jnp.bfloat16)
            attn = dot_nn(vt_s[kv, k_rows], half).astype(jnp.bfloat16)
            dprobs = dot_nt(v_s[k_rows, kv], dattn)
            attn_wide = attn.astype(jnp.float32)
            delta = jnp.sum(dattn_t.astype(jnp.float32) * attn_wide, axis=0, keepdims=True)
            dscores = (probs * (dprobs - delta)).astype(jnp.bfloat16)
            query_grad = (dot_nn(kt_s[kv, k_rows], dscores) * scale).T
            attn_rows = attn_wide.T
            dk_s[k_rows, kv] += dot_nn(dscores, query)
            dv_s[k_rows, kv] += dot_nn(half, dattn)
            for g, c in enumerate(columns):
                part = slice(g * TILE, (g + 1) * TILE)
                first_ref[q_rows, c] = attn_rows[part].astype(jnp.bfloat16)
                second_ref[q_rows, c] = rotated(query_grad[part], t_rows).astype(jnp.bfloat16)

        tiles = span // TILE
        for index in range(min(reach, tiles)):
            tile(index, 0, (index + 1) * TILE)

        def steady(index, carry):
            tile(index, pl.multiple_of((index - reach) * TILE, TILE), (reach + 1) * TILE)
            return carry

        if tiles > reach:
            lax.fori_loop(reach, tiles, steady, 0)
        out = slice(wide + head * HD, wide + (head + 1) * HD)
        for index in range(tiles):
            rows = pl.ds(index * TILE, TILE)
            first_ref[rows, out] = dv_s[rows, kv].astype(jnp.bfloat16)
            second_ref[rows, out] = rotated(
                dk_s[rows, kv] * scale, stored(jnp.int32(index))
            ).astype(jnp.bfloat16)


def attention(at, packs, dpacks, low, cosine, sine, heads, group):
    blocks = len(packs)
    count = dpacks[0].shape[0]
    span = blocks * count
    wide = heads * group * HD
    narrow = heads * HD
    half = jnp.bfloat16
    pairs = heads * group * span * (W + TILE)
    return pl.pallas_call(
        functools.partial(attention_kernel, blocks, count, heads, group),
        out_shape=(jax.ShapeDtypeStruct((span, wide + narrow), half),) * 2,
        in_specs=[scalars()] + [whole()] * (2 * blocks + 3),
        out_specs=(whole(),) * 2,
        scratch_shapes=[
            pltpu.VMEM((span, wide), half),
            pltpu.VMEM((span, narrow), half),
            pltpu.VMEM((span, narrow), half),
            pltpu.VMEM((narrow, span), half),
            pltpu.VMEM((narrow, span), half),
            pltpu.VMEM((span, wide), half),
            pltpu.VMEM((wide, span), half),
            pltpu.VMEM((span, narrow), jnp.float32),
            pltpu.VMEM((span, narrow), jnp.float32),
        ],
        compiler_params=params(),
        cost_estimate=pl.CostEstimate(
            flops=10 * pairs * HD, bytes_accessed=span * wide * 12, transcendentals=pairs
        ),
        name="attention_backward",
    )(at, *packs, *dpacks, low, cosine, sine)


def weight_terms_kernel(blocks, wide, at_ref, *refs):
    pieces = 1 + 2 * (blocks - 1)
    grad_refs, input_refs = refs[:pieces], refs[pieces : 2 * pieces]
    first_ref, second_ref, out_ref = refs[2 * pieces :]
    me, side = at_ref[0], at_ref[1]
    count = grad_refs[0].shape[1]
    half = count // 2
    rows = [aligned(me, count)]
    for part in range(1, blocks):
        rows.append(aligned((me ^ part) * 2 + side, half))
        rows.append(aligned((me ^ part) * 2 + 1 - side, half))
    total = [None, None, None]
    for piece in range(pieces):
        grad = grad_refs[piece][...]
        inp = input_refs[piece][...]
        terms = (
            dot_nn(grad, first_ref[rows[piece], :wide]),
            dot_nn(inp, first_ref[rows[piece], wide:]),
            dot_nn(inp, second_ref[rows[piece], :]),
        )
        total = [new if old is None else old + new for old, new in zip(total, terms)]
    edge = first_ref.shape[1]
    out_ref[:, :wide] = total[0].astype(out_ref.dtype)
    out_ref[:, wide:edge] = total[1].astype(out_ref.dtype)
    out_ref[:, edge:] = total[2].astype(out_ref.dtype)


def weight_terms(at, grads, ins, first, second, blocks, replicas, wide):
    share, count = grads[0].shape
    rows = share // replicas
    span, cols = first.shape

    def piece(x):
        return pl.BlockSpec((rows, x.shape[1]), lambda i, at: (i, 0))

    def fixed(x):
        return pl.BlockSpec(x.shape, lambda i, at: (0, 0))

    return pl.pallas_call(
        functools.partial(weight_terms_kernel, blocks, wide),
        out_shape=jax.ShapeDtypeStruct((share, 2 * cols), first.dtype),
        grid_spec=pltpu.PrefetchScalarGridSpec(
            num_scalar_prefetch=1,
            grid=(replicas,),
            in_specs=[piece(x) for x in grads + ins] + [fixed(first), fixed(second)],
            out_specs=pl.BlockSpec((rows, 2 * cols), lambda i, at: (i, 0)),
        ),
        compiler_params=params(),
        cost_estimate=pl.CostEstimate(
            flops=4 * share * span * cols,
            bytes_accessed=4 * share * span + 4 * (span + share) * cols,
            transcendentals=0,
        ),
        name="weight_terms",
    )(at, *grads, *ins, first, second)


def assemble_kernel(sources, wide, narrow, at_ref, *refs):
    parts = refs[: len(sources)]
    output_ref, value_ref, query_ref, key_ref = refs[len(sources) :]
    me = at_ref[0]
    edge = wide + narrow
    for (source_first, source_second), part in zip(sources, parts):
        first, second = me ^ source_first, me ^ source_second
        output_ref[:, aligned(first, wide)] = part[:, :wide].astype(jnp.float32)
        value_ref[:, aligned(first, narrow)] = part[:, wide:edge].astype(jnp.float32)
        query_ref[:, aligned(second, wide)] = part[:, edge : edge + wide].astype(jnp.float32)
        key_ref[:, aligned(second, narrow)] = part[:, edge + wide :].astype(jnp.float32)


def assemble(at, sources, parts, wide, narrow):
    rows = parts[0].shape[0]
    blocks = len(sources)
    shapes = [
        jax.ShapeDtypeStruct((rows, blocks * cols), jnp.float32)
        for cols in (wide, narrow, wide, narrow)
    ]
    return pl.pallas_call(
        functools.partial(assemble_kernel, sources, wide, narrow),
        out_shape=tuple(shapes),
        in_specs=[scalars()] + [whole()] * blocks,
        out_specs=(whole(),) * 4,
        compiler_params=params(),
        name="assemble",
    )(at, *parts)


def input_terms_kernel(blocks, wide, narrow, at_ref, *refs):
    firsts, seconds = refs[:blocks], refs[blocks : 2 * blocks]
    wq_ref, wk_ref, wv_ref, mine_ref, sent_ref, q_s, k_s, v_s = refs[2 * blocks :]
    me, side = at_ref[0], at_ref[1]

    @pl.when(pl.program_id(0) == 0)
    def _():
        for part in range(blocks):
            there = me ^ part
            q_s[:, aligned(there, wide)] = seconds[part][:, :wide]
            k_s[:, aligned(there, narrow)] = seconds[part][:, wide:]
            v_s[:, aligned(there, narrow)] = firsts[part][:, wide:]

    half = q_s.shape[0] // 2
    for target, which in ((sent_ref, 1 - side), (mine_ref, side)):
        rows = aligned(which, half)
        total = dot_nt(q_s[rows, :], wq_ref[...])
        total = total + dot_nt(k_s[rows, :], wk_ref[...])
        total = total + dot_nt(v_s[rows, :], wv_ref[...])
        target[...] = total.astype(target.dtype)


def input_terms(at, firsts, seconds, w_query, w_key, w_value, count, wide, narrow):
    blocks = len(firsts)
    width = w_query.shape[0]
    step = next(s for s in (768, 512, 256, 128, width) if width % s == 0)

    def own(x):
        return pl.BlockSpec((count, x.shape[1]), lambda i, at: (at[0], 0))

    def weight(x):
        return pl.BlockSpec((step, x.shape[1]), lambda i, at: (i, 0))

    out = pl.BlockSpec((count // 2, step), lambda i, at: (0, i))
    ins = firsts + seconds
    half = jnp.bfloat16
    return pl.pallas_call(
        functools.partial(input_terms_kernel, blocks, wide, narrow),
        out_shape=(
            jax.ShapeDtypeStruct((count // 2, width), jnp.float32),
            jax.ShapeDtypeStruct((count // 2, width), half),
        ),
        grid_spec=pltpu.PrefetchScalarGridSpec(
            num_scalar_prefetch=1,
            grid=(width // step,),
            in_specs=[own(x) for x in ins] + [weight(x) for x in (w_query, w_key, w_value)],
            out_specs=(out, out),
            scratch_shapes=[
                pltpu.VMEM((count, blocks * wide), half),
                pltpu.VMEM((count, blocks * narrow), half),
                pltpu.VMEM((count, blocks * narrow), half),
            ],
        ),
        compiler_params=params(),
        cost_estimate=pl.CostEstimate(
            flops=2 * count * width * blocks * (wide + 2 * narrow),
            bytes_accessed=2 * width * blocks * (wide + 2 * narrow) + 3 * width * count,
            transcendentals=0,
        ),
        name="input_terms",
    )(at, *ins, w_query, w_key, w_value)


def swap(x, axis, by):
    count = lax.axis_size(axis)
    return lax.ppermute(x, axis, [(i, i ^ by) for i in range(count)])


def rotation_tables(places):
    half = HD // 2
    index = jnp.arange(half, dtype=jnp.float32)
    freq = jnp.power(jnp.float32(10000.0), index * (-2.0 / HD))
    angle = places.astype(jnp.float32)[:, None] * freq[None, :]
    cosine = jnp.cos(angle)
    sine = jnp.sin(angle)
    return jnp.concatenate([cosine, cosine], axis=1), jnp.concatenate([sine, -sine], axis=1)


def on_device(
    inputs,
    queries,
    key_states,
    value_states,
    out_grad,
    positions,
    w_query,
    w_key,
    w_value,
    w_output,
):
    count = queries.shape[0]
    head_cols = queries.shape[1]
    kv_cols = key_states.shape[1]
    kv_here = kv_cols // HD
    group = head_cols // kv_cols
    blocks = lax.axis_size("context")
    replicas = lax.axis_size("dp")
    cores = lax.axis_size("tensor")
    width = inputs.shape[1]
    heads = kv_here // blocks
    wide = heads * group * HD
    narrow = heads * HD
    fits = (
        blocks == 4
        and kv_here % blocks == 0
        and cores == 2
        and count % (2 * HD) == 0
        and count % TILE == 0
        and W % TILE == 0
        and width % HD == 0
        and width % (replicas * blocks * EXTRA) == 0
        and wide + 2 * narrow >= count
    )
    if not fits:
        return banded(
            inputs, queries, key_states, value_states, out_grad, positions,
            w_query, w_key, w_value, w_output,
        )
    me = lax.axis_index("context")
    side = lax.axis_index("tensor")
    at = jnp.stack([me, side]).astype(jnp.int32)

    digits = jnp.stack([positions // RADIX, positions % RADIX]).astype(jnp.bfloat16)
    extra = jnp.pad(digits, ((0, EXTRA - 2), (0, wide + 2 * narrow - count)))
    packs = list(
        pack_heads(at, queries, key_states, value_states, extra, blocks, wide, narrow)
    )
    for part in range(1, blocks):
        packs[part] = swap(packs[part], "context", part)
    dattn = jnp.dot(out_grad, w_output, preferred_element_type=jnp.float32).astype(jnp.bfloat16)
    dpacks = []
    for part in range(blocks):
        pack = lax.dynamic_slice(dattn, (0, (me ^ part) * wide), (count, wide))
        dpacks.append(pack if part == 0 else swap(pack, "context", part))
    places = [
        (pack[count, :count].astype(jnp.float32) * RADIX + pack[count + 1, :count].astype(jnp.float32)).astype(jnp.int32)
        for pack in packs[1:]
    ]
    places = jnp.concatenate([positions] + places)
    index = jnp.concatenate(
        [(me ^ part) * count + jnp.arange(count, dtype=jnp.int32) for part in range(blocks)]
    )
    low = jnp.maximum(index - places, index - (W - 1))[None, :]
    cosine, sine = rotation_tables(places)

    def spread(packed):
        return [swap(x, "context", part + 1) for part, x in enumerate(packed)]

    def joined(own, came):
        pieces = [own]
        for x in came:
            pieces += [x, swap(x, "tensor", 1)]
        return pieces

    grad_own, *grad_packed = pack_rows(at, out_grad, blocks, replicas)
    input_own, *input_packed = pack_rows(at, inputs, blocks, replicas)
    grad_came = spread(grad_packed)
    dpacks, grad_came = lax.optimization_barrier((dpacks, grad_came))
    first, second = attention(at, packs, dpacks, low, cosine, sine, heads, group)
    grads = joined(grad_own, grad_came)
    ins = joined(input_own, spread(input_packed))

    firsts = [first, swap(first, "context", 1), swap(first, "context", 2), None]
    seconds = [second, swap(second, "context", 1), swap(second, "context", 2), None]
    firsts[3] = swap(firsts[1], "context", 2)
    seconds[3] = swap(seconds[2], "context", 1)
    sources = [(0, 0), (1, 2), (2, 1), (3, 3)]
    parts = []
    for source_first, source_second in sources:
        term = weight_terms(
            at, grads, ins, firsts[source_first], seconds[source_second], blocks, replicas, wide
        )
        parts.append(lax.psum_scatter(term, "dp", scatter_dimension=0, tiled=True))
    late, _ = lax.optimization_barrier((at, term))
    mine, sent = input_terms(
        late, firsts, seconds, w_query, w_key, w_value, count, wide, narrow
    )
    came = swap(sent, "tensor", 1)
    input_grad = (mine + came.astype(jnp.float32)).astype(jnp.bfloat16)
    last, input_grad = lax.optimization_barrier((at, input_grad))
    grad_output, grad_value, grad_query, grad_key = assemble(last, sources, parts, wide, narrow)
    return (input_grad, grad_query, grad_key, grad_value, grad_output)


def solution(mesh):
    return jax.shard_map(
        on_device,
        mesh=mesh,
        in_specs=(
            P(("dp", "context"), None),
            P(("dp", "context"), "tensor"),
            P(("dp", "context"), "tensor"),
            P(("dp", "context"), "tensor"),
            P(("dp", "context"), None),
            P(("dp", "context")),
            P(None, "tensor"),
            P(None, "tensor"),
            P(None, "tensor"),
            P(None, "tensor"),
        ),
        out_specs=(
            P(("dp", "context", "tensor"), None),
            P(("dp", "context"), "tensor"),
            P(("dp", "context"), "tensor"),
            P(("dp", "context"), "tensor"),
            P(("dp", "context"), "tensor"),
        ),
        check_vma=False,
    )
```

```python
import functools

import jax
import jax.numpy as jnp
from jax import lax
from jax.experimental import pallas as pl
from jax.experimental.pallas import tpu as pltpu
from jax.sharding import PartitionSpec as P

HD = 128
W = 1024
QSCALAR = 168


def shifted(x, axis, by):
    count = lax.axis_size(axis)
    pairs = [(i, i + by) for i in range(count) if 0 <= i + by < count]
    return lax.ppermute(x, axis, pairs)


def rotate_back(grads, places):
    count = grads.shape[0]
    half = HD // 2
    index = jnp.arange(half, dtype=jnp.float32)
    freq = jnp.power(jnp.float32(10000.0), index * (-2.0 / HD))
    angle = places.astype(jnp.float32)[:, None] * freq[None, :]
    cosine = jnp.cos(angle)[:, None, :]
    sine = jnp.sin(angle)[:, None, :]
    split = grads.reshape(count, -1, 2, half)
    first = split[:, :, 0, :]
    second = split[:, :, 1, :]
    upper = first * cosine + second * sine
    lower = second * cosine - first * sine
    return jnp.stack([upper, lower], axis=2).reshape(count, -1)


def contract_rows(left, right):
    return lax.dot_general(
        left, right, (((0,), (0,)), ((), ())), preferred_element_type=jnp.float32
    )


def contract_cols(left, right):
    return lax.dot_general(
        left, right, (((1,), (1,)), ((), ())), preferred_element_type=jnp.float32
    )


def banded(
    inputs,
    queries,
    key_states,
    value_states,
    out_grad,
    positions,
    w_query,
    w_key,
    w_value,
    w_output,
):
    count = queries.shape[0]
    head_cols = queries.shape[1]
    kv_cols = key_states.shape[1]
    kv_here = kv_cols // HD
    group = head_cols // kv_cols
    scale = QSCALAR ** (-0.5)
    block = lax.axis_index("context")
    blocks = lax.axis_size("context")
    reach = min((W + count - 2) // count, blocks - 1)
    span = (reach + 1) * count
    key_pieces = []
    value_pieces = []
    for back in range(reach, 0, -1):
        earlier_keys, earlier_values = shifted((key_states, value_states), "context", back)
        key_pieces.append(earlier_keys)
        value_pieces.append(earlier_values)
    band_keys = jnp.concatenate(key_pieces + [key_states], axis=0)
    band_values = jnp.concatenate(value_pieces + [value_states], axis=0)
    query_index = block * count + jnp.arange(count, dtype=jnp.int32)
    key_index = (block - reach) * count + jnp.arange(span, dtype=jnp.int32)
    doc_start = query_index - positions
    allowed = (key_index[None, :] <= query_index[:, None]) & (
        query_index[:, None] - key_index[None, :] < W
    )
    allowed = allowed & (key_index[None, :] >= doc_start[:, None]) & (key_index[None, :] >= 0)
    query_heads = queries.reshape(count, kv_here, group, HD)
    key_heads = band_keys.reshape(span, kv_here, HD)
    value_heads = band_values.reshape(span, kv_here, HD)
    scores = (
        jnp.einsum("qhgd,khd->hgqk", query_heads, key_heads, preferred_element_type=jnp.float32)
        * scale
    )
    scores = jnp.where(allowed, scores, -1e30)
    top = jnp.max(scores, axis=-1, keepdims=True)
    weights = jnp.exp(scores - top)
    probs = weights / jnp.sum(weights, axis=-1, keepdims=True)
    probs_half = probs.astype(jnp.bfloat16)
    attn = jnp.einsum(
        "hgqk,khd->qhgd", probs_half, value_heads, preferred_element_type=jnp.float32
    ).astype(jnp.bfloat16)
    attn_flat = attn.reshape(count, head_cols)
    dattn = jnp.dot(out_grad, w_output, preferred_element_type=jnp.float32).astype(jnp.bfloat16)
    dattn_heads = dattn.reshape(count, kv_here, group, HD)
    dprobs = jnp.einsum(
        "qhgd,khd->hgqk", dattn_heads, value_heads, preferred_element_type=jnp.float32
    )
    delta = jnp.sum(dattn_heads.astype(jnp.float32) * attn.astype(jnp.float32), axis=-1)
    delta = jnp.transpose(delta, (1, 2, 0))[..., None]
    dscores = (probs * (dprobs - delta) * scale).astype(jnp.bfloat16)
    query_grad = jnp.einsum(
        "hgqk,khd->qhgd", dscores, key_heads, preferred_element_type=jnp.float32
    ).reshape(count, head_cols)
    band_key_grad = jnp.einsum(
        "hgqk,qhgd->khd", dscores, query_heads, preferred_element_type=jnp.float32
    ).reshape(span, kv_cols)
    band_value_grad = jnp.einsum(
        "hgqk,qhgd->khd", probs_half, dattn_heads, preferred_element_type=jnp.float32
    ).reshape(span, kv_cols)
    key_grad = band_key_grad[reach * count :]
    value_grad = band_value_grad[reach * count :]
    for back in range(1, reach + 1):
        first_row = (reach - back) * count
        sent_keys, sent_values = shifted(
            (
                band_key_grad[first_row : first_row + count],
                band_value_grad[first_row : first_row + count],
            ),
            "context",
            -back,
        )
        key_grad = key_grad + sent_keys
        value_grad = value_grad + sent_values
    query_lin = rotate_back(query_grad, positions).astype(jnp.bfloat16)
    key_lin = rotate_back(key_grad, positions).astype(jnp.bfloat16)
    value_half = value_grad.astype(jnp.bfloat16)
    total = contract_cols(query_lin, w_query)
    total = total + contract_cols(key_lin, w_key)
    total = total + contract_cols(value_half, w_value)
    input_grad = lax.psum_scatter(total, "tensor", scatter_dimension=0, tiled=True).astype(
        jnp.bfloat16
    )
    terms = (
        contract_rows(inputs, query_lin),
        contract_rows(inputs, key_lin),
        contract_rows(inputs, value_half),
        contract_rows(out_grad, attn_flat),
    )
    summed = (
        lax.psum_scatter(
            terms[0].astype(jnp.bfloat16), ("dp", "context"), scatter_dimension=0, tiled=True
        ).astype(jnp.float32),
        lax.psum_scatter(
            terms[1].astype(jnp.bfloat16), ("dp", "context"), scatter_dimension=0, tiled=True
        ).astype(jnp.float32),
        lax.psum_scatter(
            terms[2].astype(jnp.bfloat16), ("dp", "context"), scatter_dimension=0, tiled=True
        ).astype(jnp.float32),
        lax.psum_scatter(
            terms[3].astype(jnp.bfloat16), ("dp", "context"), scatter_dimension=0, tiled=True
        ).astype(jnp.float32),
    )
    return (input_grad, summed[0], summed[1], summed[2], summed[3])


TILE = 256
EXTRA = 16
RADIX = 128
NEGATIVE = -1e30
LOG2E = 1.4426950408889634
VMEM_LIMIT = 48 * 1024 * 1024
LOAD = 12
COST = 20


def dot_nt(left, right):
    return lax.dot_general(
        left, right, (((1,), (1,)), ((), ())), preferred_element_type=jnp.float32
    )


def dot_nn(left, right):
    return lax.dot_general(
        left, right, (((1,), (0,)), ((), ())), preferred_element_type=jnp.float32
    )


def whole():
    return pl.BlockSpec(memory_space=pltpu.VMEM)


def scalars():
    return pl.BlockSpec(memory_space=pltpu.SMEM)


def params():
    return pltpu.CompilerParams(vmem_limit_bytes=VMEM_LIMIT)


def aligned(index, size):
    return pl.ds(pl.multiple_of(index * size, size), size)


def pack_heads_kernel(blocks, wide, narrow, at_ref, q_ref, k_ref, v_ref, extra_ref, *outs):
    me = at_ref[0]
    count = q_ref.shape[0]
    for part in range(blocks):
        there = me ^ part
        out = outs[part]
        out[:count, :wide] = q_ref[:, aligned(there, wide)]
        out[:count, wide : wide + narrow] = k_ref[:, aligned(there, narrow)]
        out[:count, wide + narrow :] = v_ref[:, aligned(there, narrow)]
        out[count:, :] = extra_ref[...]


def pack_heads(at, queries, key_states, value_states, extra, blocks, wide, narrow):
    count = queries.shape[0]
    shape = jax.ShapeDtypeStruct((count + EXTRA, wide + 2 * narrow), queries.dtype)
    return pl.pallas_call(
        functools.partial(pack_heads_kernel, blocks, wide, narrow),
        out_shape=(shape,) * blocks,
        in_specs=[scalars()] + [whole()] * 4,
        out_specs=(whole(),) * blocks,
        compiler_params=params(),
        cost_estimate=pl.CostEstimate(
            flops=0, bytes_accessed=4 * blocks * count * (wide + 2 * narrow), transcendentals=0
        ),
        name="pack_heads",
    )(at, queries, key_states, value_states, extra)


def pack_rows_kernel(blocks, replicas, rows, at_ref, x_ref, own_ref, *rest):
    outs, turned = rest[:-1], rest[-1]
    me, side = at_ref[0], at_ref[1]
    count, width = x_ref.shape
    half = count // 2

    def turn(index, carry):
        cols = aligned(index, HD)
        turned[cols, :] = x_ref[:, cols].T
        return carry

    lax.fori_loop(0, width // HD, turn, 0)
    for replica in range(replicas):
        into = pl.ds(replica * rows, rows)
        own_ref[into, :] = turned[aligned(replica * blocks + me, rows), :]
        for part in range(1, blocks):
            taken = aligned(replica * blocks + (me ^ part), rows)
            outs[part - 1][into, :] = turned[taken, aligned(side, half)]


def pack_rows(at, x, blocks, replicas):
    count, width = x.shape
    rows = width // (replicas * blocks)
    share = replicas * rows
    own = jax.ShapeDtypeStruct((share, count), x.dtype)
    sent = jax.ShapeDtypeStruct((share, count // 2), x.dtype)
    return pl.pallas_call(
        functools.partial(pack_rows_kernel, blocks, replicas, rows),
        out_shape=(own,) + (sent,) * (blocks - 1),
        in_specs=[scalars(), whole()],
        out_specs=(whole(),) * blocks,
        scratch_shapes=[pltpu.VMEM((width, count), x.dtype)],
        compiler_params=params(),
        cost_estimate=pl.CostEstimate(
            flops=0, bytes_accessed=6 * count * width, transcendentals=0
        ),
        name="pack_rows",
    )(at, x)


def attention_kernel(blocks, count, heads, group, *refs):
    at_ref = refs[0]
    packs = refs[1 : 1 + blocks]
    dpacks = refs[1 + blocks : 1 + 2 * blocks]
    low_ref, cos_ref, sin_ref = refs[1 + 2 * blocks : 4 + 2 * blocks]
    first_ref, second_ref = refs[4 + 2 * blocks : 6 + 2 * blocks]
    q_s, k_s, v_s, kt_s, vt_s, d_s, dt_s, dk_s, dv_s = refs[6 + 2 * blocks :]
    scale = QSCALAR ** (-0.5)
    factor = scale * LOG2E
    span = blocks * count
    wide = heads * group * HD
    narrow = heads * HD
    per_block = count // TILE
    reach = -(-(W - 1) // TILE)
    me = at_ref[0]
    for part in range(blocks):
        rows = aligned(me ^ part, count)
        pack = packs[part]
        q_s[rows, :] = pack[:count, :wide]
        keys = pack[:count, wide : wide + narrow]
        values = pack[:count, wide + narrow :]
        k_s[rows, :] = keys
        v_s[rows, :] = values
        kt_s[:, rows] = keys.T
        vt_s[:, rows] = values.T
        d_s[rows, :] = dpacks[part][...]
        dt_s[:, rows] = dpacks[part][...].T
    dk_s[...] = jnp.zeros_like(dk_s)
    dv_s[...] = jnp.zeros_like(dv_s)

    def stored(index):
        return aligned(((index // per_block) ^ me) * per_block + lax.rem(index, per_block), TILE)

    def rotated(grad, rows):
        return grad * cos_ref[rows, :] + pltpu.roll(grad, HD // 2, 1) * sin_ref[rows, :]

    for head in range(heads):
        kv = slice(head * HD, (head + 1) * HD)

        def tile(index, first_key, width):
            index = jnp.int32(index)
            q_rows = aligned(index, TILE)
            t_rows = stored(index)
            k_rows = pl.ds(first_key, width)
            columns = [slice(head * group * HD + g * HD, head * group * HD + (g + 1) * HD) for g in range(group)]
            query = jnp.concatenate([q_s[q_rows, c] for c in columns], axis=0)
            dattn = jnp.concatenate([d_s[q_rows, c] for c in columns], axis=0)
            dattn_t = jnp.concatenate([dt_s[c, q_rows] for c in columns], axis=1)
            scores = dot_nt(k_s[k_rows, kv], query)
            low = jnp.concatenate([low_ref[:, t_rows]] * group, axis=1)
            at = first_key + lax.broadcasted_iota(jnp.int32, (width, group * TILE), 0)
            own = index * TILE + lax.rem(
                lax.broadcasted_iota(jnp.int32, (1, group * TILE), 1), jnp.int32(TILE)
            )
            scores = jnp.where((at >= low) & (at <= own), scores, NEGATIVE)
            top = jnp.max(scores, axis=0, keepdims=True)
            weights = jnp.exp2(scores * factor - top * factor)
            inverse = 1.0 / jnp.sum(weights, axis=0, keepdims=True)
            probs = weights * inverse
            half = probs.astype(jnp.bfloat16)
            attn = dot_nn(vt_s[kv, k_rows], half).astype(jnp.bfloat16)
            dprobs = dot_nt(v_s[k_rows, kv], dattn)
            attn_wide = attn.astype(jnp.float32)
            delta = jnp.sum(dattn_t.astype(jnp.float32) * attn_wide, axis=0, keepdims=True)
            dscores = (probs * (dprobs - delta)).astype(jnp.bfloat16)
            query_grad = (dot_nn(kt_s[kv, k_rows], dscores) * scale).T
            attn_rows = attn_wide.T
            dk_s[k_rows, kv] += dot_nn(dscores, query)
            dv_s[k_rows, kv] += dot_nn(half, dattn)
            for g, c in enumerate(columns):
                part = slice(g * TILE, (g + 1) * TILE)
                first_ref[q_rows, c] = attn_rows[part].astype(jnp.bfloat16)
                second_ref[q_rows, c] = rotated(query_grad[part], t_rows).astype(jnp.bfloat16)

        tiles = span // TILE
        for index in range(min(reach, tiles)):
            tile(index, 0, (index + 1) * TILE)

        def steady(index, carry):
            tile(index, pl.multiple_of((index - reach) * TILE, TILE), (reach + 1) * TILE)
            return carry

        if tiles > reach:
            lax.fori_loop(reach, tiles, steady, 0)
        out = slice(wide + head * HD, wide + (head + 1) * HD)
        for index in range(tiles):
            rows = pl.ds(index * TILE, TILE)
            first_ref[rows, out] = dv_s[rows, kv].astype(jnp.bfloat16)
            second_ref[rows, out] = rotated(
                dk_s[rows, kv] * scale, stored(jnp.int32(index))
            ).astype(jnp.bfloat16)


def attention(at, packs, dpacks, low, cosine, sine, heads, group):
    blocks = len(packs)
    count = dpacks[0].shape[0]
    span = blocks * count
    wide = heads * group * HD
    narrow = heads * HD
    half = jnp.bfloat16
    pairs = heads * group * span * (W + TILE)
    return pl.pallas_call(
        functools.partial(attention_kernel, blocks, count, heads, group),
        out_shape=(jax.ShapeDtypeStruct((span, wide + narrow), half),) * 2,
        in_specs=[scalars()] + [whole()] * (2 * blocks + 3),
        out_specs=(whole(),) * 2,
        scratch_shapes=[
            pltpu.VMEM((span, wide), half),
            pltpu.VMEM((span, narrow), half),
            pltpu.VMEM((span, narrow), half),
            pltpu.VMEM((narrow, span), half),
            pltpu.VMEM((narrow, span), half),
            pltpu.VMEM((span, wide), half),
            pltpu.VMEM((wide, span), half),
            pltpu.VMEM((span, narrow), jnp.float32),
            pltpu.VMEM((span, narrow), jnp.float32),
        ],
        compiler_params=params(),
        cost_estimate=pl.CostEstimate(
            flops=10 * pairs * HD, bytes_accessed=span * wide * 12, transcendentals=pairs
        ),
        name="attention_backward",
    )(at, *packs, *dpacks, low, cosine, sine)


def weight_terms_kernel(blocks, jobs, at_ref, *refs):
    pieces = 1 + 2 * (blocks - 1)
    sets = 1 + max(job[0] for job in jobs)
    piece_refs = refs[: sets * pieces]
    lin_refs = refs[sets * pieces : -1]
    out_ref = refs[-1]
    me, side = at_ref[0], at_ref[1]
    count = piece_refs[0].shape[1]
    half = count // 2
    rows = [aligned(me, count)]
    for part in range(1, blocks):
        rows.append(aligned((me ^ part) * 2 + side, half))
        rows.append(aligned((me ^ part) * 2 + 1 - side, half))
    total = [None] * len(jobs)
    for piece in range(pieces):
        for index, (which, lin, low, high) in enumerate(jobs):
            left = piece_refs[which * pieces + piece][...]
            term = dot_nn(left, lin_refs[lin][rows[piece], low:high])
            total[index] = term if total[index] is None else total[index] + term
    first = 0
    for index, (which, lin, low, high) in enumerate(jobs):
        out_ref[:, first : first + high - low] = total[index].astype(out_ref.dtype)
        first += high - low


def weight_terms(at, sets, lins, jobs, blocks, replicas):
    share = sets[0][0].shape[0]
    rows = share // replicas
    span = lins[0].shape[0]
    cols = sum(job[3] - job[2] for job in jobs)
    pieces = [x for one in sets for x in one]

    def piece(x):
        return pl.BlockSpec((rows, x.shape[1]), lambda i, at: (i, 0))

    def fixed(x):
        return pl.BlockSpec(x.shape, lambda i, at: (0, 0))

    return pl.pallas_call(
        functools.partial(weight_terms_kernel, blocks, jobs),
        out_shape=jax.ShapeDtypeStruct((share, cols), lins[0].dtype),
        grid_spec=pltpu.PrefetchScalarGridSpec(
            num_scalar_prefetch=1,
            grid=(replicas,),
            in_specs=[piece(x) for x in pieces] + [fixed(x) for x in lins],
            out_specs=pl.BlockSpec((rows, cols), lambda i, at: (i, 0)),
        ),
        compiler_params=params(),
        cost_estimate=pl.CostEstimate(
            flops=LOAD * share * span * cols,
            bytes_accessed=2 * share * span * len(sets) + 2 * (span + share) * cols,
            transcendentals=0,
        ),
        name="weight_terms",
    )(at, *pieces, *lins)


def assemble_kernel(places, at_ref, *refs):
    parts, outs = refs[:-4], refs[-4:]
    me = at_ref[0]
    for part, one in zip(parts, places):
        first = 0
        for out, source, cols in one:
            outs[out][:, aligned(me ^ source, cols)] = part[:, first : first + cols].astype(
                jnp.float32
            )
            first += cols


def assemble(at, places, parts, blocks, wide, narrow):
    rows = parts[0].shape[0]
    shapes = [
        jax.ShapeDtypeStruct((rows, blocks * cols), jnp.float32)
        for cols in (wide, narrow, wide, narrow)
    ]
    return pl.pallas_call(
        functools.partial(assemble_kernel, places),
        out_shape=tuple(shapes),
        in_specs=[scalars()] + [whole()] * len(parts),
        out_specs=(whole(),) * 4,
        compiler_params=params(),
        name="assemble",
    )(at, *parts)


def input_terms_kernel(blocks, wide, narrow, at_ref, *refs):
    firsts, seconds = refs[:blocks], refs[blocks : 2 * blocks]
    wq_ref, wk_ref, wv_ref, mine_ref, sent_ref, q_s, k_s, v_s = refs[2 * blocks :]
    me, side = at_ref[0], at_ref[1]

    @pl.when(pl.program_id(0) == 0)
    def _():
        for part in range(blocks):
            there = me ^ part
            q_s[:, aligned(there, wide)] = seconds[part][:, :wide]
            k_s[:, aligned(there, narrow)] = seconds[part][:, wide:]
            v_s[:, aligned(there, narrow)] = firsts[part][:, wide:]

    half = q_s.shape[0] // 2
    for target, which in ((sent_ref, 1 - side), (mine_ref, side)):
        rows = aligned(which, half)
        total = dot_nt(q_s[rows, :], wq_ref[...])
        total = total + dot_nt(k_s[rows, :], wk_ref[...])
        total = total + dot_nt(v_s[rows, :], wv_ref[...])
        target[...] = total.astype(target.dtype)


def input_terms(at, firsts, seconds, w_query, w_key, w_value, count, wide, narrow):
    blocks = len(firsts)
    width = w_query.shape[0]
    step = next(s for s in (768, 512, 256, 128, width) if width % s == 0)

    def own(x):
        return pl.BlockSpec((count, x.shape[1]), lambda i, at: (at[0], 0))

    def weight(x):
        return pl.BlockSpec((step, x.shape[1]), lambda i, at: (i, 0))

    out = pl.BlockSpec((count // 2, step), lambda i, at: (0, i))
    ins = firsts + seconds
    half = jnp.bfloat16
    return pl.pallas_call(
        functools.partial(input_terms_kernel, blocks, wide, narrow),
        out_shape=(
            jax.ShapeDtypeStruct((count // 2, width), jnp.float32),
            jax.ShapeDtypeStruct((count // 2, width), half),
        ),
        grid_spec=pltpu.PrefetchScalarGridSpec(
            num_scalar_prefetch=1,
            grid=(width // step,),
            in_specs=[own(x) for x in ins] + [weight(x) for x in (w_query, w_key, w_value)],
            out_specs=(out, out),
            scratch_shapes=[
                pltpu.VMEM((count, blocks * wide), half),
                pltpu.VMEM((count, blocks * narrow), half),
                pltpu.VMEM((count, blocks * narrow), half),
            ],
        ),
        compiler_params=params(),
        cost_estimate=pl.CostEstimate(
            flops=COST * count * width * blocks * (wide + 2 * narrow),
            bytes_accessed=2 * width * blocks * (wide + 2 * narrow) + 3 * width * count,
            transcendentals=0,
        ),
        name="input_terms",
    )(at, *ins, w_query, w_key, w_value)


def swap(x, axis, by):
    count = lax.axis_size(axis)
    return lax.ppermute(x, axis, [(i, i ^ by) for i in range(count)])


def rotation_tables(places):
    half = HD // 2
    index = jnp.arange(half, dtype=jnp.float32)
    freq = jnp.power(jnp.float32(10000.0), index * (-2.0 / HD))
    angle = places.astype(jnp.float32)[:, None] * freq[None, :]
    cosine = jnp.cos(angle)
    sine = jnp.sin(angle)
    return jnp.concatenate([cosine, cosine], axis=1), jnp.concatenate([sine, -sine], axis=1)


def on_device(
    inputs,
    queries,
    key_states,
    value_states,
    out_grad,
    positions,
    w_query,
    w_key,
    w_value,
    w_output,
):
    count = queries.shape[0]
    head_cols = queries.shape[1]
    kv_cols = key_states.shape[1]
    kv_here = kv_cols // HD
    group = head_cols // kv_cols
    blocks = lax.axis_size("context")
    replicas = lax.axis_size("dp")
    cores = lax.axis_size("tensor")
    width = inputs.shape[1]
    heads = kv_here // blocks
    wide = heads * group * HD
    narrow = heads * HD
    fits = (
        blocks == 4
        and kv_here % blocks == 0
        and cores == 2
        and count % (2 * HD) == 0
        and count % TILE == 0
        and W % TILE == 0
        and width % HD == 0
        and width % (replicas * blocks * EXTRA) == 0
        and wide + 2 * narrow >= count
    )
    if not fits:
        return banded(
            inputs, queries, key_states, value_states, out_grad, positions,
            w_query, w_key, w_value, w_output,
        )
    me = lax.axis_index("context")
    side = lax.axis_index("tensor")
    at = jnp.stack([me, side]).astype(jnp.int32)

    barrier = lax.optimization_barrier

    digits = jnp.stack([positions // RADIX, positions % RADIX]).astype(jnp.bfloat16)
    extra = jnp.pad(digits, ((0, EXTRA - 2), (0, wide + 2 * narrow - count)))
    packs = list(
        pack_heads(at, queries, key_states, value_states, extra, blocks, wide, narrow)
    )
    for part in range(1, blocks):
        packs[part] = swap(packs[part], "context", part)
    dattn = jnp.dot(out_grad, w_output, preferred_element_type=jnp.float32).astype(jnp.bfloat16)
    dpacks = [
        lax.dynamic_slice(dattn, (0, (me ^ part) * wide), (count, wide)) for part in range(blocks)
    ]
    grad_own, *grad_packed = pack_rows(at, out_grad, blocks, replicas)

    def spread(packed):
        return [swap(x, "context", part + 1) for part, x in enumerate(packed)]

    def joined(own, came):
        pieces = [own]
        for x in came:
            pieces += [x, swap(x, "tensor", 1)]
        return pieces

    packs, dpacks, grad_packed = barrier((packs, dpacks, grad_packed))
    dpacks = [dpacks[0]] + spread(dpacks[1:])
    places = [
        (pack[count, :count].astype(jnp.float32) * RADIX + pack[count + 1, :count].astype(jnp.float32)).astype(jnp.int32)
        for pack in packs[1:]
    ]
    places = jnp.concatenate([positions] + places)
    index = jnp.concatenate(
        [(me ^ part) * count + jnp.arange(count, dtype=jnp.int32) for part in range(blocks)]
    )
    low = jnp.maximum(index - places, index - (W - 1))[None, :]
    cosine, sine = rotation_tables(places)
    input_own, *input_packed = pack_rows(at, inputs, blocks, replicas)
    dpacks, input_packed = barrier((dpacks, input_packed))

    grad_came = spread(grad_packed)
    first, second = attention(at, packs, dpacks, low, cosine, sine, heads, group)
    first, second, grad_came, input_packed = barrier((first, second, grad_came, input_packed))

    input_came = spread(input_packed)
    grads = joined(grad_own, grad_came)
    edge = wide + narrow
    def summed(term):
        return lax.psum_scatter(term, "dp", scatter_dimension=0, tiled=True)

    parts = []
    term = weight_terms(at, [grads], [first], [(0, 0, 0, wide)], blocks, replicas)
    parts.append(summed(term))
    term, input_came, first, second = barrier((term, input_came, first, second))

    firsts = [first, swap(first, "context", 1), None, None]
    seconds = [second, None, swap(second, "context", 2), None]
    ins = joined(input_own, input_came)
    jobs = [(0, 0, wide, edge), (0, 1, 0, edge)]
    term = weight_terms(at, [ins], [first, second], jobs, blocks, replicas)
    parts.append(summed(term))
    term, firsts[1], seconds[2], first, second = barrier(
        (term, firsts[1], seconds[2], first, second)
    )
    seconds[1] = swap(second, "context", 1)
    firsts[2] = swap(first, "context", 2)
    jobs = [(0, 0, 0, wide), (1, 0, wide, edge), (1, 1, 0, edge)]

    def terms_of(source_first, source_second):
        lins = [firsts[source_first], seconds[source_second]]
        return weight_terms(at, [grads, ins], lins, jobs, blocks, replicas)

    term = terms_of(1, 2)
    parts.append(summed(term))
    term, parts[0], firsts[1], firsts[2], seconds[1], seconds[2] = barrier(
        (term, parts[0], firsts[1], firsts[2], seconds[1], seconds[2])
    )
    firsts[3] = swap(firsts[1], "context", 2)
    seconds[3] = swap(seconds[2], "context", 1)
    term = terms_of(2, 1)
    parts.append(summed(term))
    term, parts[1], firsts[3], seconds[3] = barrier((term, parts[1], firsts[3], seconds[3]))
    late, term = barrier((at, term))
    mine, sent = input_terms(
        late, firsts, seconds, w_query, w_key, w_value, count, wide, narrow
    )
    came = swap(sent, "tensor", 1)
    mine, parts[2], firsts[3] = barrier((mine, parts[2], firsts[3]))
    term = terms_of(3, 3)
    parts.append(summed(term))
    mine, came, parts[3] = barrier((mine, came, parts[3]))
    input_grad = (mine + came.astype(jnp.float32)).astype(jnp.bfloat16)
    last, input_grad = barrier((at, input_grad))

    def rest(source_first, source_second):
        return [(1, source_first, narrow), (2, source_second, wide), (3, source_second, narrow)]

    layout = [[(0, 0, wide)], rest(0, 0)]
    for source_first, source_second in ((1, 2), (2, 1), (3, 3)):
        layout.append([(0, source_first, wide)] + rest(source_first, source_second))
    grad_output, grad_value, grad_query, grad_key = assemble(
        last, layout, parts, blocks, wide, narrow
    )
    return (input_grad, grad_query, grad_key, grad_value, grad_output)


def solution(mesh):
    return jax.shard_map(
        on_device,
        mesh=mesh,
        in_specs=(
            P(("dp", "context"), None),
            P(("dp", "context"), "tensor"),
            P(("dp", "context"), "tensor"),
            P(("dp", "context"), "tensor"),
            P(("dp", "context"), None),
            P(("dp", "context")),
            P(None, "tensor"),
            P(None, "tensor"),
            P(None, "tensor"),
            P(None, "tensor"),
        ),
        out_specs=(
            P(("dp", "context", "tensor"), None),
            P(("dp", "context"), "tensor"),
            P(("dp", "context"), "tensor"),
            P(("dp", "context"), "tensor"),
            P(("dp", "context"), "tensor"),
        ),
        check_vma=False,
    )
```

```python
import functools

import jax
import jax.numpy as jnp
from jax import lax
from jax.experimental import pallas as pl
from jax.experimental.pallas import tpu as pltpu
from jax.sharding import PartitionSpec as P

HD = 128
W = 1024
QSCALAR = 168


def shifted(x, axis, by):
    count = lax.axis_size(axis)
    pairs = [(i, i + by) for i in range(count) if 0 <= i + by < count]
    return lax.ppermute(x, axis, pairs)


def rotate_back(grads, places):
    count = grads.shape[0]
    half = HD // 2
    index = jnp.arange(half, dtype=jnp.float32)
    freq = jnp.power(jnp.float32(10000.0), index * (-2.0 / HD))
    angle = places.astype(jnp.float32)[:, None] * freq[None, :]
    cosine = jnp.cos(angle)[:, None, :]
    sine = jnp.sin(angle)[:, None, :]
    split = grads.reshape(count, -1, 2, half)
    first = split[:, :, 0, :]
    second = split[:, :, 1, :]
    upper = first * cosine + second * sine
    lower = second * cosine - first * sine
    return jnp.stack([upper, lower], axis=2).reshape(count, -1)


def contract_rows(left, right):
    return lax.dot_general(
        left, right, (((0,), (0,)), ((), ())), preferred_element_type=jnp.float32
    )


def contract_cols(left, right):
    return lax.dot_general(
        left, right, (((1,), (1,)), ((), ())), preferred_element_type=jnp.float32
    )


def banded(
    inputs,
    queries,
    key_states,
    value_states,
    out_grad,
    positions,
    w_query,
    w_key,
    w_value,
    w_output,
):
    count = queries.shape[0]
    head_cols = queries.shape[1]
    kv_cols = key_states.shape[1]
    kv_here = kv_cols // HD
    group = head_cols // kv_cols
    scale = QSCALAR ** (-0.5)
    block = lax.axis_index("context")
    blocks = lax.axis_size("context")
    reach = min((W + count - 2) // count, blocks - 1)
    span = (reach + 1) * count
    key_pieces = []
    value_pieces = []
    for back in range(reach, 0, -1):
        earlier_keys, earlier_values = shifted((key_states, value_states), "context", back)
        key_pieces.append(earlier_keys)
        value_pieces.append(earlier_values)
    band_keys = jnp.concatenate(key_pieces + [key_states], axis=0)
    band_values = jnp.concatenate(value_pieces + [value_states], axis=0)
    query_index = block * count + jnp.arange(count, dtype=jnp.int32)
    key_index = (block - reach) * count + jnp.arange(span, dtype=jnp.int32)
    doc_start = query_index - positions
    allowed = (key_index[None, :] <= query_index[:, None]) & (
        query_index[:, None] - key_index[None, :] < W
    )
    allowed = allowed & (key_index[None, :] >= doc_start[:, None]) & (key_index[None, :] >= 0)
    query_heads = queries.reshape(count, kv_here, group, HD)
    key_heads = band_keys.reshape(span, kv_here, HD)
    value_heads = band_values.reshape(span, kv_here, HD)
    scores = (
        jnp.einsum("qhgd,khd->hgqk", query_heads, key_heads, preferred_element_type=jnp.float32)
        * scale
    )
    scores = jnp.where(allowed, scores, -1e30)
    top = jnp.max(scores, axis=-1, keepdims=True)
    weights = jnp.exp(scores - top)
    probs = weights / jnp.sum(weights, axis=-1, keepdims=True)
    probs_half = probs.astype(jnp.bfloat16)
    attn = jnp.einsum(
        "hgqk,khd->qhgd", probs_half, value_heads, preferred_element_type=jnp.float32
    ).astype(jnp.bfloat16)
    attn_flat = attn.reshape(count, head_cols)
    dattn = jnp.dot(out_grad, w_output, preferred_element_type=jnp.float32).astype(jnp.bfloat16)
    dattn_heads = dattn.reshape(count, kv_here, group, HD)
    dprobs = jnp.einsum(
        "qhgd,khd->hgqk", dattn_heads, value_heads, preferred_element_type=jnp.float32
    )
    delta = jnp.sum(dattn_heads.astype(jnp.float32) * attn.astype(jnp.float32), axis=-1)
    delta = jnp.transpose(delta, (1, 2, 0))[..., None]
    dscores = (probs * (dprobs - delta) * scale).astype(jnp.bfloat16)
    query_grad = jnp.einsum(
        "hgqk,khd->qhgd", dscores, key_heads, preferred_element_type=jnp.float32
    ).reshape(count, head_cols)
    band_key_grad = jnp.einsum(
        "hgqk,qhgd->khd", dscores, query_heads, preferred_element_type=jnp.float32
    ).reshape(span, kv_cols)
    band_value_grad = jnp.einsum(
        "hgqk,qhgd->khd", probs_half, dattn_heads, preferred_element_type=jnp.float32
    ).reshape(span, kv_cols)
    key_grad = band_key_grad[reach * count :]
    value_grad = band_value_grad[reach * count :]
    for back in range(1, reach + 1):
        first_row = (reach - back) * count
        sent_keys, sent_values = shifted(
            (
                band_key_grad[first_row : first_row + count],
                band_value_grad[first_row : first_row + count],
            ),
            "context",
            -back,
        )
        key_grad = key_grad + sent_keys
        value_grad = value_grad + sent_values
    query_lin = rotate_back(query_grad, positions).astype(jnp.bfloat16)
    key_lin = rotate_back(key_grad, positions).astype(jnp.bfloat16)
    value_half = value_grad.astype(jnp.bfloat16)
    total = contract_cols(query_lin, w_query)
    total = total + contract_cols(key_lin, w_key)
    total = total + contract_cols(value_half, w_value)
    input_grad = lax.psum_scatter(total, "tensor", scatter_dimension=0, tiled=True).astype(
        jnp.bfloat16
    )
    terms = (
        contract_rows(inputs, query_lin),
        contract_rows(inputs, key_lin),
        contract_rows(inputs, value_half),
        contract_rows(out_grad, attn_flat),
    )
    summed = (
        lax.psum_scatter(
            terms[0].astype(jnp.bfloat16), ("dp", "context"), scatter_dimension=0, tiled=True
        ).astype(jnp.float32),
        lax.psum_scatter(
            terms[1].astype(jnp.bfloat16), ("dp", "context"), scatter_dimension=0, tiled=True
        ).astype(jnp.float32),
        lax.psum_scatter(
            terms[2].astype(jnp.bfloat16), ("dp", "context"), scatter_dimension=0, tiled=True
        ).astype(jnp.float32),
        lax.psum_scatter(
            terms[3].astype(jnp.bfloat16), ("dp", "context"), scatter_dimension=0, tiled=True
        ).astype(jnp.float32),
    )
    return (input_grad, summed[0], summed[1], summed[2], summed[3])


TILE = 256
EXTRA = 16
RADIX = 128
NEGATIVE = -1e30
LOG2E = 1.4426950408889634
VMEM_LIMIT = 48 * 1024 * 1024
LOAD = 12
COST = 20
CHUNKS = 1
VMEM_MOST = 60 * 1024 * 1024


def dot_nt(left, right):
    return lax.dot_general(
        left, right, (((1,), (1,)), ((), ())), preferred_element_type=jnp.float32
    )


def dot_nn(left, right):
    return lax.dot_general(
        left, right, (((1,), (0,)), ((), ())), preferred_element_type=jnp.float32
    )


def whole():
    return pl.BlockSpec(memory_space=pltpu.VMEM)


def scalars():
    return pl.BlockSpec(memory_space=pltpu.SMEM)


def params(limit=VMEM_LIMIT):
    return pltpu.CompilerParams(vmem_limit_bytes=limit)


def aligned(index, size):
    return pl.ds(pl.multiple_of(index * size, size), size)


def pack_heads_kernel(blocks, wide, narrow, at_ref, q_ref, k_ref, v_ref, extra_ref, *outs):
    me = at_ref[0]
    count = q_ref.shape[0]
    for part in range(blocks):
        there = me ^ part
        out = outs[part]
        out[:count, :wide] = q_ref[:, aligned(there, wide)]
        out[:count, wide : wide + narrow] = k_ref[:, aligned(there, narrow)]
        out[:count, wide + narrow :] = v_ref[:, aligned(there, narrow)]
        out[count:, :] = extra_ref[...]


def pack_heads(at, queries, key_states, value_states, extra, blocks, wide, narrow):
    count = queries.shape[0]
    shape = jax.ShapeDtypeStruct((count + EXTRA, wide + 2 * narrow), queries.dtype)
    return pl.pallas_call(
        functools.partial(pack_heads_kernel, blocks, wide, narrow),
        out_shape=(shape,) * blocks,
        in_specs=[scalars()] + [whole()] * 4,
        out_specs=(whole(),) * blocks,
        compiler_params=params(),
        cost_estimate=pl.CostEstimate(
            flops=0, bytes_accessed=4 * blocks * count * (wide + 2 * narrow), transcendentals=0
        ),
        name="pack_heads",
    )(at, queries, key_states, value_states, extra)


def pack_rows_kernel(blocks, replicas, rows, at_ref, x_ref, own_ref, *rest):
    outs, turned = rest[:-1], rest[-1]
    me, side = at_ref[0], at_ref[1]
    count, width = x_ref.shape
    half = count // 2

    def turn(index, carry):
        cols = aligned(index, HD)
        turned[cols, :] = x_ref[:, cols].T
        return carry

    lax.fori_loop(0, width // HD, turn, 0)
    for replica in range(replicas):
        into = pl.ds(replica * rows, rows)
        own_ref[into, :] = turned[aligned(replica * blocks + me, rows), :]
        for part in range(1, blocks):
            taken = aligned(replica * blocks + (me ^ part), rows)
            outs[part - 1][into, :] = turned[taken, aligned(side, half)]


def pack_rows(at, x, blocks, replicas):
    count, width = x.shape
    rows = width // (replicas * blocks)
    share = replicas * rows
    own = jax.ShapeDtypeStruct((share, count), x.dtype)
    sent = jax.ShapeDtypeStruct((share, count // 2), x.dtype)
    return pl.pallas_call(
        functools.partial(pack_rows_kernel, blocks, replicas, rows),
        out_shape=(own,) + (sent,) * (blocks - 1),
        in_specs=[scalars(), whole()],
        out_specs=(whole(),) * blocks,
        scratch_shapes=[pltpu.VMEM((width, count), x.dtype)],
        compiler_params=params(),
        cost_estimate=pl.CostEstimate(
            flops=0, bytes_accessed=6 * count * width, transcendentals=0
        ),
        name="pack_rows",
    )(at, x)


def attention_kernel(blocks, count, heads, group, *refs):
    at_ref = refs[0]
    packs = refs[1 : 1 + blocks]
    dpacks = refs[1 + blocks : 1 + 2 * blocks]
    low_ref, cos_ref, sin_ref = refs[1 + 2 * blocks : 4 + 2 * blocks]
    first_ref, second_ref = refs[4 + 2 * blocks : 6 + 2 * blocks]
    q_s, k_s, v_s, kt_s, vt_s, d_s, dt_s, dk_s, dv_s = refs[6 + 2 * blocks :]
    scale = QSCALAR ** (-0.5)
    factor = scale * LOG2E
    span = blocks * count
    wide = heads * group * HD
    narrow = heads * HD
    per_block = count // TILE
    reach = -(-(W - 1) // TILE)
    me = at_ref[0]
    for part in range(blocks):
        rows = aligned(me ^ part, count)
        pack = packs[part]
        q_s[rows, :] = pack[:count, :wide]
        keys = pack[:count, wide : wide + narrow]
        values = pack[:count, wide + narrow :]
        k_s[rows, :] = keys
        v_s[rows, :] = values
        kt_s[:, rows] = keys.T
        vt_s[:, rows] = values.T
        d_s[rows, :] = dpacks[part][...]
        dt_s[:, rows] = dpacks[part][...].T
    dk_s[...] = jnp.zeros_like(dk_s)
    dv_s[...] = jnp.zeros_like(dv_s)

    def stored(index):
        return aligned(((index // per_block) ^ me) * per_block + lax.rem(index, per_block), TILE)

    def rotated(grad, rows):
        return grad * cos_ref[rows, :] + pltpu.roll(grad, HD // 2, 1) * sin_ref[rows, :]

    for head in range(heads):
        kv = slice(head * HD, (head + 1) * HD)

        def tile(index, first_key, width):
            index = jnp.int32(index)
            q_rows = aligned(index, TILE)
            t_rows = stored(index)
            k_rows = pl.ds(first_key, width)
            columns = [slice(head * group * HD + g * HD, head * group * HD + (g + 1) * HD) for g in range(group)]
            query = jnp.concatenate([q_s[q_rows, c] for c in columns], axis=0)
            dattn = jnp.concatenate([d_s[q_rows, c] for c in columns], axis=0)
            dattn_t = jnp.concatenate([dt_s[c, q_rows] for c in columns], axis=1)
            scores = dot_nt(k_s[k_rows, kv], query)
            low = jnp.concatenate([low_ref[:, t_rows]] * group, axis=1)
            at = first_key + lax.broadcasted_iota(jnp.int32, (width, group * TILE), 0)
            own = index * TILE + lax.rem(
                lax.broadcasted_iota(jnp.int32, (1, group * TILE), 1), jnp.int32(TILE)
            )
            scores = jnp.where((at >= low) & (at <= own), scores, NEGATIVE)
            top = jnp.max(scores, axis=0, keepdims=True)
            weights = jnp.exp2(scores * factor - top * factor)
            inverse = 1.0 / jnp.sum(weights, axis=0, keepdims=True)
            probs = weights * inverse
            half = probs.astype(jnp.bfloat16)
            attn = dot_nn(vt_s[kv, k_rows], half).astype(jnp.bfloat16)
            dprobs = dot_nt(v_s[k_rows, kv], dattn)
            attn_wide = attn.astype(jnp.float32)
            delta = jnp.sum(dattn_t.astype(jnp.float32) * attn_wide, axis=0, keepdims=True)
            dscores = (probs * (dprobs - delta)).astype(jnp.bfloat16)
            query_grad = (dot_nn(kt_s[kv, k_rows], dscores) * scale).T
            attn_rows = attn_wide.T
            dk_s[k_rows, kv] += dot_nn(dscores, query)
            dv_s[k_rows, kv] += dot_nn(half, dattn)
            for g, c in enumerate(columns):
                part = slice(g * TILE, (g + 1) * TILE)
                first_ref[q_rows, c] = attn_rows[part].astype(jnp.bfloat16)
                second_ref[q_rows, c] = rotated(query_grad[part], t_rows).astype(jnp.bfloat16)

        tiles = span // TILE
        for index in range(min(reach, tiles)):
            tile(index, 0, (index + 1) * TILE)

        def steady(index, carry):
            tile(index, pl.multiple_of((index - reach) * TILE, TILE), (reach + 1) * TILE)
            return carry

        if tiles > reach:
            lax.fori_loop(reach, tiles, steady, 0)
        out = slice(wide + head * HD, wide + (head + 1) * HD)
        for index in range(tiles):
            rows = pl.ds(index * TILE, TILE)
            first_ref[rows, out] = dv_s[rows, kv].astype(jnp.bfloat16)
            second_ref[rows, out] = rotated(
                dk_s[rows, kv] * scale, stored(jnp.int32(index))
            ).astype(jnp.bfloat16)


def attention(at, packs, dpacks, low, cosine, sine, heads, group):
    blocks = len(packs)
    count = dpacks[0].shape[0]
    span = blocks * count
    wide = heads * group * HD
    narrow = heads * HD
    half = jnp.bfloat16
    pairs = heads * group * span * (W + TILE)
    return pl.pallas_call(
        functools.partial(attention_kernel, blocks, count, heads, group),
        out_shape=(jax.ShapeDtypeStruct((span, wide + narrow), half),) * 2,
        in_specs=[scalars()] + [whole()] * (2 * blocks + 3),
        out_specs=(whole(),) * 2,
        scratch_shapes=[
            pltpu.VMEM((span, wide), half),
            pltpu.VMEM((span, narrow), half),
            pltpu.VMEM((span, narrow), half),
            pltpu.VMEM((narrow, span), half),
            pltpu.VMEM((narrow, span), half),
            pltpu.VMEM((span, wide), half),
            pltpu.VMEM((wide, span), half),
            pltpu.VMEM((span, narrow), jnp.float32),
            pltpu.VMEM((span, narrow), jnp.float32),
        ],
        compiler_params=params(),
        cost_estimate=pl.CostEstimate(
            flops=10 * pairs * HD, bytes_accessed=span * wide * 12, transcendentals=pairs
        ),
        name="attention_backward",
    )(at, *packs, *dpacks, low, cosine, sine)


def weight_terms_kernel(blocks, jobs, at_ref, *refs):
    pieces = 1 + 2 * (blocks - 1)
    sets = 1 + max(job[0] for job in jobs)
    piece_refs = refs[: sets * pieces]
    lin_refs = refs[sets * pieces : -1]
    out_ref = refs[-1]
    me, side = at_ref[0], at_ref[1]
    count = piece_refs[0].shape[1]
    half = count // 2
    rows = [aligned(me, count)]
    for part in range(1, blocks):
        rows.append(aligned((me ^ part) * 2 + side, half))
        rows.append(aligned((me ^ part) * 2 + 1 - side, half))
    total = [None] * len(jobs)
    for piece in range(pieces):
        for index, (which, lin, low, high) in enumerate(jobs):
            left = piece_refs[which * pieces + piece][...]
            term = dot_nn(left, lin_refs[lin][rows[piece], low:high])
            total[index] = term if total[index] is None else total[index] + term
    first = 0
    for index, (which, lin, low, high) in enumerate(jobs):
        out_ref[:, first : first + high - low] = total[index].astype(out_ref.dtype)
        first += high - low


def weight_terms(at, sets, lins, jobs, blocks, replicas):
    share = sets[0][0].shape[0]
    rows = share // replicas
    span = lins[0].shape[0]
    cols = sum(job[3] - job[2] for job in jobs)
    pieces = [x for one in sets for x in one]

    def piece(x):
        return pl.BlockSpec((rows, x.shape[1]), lambda i, at: (i, 0))

    def fixed(x):
        return pl.BlockSpec(x.shape, lambda i, at: (0, 0))

    return pl.pallas_call(
        functools.partial(weight_terms_kernel, blocks, jobs),
        out_shape=jax.ShapeDtypeStruct((share, cols), lins[0].dtype),
        grid_spec=pltpu.PrefetchScalarGridSpec(
            num_scalar_prefetch=1,
            grid=(replicas,),
            in_specs=[piece(x) for x in pieces] + [fixed(x) for x in lins],
            out_specs=pl.BlockSpec((rows, cols), lambda i, at: (i, 0)),
        ),
        compiler_params=params(VMEM_MOST),
        cost_estimate=pl.CostEstimate(
            flops=LOAD * share * span * cols,
            bytes_accessed=2 * share * span * len(sets) + 2 * (span + share) * cols,
            transcendentals=0,
        ),
        name="weight_terms",
    )(at, *pieces, *lins)


def assemble_kernel(places, at_ref, *refs):
    parts, outs = refs[:-4], refs[-4:]
    me = at_ref[0]
    for part, one in zip(parts, places):
        first = 0
        for out, source, cols in one:
            outs[out][:, aligned(me ^ source, cols)] = part[:, first : first + cols].astype(
                jnp.float32
            )
            first += cols


def assemble(at, places, parts, blocks, wide, narrow):
    rows = parts[0].shape[0]
    shapes = [
        jax.ShapeDtypeStruct((rows, blocks * cols), jnp.float32)
        for cols in (wide, narrow, wide, narrow)
    ]
    return pl.pallas_call(
        functools.partial(assemble_kernel, places),
        out_shape=tuple(shapes),
        in_specs=[scalars()] + [whole()] * len(parts),
        out_specs=(whole(),) * 4,
        compiler_params=params(),
        name="assemble",
    )(at, *parts)


def input_terms_kernel(blocks, wide, narrow, at_ref, *refs):
    firsts, seconds = refs[:blocks], refs[blocks : 2 * blocks]
    wq_ref, wk_ref, wv_ref, mine_ref, sent_ref, q_s, k_s, v_s = refs[2 * blocks :]
    me, side = at_ref[0], at_ref[1]

    @pl.when(pl.program_id(0) == 0)
    def _():
        for part in range(blocks):
            there = me ^ part
            q_s[:, aligned(there, wide)] = seconds[part][:, :wide]
            k_s[:, aligned(there, narrow)] = seconds[part][:, wide:]
            v_s[:, aligned(there, narrow)] = firsts[part][:, wide:]

    half = q_s.shape[0] // 2
    for target, which in ((sent_ref, 1 - side), (mine_ref, side)):
        rows = aligned(which, half)
        total = dot_nt(q_s[rows, :], wq_ref[...])
        total = total + dot_nt(k_s[rows, :], wk_ref[...])
        total = total + dot_nt(v_s[rows, :], wv_ref[...])
        target[...] = total.astype(target.dtype)


def input_terms(at, firsts, seconds, w_query, w_key, w_value, count, wide, narrow):
    blocks = len(firsts)
    width = w_query.shape[0]
    step = next(s for s in (768, 512, 256, 128, width) if width % s == 0)

    def own(x):
        return pl.BlockSpec((count, x.shape[1]), lambda i, at: (at[0], 0))

    def weight(x):
        return pl.BlockSpec((step, x.shape[1]), lambda i, at: (i, 0))

    out = pl.BlockSpec((count // 2, step), lambda i, at: (0, i))
    ins = firsts + seconds
    half = jnp.bfloat16
    return pl.pallas_call(
        functools.partial(input_terms_kernel, blocks, wide, narrow),
        out_shape=(
            jax.ShapeDtypeStruct((count // 2, width), jnp.float32),
            jax.ShapeDtypeStruct((count // 2, width), half),
        ),
        grid_spec=pltpu.PrefetchScalarGridSpec(
            num_scalar_prefetch=1,
            grid=(width // step,),
            in_specs=[own(x) for x in ins] + [weight(x) for x in (w_query, w_key, w_value)],
            out_specs=(out, out),
            scratch_shapes=[
                pltpu.VMEM((count, blocks * wide), half),
                pltpu.VMEM((count, blocks * narrow), half),
                pltpu.VMEM((count, blocks * narrow), half),
            ],
        ),
        compiler_params=params(VMEM_MOST),
        cost_estimate=pl.CostEstimate(
            flops=COST * count * width * blocks * (wide + 2 * narrow),
            bytes_accessed=2 * width * blocks * (wide + 2 * narrow) + 3 * width * count,
            transcendentals=0,
        ),
        name="input_terms",
    )(at, *ins, w_query, w_key, w_value)


def swap(x, axis, by):
    count = lax.axis_size(axis)
    return lax.ppermute(x, axis, [(i, i ^ by) for i in range(count)])


def rotation_tables(places):
    half = HD // 2
    index = jnp.arange(half, dtype=jnp.float32)
    freq = jnp.power(jnp.float32(10000.0), index * (-2.0 / HD))
    angle = places.astype(jnp.float32)[:, None] * freq[None, :]
    cosine = jnp.cos(angle)
    sine = jnp.sin(angle)
    return jnp.concatenate([cosine, cosine], axis=1), jnp.concatenate([sine, -sine], axis=1)


def on_device(
    inputs,
    queries,
    key_states,
    value_states,
    out_grad,
    positions,
    w_query,
    w_key,
    w_value,
    w_output,
):
    count = queries.shape[0]
    head_cols = queries.shape[1]
    kv_cols = key_states.shape[1]
    kv_here = kv_cols // HD
    group = head_cols // kv_cols
    blocks = lax.axis_size("context")
    replicas = lax.axis_size("dp")
    cores = lax.axis_size("tensor")
    width = inputs.shape[1]
    heads = kv_here // blocks
    wide = heads * group * HD
    narrow = heads * HD
    fits = (
        blocks == 4
        and kv_here % blocks == 0
        and cores == 2
        and count % (2 * HD) == 0
        and count % TILE == 0
        and W % TILE == 0
        and width % HD == 0
        and width % (replicas * blocks * EXTRA) == 0
        and wide + 2 * narrow >= count
    )
    if not fits:
        return banded(
            inputs, queries, key_states, value_states, out_grad, positions,
            w_query, w_key, w_value, w_output,
        )
    me = lax.axis_index("context")
    side = lax.axis_index("tensor")
    at = jnp.stack([me, side]).astype(jnp.int32)

    barrier = lax.optimization_barrier

    digits = jnp.stack([positions // RADIX, positions % RADIX]).astype(jnp.bfloat16)
    extra = jnp.pad(digits, ((0, EXTRA - 2), (0, wide + 2 * narrow - count)))
    packs = list(
        pack_heads(at, queries, key_states, value_states, extra, blocks, wide, narrow)
    )
    after, packs = barrier((out_grad, packs))
    for part in range(1, blocks):
        packs[part] = swap(packs[part], "context", part)
    dattn = jnp.dot(after, w_output, preferred_element_type=jnp.float32).astype(jnp.bfloat16)
    dpacks = [
        lax.dynamic_slice(dattn, (0, (me ^ part) * wide), (count, wide)) for part in range(blocks)
    ]
    def spread(packed):
        return [swap(x, "context", part + 1) for part, x in enumerate(packed)]

    def joined(own, came):
        pieces = [own]
        for x in came:
            pieces += [x, swap(x, "tensor", 1)]
        return pieces

    soon, dpacks = barrier((at, dpacks))
    grad_own, *grad_packed = pack_rows(soon, out_grad, blocks, replicas)
    dpacks = [dpacks[0]] + spread(dpacks[1:])
    places = [
        (pack[count, :count].astype(jnp.float32) * RADIX + pack[count + 1, :count].astype(jnp.float32)).astype(jnp.int32)
        for pack in packs[1:]
    ]
    places = jnp.concatenate([positions] + places)
    index = jnp.concatenate(
        [(me ^ part) * count + jnp.arange(count, dtype=jnp.int32) for part in range(blocks)]
    )
    low = jnp.maximum(index - places, index - (W - 1))[None, :]
    cosine, sine = rotation_tables(places)
    soon, grad_packed = barrier((soon, grad_packed))
    input_own, *input_packed = pack_rows(soon, inputs, blocks, replicas)
    dpacks, grad_packed, input_packed = barrier((dpacks, grad_packed, input_packed))

    grad_came = spread(grad_packed)
    first, second = attention(at, packs, dpacks, low, cosine, sine, heads, group)
    first, second, grad_came, input_packed = barrier((first, second, grad_came, input_packed))

    input_came = spread(input_packed)
    grads = joined(grad_own, grad_came)
    edge = wide + narrow
    def summed(term):
        return lax.psum_scatter(term, "dp", scatter_dimension=0, tiled=True)

    parts = []
    term = weight_terms(at, [grads], [first], [(0, 0, 0, wide)], blocks, replicas)
    parts.append(summed(term))
    term, parts[0], input_came, first, second = barrier(
        (term, parts[0], input_came, first, second)
    )

    firsts = [first, swap(first, "context", 1), None, None]
    seconds = [second, None, swap(second, "context", 2), None]
    ins = joined(input_own, input_came)
    jobs = [(0, 0, wide, edge), (0, 1, 0, edge)]
    term = weight_terms(at, [ins], [first, second], jobs, blocks, replicas)
    parts.append(summed(term))
    term, firsts[1], seconds[2], first, second = barrier(
        (term, firsts[1], seconds[2], first, second)
    )
    seconds[1] = swap(second, "context", 1)
    firsts[2] = swap(first, "context", 2)
    jobs = [(0, 0, 0, wide), (1, 0, wide, edge), (1, 1, 0, edge)]

    def terms_of(source_first, source_second):
        lins = [firsts[source_first], seconds[source_second]]
        return weight_terms(at, [grads, ins], lins, jobs, blocks, replicas)

    term = terms_of(1, 2)
    parts.append(summed(term))
    term, firsts[1], firsts[2], seconds[1], seconds[2] = barrier(
        (term, firsts[1], firsts[2], seconds[1], seconds[2])
    )
    firsts[3] = swap(firsts[1], "context", 2)
    seconds[3] = swap(seconds[2], "context", 1)
    term = terms_of(2, 1)
    parts.append(summed(term))
    term, parts[1], firsts[3], seconds[3] = barrier((term, parts[1], firsts[3], seconds[3]))
    late, term = barrier((at, term))
    mine, sent = input_terms(
        late, firsts, seconds, w_query, w_key, w_value, count, wide, narrow
    )
    came = swap(sent, "tensor", 1)
    mine, parts[2], firsts[3] = barrier((mine, parts[2], firsts[3]))
    term = terms_of(3, 3)
    parts.append(summed(term))
    mine, came, parts[3] = barrier((mine, came, parts[3]))
    input_grad = (mine + came.astype(jnp.float32)).astype(jnp.bfloat16)
    last, input_grad = barrier((at, input_grad))

    def rest(source_first, source_second):
        return [(1, source_first, narrow), (2, source_second, wide), (3, source_second, narrow)]

    layout = [[(0, 0, wide)], rest(0, 0)]
    for source_first, source_second in ((1, 2), (2, 1), (3, 3)):
        layout.append([(0, source_first, wide)] + rest(source_first, source_second))
    grad_output, grad_value, grad_query, grad_key = assemble(
        last, layout, parts, blocks, wide, narrow
    )
    return (input_grad, grad_query, grad_key, grad_value, grad_output)


def solution(mesh):
    return jax.shard_map(
        on_device,
        mesh=mesh,
        in_specs=(
            P(("dp", "context"), None),
            P(("dp", "context"), "tensor"),
            P(("dp", "context"), "tensor"),
            P(("dp", "context"), "tensor"),
            P(("dp", "context"), None),
            P(("dp", "context")),
            P(None, "tensor"),
            P(None, "tensor"),
            P(None, "tensor"),
            P(None, "tensor"),
        ),
        out_specs=(
            P(("dp", "context", "tensor"), None),
            P(("dp", "context"), "tensor"),
            P(("dp", "context"), "tensor"),
            P(("dp", "context"), "tensor"),
            P(("dp", "context"), "tensor"),
        ),
        check_vma=False,
    )
```

```python
import functools

import jax
import jax.numpy as jnp
from jax import lax
from jax.experimental import pallas as pl
from jax.experimental.pallas import tpu as pltpu
from jax.sharding import PartitionSpec as P

HD = 128
W = 1024
QSCALAR = 168


def shifted(x, axis, by):
    count = lax.axis_size(axis)
    pairs = [(i, i + by) for i in range(count) if 0 <= i + by < count]
    return lax.ppermute(x, axis, pairs)


def rotate_back(grads, places):
    count = grads.shape[0]
    half = HD // 2
    index = jnp.arange(half, dtype=jnp.float32)
    freq = jnp.power(jnp.float32(10000.0), index * (-2.0 / HD))
    angle = places.astype(jnp.float32)[:, None] * freq[None, :]
    cosine = jnp.cos(angle)[:, None, :]
    sine = jnp.sin(angle)[:, None, :]
    split = grads.reshape(count, -1, 2, half)
    first = split[:, :, 0, :]
    second = split[:, :, 1, :]
    upper = first * cosine + second * sine
    lower = second * cosine - first * sine
    return jnp.stack([upper, lower], axis=2).reshape(count, -1)


def contract_rows(left, right):
    return lax.dot_general(
        left, right, (((0,), (0,)), ((), ())), preferred_element_type=jnp.float32
    )


def contract_cols(left, right):
    return lax.dot_general(
        left, right, (((1,), (1,)), ((), ())), preferred_element_type=jnp.float32
    )


def banded(
    inputs,
    queries,
    key_states,
    value_states,
    out_grad,
    positions,
    w_query,
    w_key,
    w_value,
    w_output,
):
    count = queries.shape[0]
    head_cols = queries.shape[1]
    kv_cols = key_states.shape[1]
    kv_here = kv_cols // HD
    group = head_cols // kv_cols
    scale = QSCALAR ** (-0.5)
    block = lax.axis_index("context")
    blocks = lax.axis_size("context")
    reach = min((W + count - 2) // count, blocks - 1)
    span = (reach + 1) * count
    key_pieces = []
    value_pieces = []
    for back in range(reach, 0, -1):
        earlier_keys, earlier_values = shifted((key_states, value_states), "context", back)
        key_pieces.append(earlier_keys)
        value_pieces.append(earlier_values)
    band_keys = jnp.concatenate(key_pieces + [key_states], axis=0)
    band_values = jnp.concatenate(value_pieces + [value_states], axis=0)
    query_index = block * count + jnp.arange(count, dtype=jnp.int32)
    key_index = (block - reach) * count + jnp.arange(span, dtype=jnp.int32)
    doc_start = query_index - positions
    allowed = (key_index[None, :] <= query_index[:, None]) & (
        query_index[:, None] - key_index[None, :] < W
    )
    allowed = allowed & (key_index[None, :] >= doc_start[:, None]) & (key_index[None, :] >= 0)
    query_heads = queries.reshape(count, kv_here, group, HD)
    key_heads = band_keys.reshape(span, kv_here, HD)
    value_heads = band_values.reshape(span, kv_here, HD)
    scores = (
        jnp.einsum("qhgd,khd->hgqk", query_heads, key_heads, preferred_element_type=jnp.float32)
        * scale
    )
    scores = jnp.where(allowed, scores, -1e30)
    top = jnp.max(scores, axis=-1, keepdims=True)
    weights = jnp.exp(scores - top)
    probs = weights / jnp.sum(weights, axis=-1, keepdims=True)
    probs_half = probs.astype(jnp.bfloat16)
    attn = jnp.einsum(
        "hgqk,khd->qhgd", probs_half, value_heads, preferred_element_type=jnp.float32
    ).astype(jnp.bfloat16)
    attn_flat = attn.reshape(count, head_cols)
    dattn = jnp.dot(out_grad, w_output, preferred_element_type=jnp.float32).astype(jnp.bfloat16)
    dattn_heads = dattn.reshape(count, kv_here, group, HD)
    dprobs = jnp.einsum(
        "qhgd,khd->hgqk", dattn_heads, value_heads, preferred_element_type=jnp.float32
    )
    delta = jnp.sum(dattn_heads.astype(jnp.float32) * attn.astype(jnp.float32), axis=-1)
    delta = jnp.transpose(delta, (1, 2, 0))[..., None]
    dscores = (probs * (dprobs - delta) * scale).astype(jnp.bfloat16)
    query_grad = jnp.einsum(
        "hgqk,khd->qhgd", dscores, key_heads, preferred_element_type=jnp.float32
    ).reshape(count, head_cols)
    band_key_grad = jnp.einsum(
        "hgqk,qhgd->khd", dscores, query_heads, preferred_element_type=jnp.float32
    ).reshape(span, kv_cols)
    band_value_grad = jnp.einsum(
        "hgqk,qhgd->khd", probs_half, dattn_heads, preferred_element_type=jnp.float32
    ).reshape(span, kv_cols)
    key_grad = band_key_grad[reach * count :]
    value_grad = band_value_grad[reach * count :]
    for back in range(1, reach + 1):
        first_row = (reach - back) * count
        sent_keys, sent_values = shifted(
            (
                band_key_grad[first_row : first_row + count],
                band_value_grad[first_row : first_row + count],
            ),
            "context",
            -back,
        )
        key_grad = key_grad + sent_keys
        value_grad = value_grad + sent_values
    query_lin = rotate_back(query_grad, positions).astype(jnp.bfloat16)
    key_lin = rotate_back(key_grad, positions).astype(jnp.bfloat16)
    value_half = value_grad.astype(jnp.bfloat16)
    total = contract_cols(query_lin, w_query)
    total = total + contract_cols(key_lin, w_key)
    total = total + contract_cols(value_half, w_value)
    input_grad = lax.psum_scatter(total, "tensor", scatter_dimension=0, tiled=True).astype(
        jnp.bfloat16
    )
    terms = (
        contract_rows(inputs, query_lin),
        contract_rows(inputs, key_lin),
        contract_rows(inputs, value_half),
        contract_rows(out_grad, attn_flat),
    )
    summed = (
        lax.psum_scatter(
            terms[0].astype(jnp.bfloat16), ("dp", "context"), scatter_dimension=0, tiled=True
        ).astype(jnp.float32),
        lax.psum_scatter(
            terms[1].astype(jnp.bfloat16), ("dp", "context"), scatter_dimension=0, tiled=True
        ).astype(jnp.float32),
        lax.psum_scatter(
            terms[2].astype(jnp.bfloat16), ("dp", "context"), scatter_dimension=0, tiled=True
        ).astype(jnp.float32),
        lax.psum_scatter(
            terms[3].astype(jnp.bfloat16), ("dp", "context"), scatter_dimension=0, tiled=True
        ).astype(jnp.float32),
    )
    return (input_grad, summed[0], summed[1], summed[2], summed[3])


TILE = 256
EXTRA = 16
RADIX = 128
NEGATIVE = -1e30
LOG2E = 1.4426950408889634
VMEM_LIMIT = 48 * 1024 * 1024
LOAD = 12
LOAD1 = 12
LOAD2 = 12
COST = 20
VMEM_MOST = 60 * 1024 * 1024


def dot_nt(left, right):
    return lax.dot_general(
        left, right, (((1,), (1,)), ((), ())), preferred_element_type=jnp.float32
    )


def dot_nn(left, right):
    return lax.dot_general(
        left, right, (((1,), (0,)), ((), ())), preferred_element_type=jnp.float32
    )


def whole():
    return pl.BlockSpec(memory_space=pltpu.VMEM)


def scalars():
    return pl.BlockSpec(memory_space=pltpu.SMEM)


def params(limit=VMEM_LIMIT):
    return pltpu.CompilerParams(vmem_limit_bytes=limit)


def aligned(index, size):
    return pl.ds(pl.multiple_of(index * size, size), size)


def pack_heads_kernel(blocks, wide, narrow, at_ref, q_ref, k_ref, v_ref, extra_ref, *outs):
    me = at_ref[0]
    count = q_ref.shape[0]
    for part in range(blocks):
        there = me ^ part
        out = outs[part]
        out[:count, :wide] = q_ref[:, aligned(there, wide)]
        out[:count, wide : wide + narrow] = k_ref[:, aligned(there, narrow)]
        out[:count, wide + narrow :] = v_ref[:, aligned(there, narrow)]
        out[count:, :] = extra_ref[...]


def pack_heads(at, queries, key_states, value_states, extra, blocks, wide, narrow):
    count = queries.shape[0]
    shape = jax.ShapeDtypeStruct((count + EXTRA, wide + 2 * narrow), queries.dtype)
    return pl.pallas_call(
        functools.partial(pack_heads_kernel, blocks, wide, narrow),
        out_shape=(shape,) * blocks,
        in_specs=[scalars()] + [whole()] * 4,
        out_specs=(whole(),) * blocks,
        compiler_params=params(),
        cost_estimate=pl.CostEstimate(
            flops=0, bytes_accessed=4 * blocks * count * (wide + 2 * narrow), transcendentals=0
        ),
        name="pack_heads",
    )(at, queries, key_states, value_states, extra)


def pack_rows_kernel(blocks, replicas, rows, at_ref, x_ref, own_ref, *rest):
    outs, turned = rest[:-1], rest[-1]
    me, side = at_ref[0], at_ref[1]
    count, width = x_ref.shape
    half = count // 2

    def turn(index, carry):
        cols = aligned(index, HD)
        turned[cols, :] = x_ref[:, cols].T
        return carry

    lax.fori_loop(0, width // HD, turn, 0)
    for replica in range(replicas):
        into = pl.ds(replica * rows, rows)
        own_ref[into, :] = turned[aligned(replica * blocks + me, rows), :]
        for part in range(1, blocks):
            taken = aligned(replica * blocks + (me ^ part), rows)
            outs[part - 1][into, :] = turned[taken, aligned(side, half)]


def pack_rows(at, x, blocks, replicas):
    count, width = x.shape
    rows = width // (replicas * blocks)
    share = replicas * rows
    own = jax.ShapeDtypeStruct((share, count), x.dtype)
    sent = jax.ShapeDtypeStruct((share, count // 2), x.dtype)
    return pl.pallas_call(
        functools.partial(pack_rows_kernel, blocks, replicas, rows),
        out_shape=(own,) + (sent,) * (blocks - 1),
        in_specs=[scalars(), whole()],
        out_specs=(whole(),) * blocks,
        scratch_shapes=[pltpu.VMEM((width, count), x.dtype)],
        compiler_params=params(),
        cost_estimate=pl.CostEstimate(
            flops=0, bytes_accessed=6 * count * width, transcendentals=0
        ),
        name="pack_rows",
    )(at, x)


def attention_kernel(blocks, count, heads, group, *refs):
    at_ref = refs[0]
    packs = refs[1 : 1 + blocks]
    dpacks = refs[1 + blocks : 1 + 2 * blocks]
    low_ref, cos_ref, sin_ref = refs[1 + 2 * blocks : 4 + 2 * blocks]
    first_ref, second_ref = refs[4 + 2 * blocks : 6 + 2 * blocks]
    q_s, k_s, v_s, kt_s, vt_s, d_s, dt_s, dk_s, dv_s = refs[6 + 2 * blocks :]
    scale = QSCALAR ** (-0.5)
    factor = scale * LOG2E
    span = blocks * count
    wide = heads * group * HD
    narrow = heads * HD
    per_block = count // TILE
    reach = -(-(W - 1) // TILE)
    me = at_ref[0]
    for part in range(blocks):
        rows = aligned(me ^ part, count)
        pack = packs[part]
        q_s[rows, :] = pack[:count, :wide]
        keys = pack[:count, wide : wide + narrow]
        values = pack[:count, wide + narrow :]
        k_s[rows, :] = keys
        v_s[rows, :] = values
        kt_s[:, rows] = keys.T
        vt_s[:, rows] = values.T
        d_s[rows, :] = dpacks[part][...]
        dt_s[:, rows] = dpacks[part][...].T
    dk_s[...] = jnp.zeros_like(dk_s)
    dv_s[...] = jnp.zeros_like(dv_s)

    def stored(index):
        return aligned(((index // per_block) ^ me) * per_block + lax.rem(index, per_block), TILE)

    def rotated(grad, rows):
        return grad * cos_ref[rows, :] + pltpu.roll(grad, HD // 2, 1) * sin_ref[rows, :]

    for head in range(heads):
        kv = slice(head * HD, (head + 1) * HD)

        def tile(index, first_key, width):
            index = jnp.int32(index)
            q_rows = aligned(index, TILE)
            t_rows = stored(index)
            k_rows = pl.ds(first_key, width)
            columns = [slice(head * group * HD + g * HD, head * group * HD + (g + 1) * HD) for g in range(group)]
            query = jnp.concatenate([q_s[q_rows, c] for c in columns], axis=0)
            dattn = jnp.concatenate([d_s[q_rows, c] for c in columns], axis=0)
            dattn_t = jnp.concatenate([dt_s[c, q_rows] for c in columns], axis=1)
            scores = dot_nt(k_s[k_rows, kv], query)
            low = jnp.concatenate([low_ref[:, t_rows]] * group, axis=1)
            at = first_key + lax.broadcasted_iota(jnp.int32, (width, group * TILE), 0)
            own = index * TILE + lax.rem(
                lax.broadcasted_iota(jnp.int32, (1, group * TILE), 1), jnp.int32(TILE)
            )
            scores = jnp.where((at >= low) & (at <= own), scores, NEGATIVE)
            top = jnp.max(scores, axis=0, keepdims=True)
            weights = jnp.exp2(scores * factor - top * factor)
            inverse = 1.0 / jnp.sum(weights, axis=0, keepdims=True)
            probs = weights * inverse
            half = probs.astype(jnp.bfloat16)
            attn = dot_nn(vt_s[kv, k_rows], half).astype(jnp.bfloat16)
            dprobs = dot_nt(v_s[k_rows, kv], dattn)
            attn_wide = attn.astype(jnp.float32)
            delta = jnp.sum(dattn_t.astype(jnp.float32) * attn_wide, axis=0, keepdims=True)
            dscores = (probs * (dprobs - delta)).astype(jnp.bfloat16)
            query_grad = (dot_nn(kt_s[kv, k_rows], dscores) * scale).T
            attn_rows = attn_wide.T
            dk_s[k_rows, kv] += dot_nn(dscores, query)
            dv_s[k_rows, kv] += dot_nn(half, dattn)
            for g, c in enumerate(columns):
                part = slice(g * TILE, (g + 1) * TILE)
                first_ref[q_rows, c] = attn_rows[part].astype(jnp.bfloat16)
                second_ref[q_rows, c] = rotated(query_grad[part], t_rows).astype(jnp.bfloat16)

        tiles = span // TILE
        for index in range(min(reach, tiles)):
            tile(index, 0, (index + 1) * TILE)

        def steady(index, carry):
            tile(index, pl.multiple_of((index - reach) * TILE, TILE), (reach + 1) * TILE)
            return carry

        if tiles > reach:
            lax.fori_loop(reach, tiles, steady, 0)
        out = slice(wide + head * HD, wide + (head + 1) * HD)
        for index in range(tiles):
            rows = pl.ds(index * TILE, TILE)
            first_ref[rows, out] = dv_s[rows, kv].astype(jnp.bfloat16)
            second_ref[rows, out] = rotated(
                dk_s[rows, kv] * scale, stored(jnp.int32(index))
            ).astype(jnp.bfloat16)


def attention(at, packs, dpacks, low, cosine, sine, heads, group):
    blocks = len(packs)
    count = dpacks[0].shape[0]
    span = blocks * count
    wide = heads * group * HD
    narrow = heads * HD
    half = jnp.bfloat16
    pairs = heads * group * span * (W + TILE)
    return pl.pallas_call(
        functools.partial(attention_kernel, blocks, count, heads, group),
        out_shape=(jax.ShapeDtypeStruct((span, wide + narrow), half),) * 2,
        in_specs=[scalars()] + [whole()] * (2 * blocks + 3),
        out_specs=(whole(),) * 2,
        scratch_shapes=[
            pltpu.VMEM((span, wide), half),
            pltpu.VMEM((span, narrow), half),
            pltpu.VMEM((span, narrow), half),
            pltpu.VMEM((narrow, span), half),
            pltpu.VMEM((narrow, span), half),
            pltpu.VMEM((span, wide), half),
            pltpu.VMEM((wide, span), half),
            pltpu.VMEM((span, narrow), jnp.float32),
            pltpu.VMEM((span, narrow), jnp.float32),
        ],
        compiler_params=params(),
        cost_estimate=pl.CostEstimate(
            flops=10 * pairs * HD, bytes_accessed=span * wide * 12, transcendentals=pairs
        ),
        name="attention_backward",
    )(at, *packs, *dpacks, low, cosine, sine)


def weight_terms_kernel(blocks, jobs, at_ref, *refs):
    pieces = 1 + 2 * (blocks - 1)
    sets = 1 + max(job[0] for job in jobs)
    piece_refs = refs[: sets * pieces]
    lin_refs = refs[sets * pieces : -1]
    out_ref = refs[-1]
    me, side = at_ref[0], at_ref[1]
    count = piece_refs[0].shape[1]
    half = count // 2
    rows = [aligned(me, count)]
    for part in range(1, blocks):
        rows.append(aligned((me ^ part) * 2 + side, half))
        rows.append(aligned((me ^ part) * 2 + 1 - side, half))
    total = [None] * len(jobs)
    for piece in range(pieces):
        for index, (which, lin, low, high) in enumerate(jobs):
            left = piece_refs[which * pieces + piece][...]
            term = dot_nn(left, lin_refs[lin][rows[piece], low:high])
            total[index] = term if total[index] is None else total[index] + term
    first = 0
    for index, (which, lin, low, high) in enumerate(jobs):
        out_ref[:, first : first + high - low] = total[index].astype(out_ref.dtype)
        first += high - low


def weight_terms(at, sets, lins, jobs, blocks, replicas, load=LOAD):
    share = sets[0][0].shape[0]
    rows = share // replicas
    span = lins[0].shape[0]
    cols = sum(job[3] - job[2] for job in jobs)
    pieces = [x for one in sets for x in one]

    def piece(x):
        return pl.BlockSpec((rows, x.shape[1]), lambda i, at: (i, 0))

    def fixed(x):
        return pl.BlockSpec(x.shape, lambda i, at: (0, 0))

    return pl.pallas_call(
        functools.partial(weight_terms_kernel, blocks, jobs),
        out_shape=jax.ShapeDtypeStruct((share, cols), lins[0].dtype),
        grid_spec=pltpu.PrefetchScalarGridSpec(
            num_scalar_prefetch=1,
            grid=(replicas,),
            in_specs=[piece(x) for x in pieces] + [fixed(x) for x in lins],
            out_specs=pl.BlockSpec((rows, cols), lambda i, at: (i, 0)),
        ),
        compiler_params=params(VMEM_MOST),
        cost_estimate=pl.CostEstimate(
            flops=load * share * span * cols,
            bytes_accessed=2 * share * span * len(sets) + 2 * (span + share) * cols,
            transcendentals=0,
        ),
        name="weight_terms",
    )(at, *pieces, *lins)


def assemble_kernel(places, at_ref, *refs):
    parts, outs = refs[:-4], refs[-4:]
    me = at_ref[0]
    for part, one in zip(parts, places):
        first = 0
        for out, source, cols in one:
            outs[out][:, aligned(me ^ source, cols)] = part[:, first : first + cols].astype(
                jnp.float32
            )
            first += cols


def assemble(at, places, parts, blocks, wide, narrow):
    rows = parts[0].shape[0]
    shapes = [
        jax.ShapeDtypeStruct((rows, blocks * cols), jnp.float32)
        for cols in (wide, narrow, wide, narrow)
    ]
    return pl.pallas_call(
        functools.partial(assemble_kernel, places),
        out_shape=tuple(shapes),
        in_specs=[scalars()] + [whole()] * len(parts),
        out_specs=(whole(),) * 4,
        compiler_params=params(),
        name="assemble",
    )(at, *parts)


def input_terms_kernel(blocks, wide, narrow, at_ref, *refs):
    firsts, seconds = refs[:blocks], refs[blocks : 2 * blocks]
    wq_ref, wk_ref, wv_ref, mine_ref, sent_ref, q_s, k_s, v_s, total_s = refs[2 * blocks :]
    me, side = at_ref[0], at_ref[1]

    @pl.when(pl.program_id(0) == 0)
    def _():
        for part in range(blocks):
            there = me ^ part
            q_s[:, aligned(there, wide)] = seconds[part][:, :wide]
            k_s[:, aligned(there, narrow)] = seconds[part][:, wide:]
            v_s[:, aligned(there, narrow)] = firsts[part][:, wide:]

    half = q_s.shape[0] // 2
    total = dot_nt(q_s[...], wq_ref[...])
    total = total + dot_nt(k_s[...], wk_ref[...])
    total_s[...] = total + dot_nt(v_s[...], wv_ref[...])
    for target, which in ((sent_ref, 1 - side), (mine_ref, side)):
        target[...] = total_s[aligned(which, half), :].astype(target.dtype)


def input_terms(at, firsts, seconds, w_query, w_key, w_value, count, wide, narrow):
    blocks = len(firsts)
    width = w_query.shape[0]
    step = next(s for s in (768, 512, 256, 128, width) if width % s == 0)

    def own(x):
        return pl.BlockSpec((count, x.shape[1]), lambda i, at: (at[0], 0))

    def weight(x):
        return pl.BlockSpec((step, x.shape[1]), lambda i, at: (i, 0))

    out = pl.BlockSpec((count // 2, step), lambda i, at: (0, i))
    ins = firsts + seconds
    half = jnp.bfloat16
    return pl.pallas_call(
        functools.partial(input_terms_kernel, blocks, wide, narrow),
        out_shape=(
            jax.ShapeDtypeStruct((count // 2, width), jnp.float32),
            jax.ShapeDtypeStruct((count // 2, width), half),
        ),
        grid_spec=pltpu.PrefetchScalarGridSpec(
            num_scalar_prefetch=1,
            grid=(width // step,),
            in_specs=[own(x) for x in ins] + [weight(x) for x in (w_query, w_key, w_value)],
            out_specs=(out, out),
            scratch_shapes=[
                pltpu.VMEM((count, blocks * wide), half),
                pltpu.VMEM((count, blocks * narrow), half),
                pltpu.VMEM((count, blocks * narrow), half),
                pltpu.VMEM((count, step), jnp.float32),
            ],
        ),
        compiler_params=params(VMEM_MOST),
        cost_estimate=pl.CostEstimate(
            flops=COST * count * width * blocks * (wide + 2 * narrow),
            bytes_accessed=2 * width * blocks * (wide + 2 * narrow) + 3 * width * count,
            transcendentals=0,
        ),
        name="input_terms",
    )(at, *ins, w_query, w_key, w_value)


def swap(x, axis, by):
    count = lax.axis_size(axis)
    return lax.ppermute(x, axis, [(i, i ^ by) for i in range(count)])


def rotation_tables(places):
    half = HD // 2
    index = jnp.arange(half, dtype=jnp.float32)
    freq = jnp.power(jnp.float32(10000.0), index * (-2.0 / HD))
    angle = places.astype(jnp.float32)[:, None] * freq[None, :]
    cosine = jnp.cos(angle)
    sine = jnp.sin(angle)
    return jnp.concatenate([cosine, cosine], axis=1), jnp.concatenate([sine, -sine], axis=1)


def on_device(
    inputs,
    queries,
    key_states,
    value_states,
    out_grad,
    positions,
    w_query,
    w_key,
    w_value,
    w_output,
):
    count = queries.shape[0]
    head_cols = queries.shape[1]
    kv_cols = key_states.shape[1]
    kv_here = kv_cols // HD
    group = head_cols // kv_cols
    blocks = lax.axis_size("context")
    replicas = lax.axis_size("dp")
    cores = lax.axis_size("tensor")
    width = inputs.shape[1]
    heads = kv_here // blocks
    wide = heads * group * HD
    narrow = heads * HD
    fits = (
        blocks == 4
        and kv_here % blocks == 0
        and cores == 2
        and count % (2 * HD) == 0
        and count % TILE == 0
        and W % TILE == 0
        and width % HD == 0
        and width % (replicas * blocks * EXTRA) == 0
        and wide + 2 * narrow >= count
    )
    if not fits:
        return banded(
            inputs, queries, key_states, value_states, out_grad, positions,
            w_query, w_key, w_value, w_output,
        )
    me = lax.axis_index("context")
    side = lax.axis_index("tensor")
    at = jnp.stack([me, side]).astype(jnp.int32)

    barrier = lax.optimization_barrier

    digits = jnp.stack([positions // RADIX, positions % RADIX]).astype(jnp.bfloat16)
    extra = jnp.pad(digits, ((0, EXTRA - 2), (0, wide + 2 * narrow - count)))
    packs = list(
        pack_heads(at, queries, key_states, value_states, extra, blocks, wide, narrow)
    )
    after, packs = barrier((out_grad, packs))
    for part in range(1, blocks):
        packs[part] = swap(packs[part], "context", part)
    dattn = jnp.dot(after, w_output, preferred_element_type=jnp.float32).astype(jnp.bfloat16)
    dpacks = [
        lax.dynamic_slice(dattn, (0, (me ^ part) * wide), (count, wide)) for part in range(blocks)
    ]
    def spread(packed):
        return [swap(x, "context", part + 1) for part, x in enumerate(packed)]

    def joined(own, came):
        pieces = [own]
        for x in came:
            pieces += [x, swap(x, "tensor", 1)]
        return pieces

    soon, dpacks = barrier((at, dpacks))
    packs, dpacks = barrier((packs, dpacks))
    grad_own, *grad_packed = pack_rows(soon, out_grad, blocks, replicas)
    dpacks = [dpacks[0]] + spread(dpacks[1:])
    places = [
        (pack[count, :count].astype(jnp.float32) * RADIX + pack[count + 1, :count].astype(jnp.float32)).astype(jnp.int32)
        for pack in packs[1:]
    ]
    places = jnp.concatenate([positions] + places)
    index = jnp.concatenate(
        [(me ^ part) * count + jnp.arange(count, dtype=jnp.int32) for part in range(blocks)]
    )
    low = jnp.maximum(index - places, index - (W - 1))[None, :]
    cosine, sine = rotation_tables(places)
    soon, grad_packed, packs = barrier((soon, grad_packed, packs))
    input_own, *input_packed = pack_rows(soon, inputs, blocks, replicas)
    dpacks, grad_packed, input_packed = barrier((dpacks, grad_packed, input_packed))

    grad_came = spread(grad_packed)
    first, second = attention(at, packs, dpacks, low, cosine, sine, heads, group)
    first, second, grad_came, input_packed = barrier((first, second, grad_came, input_packed))

    input_came = spread(input_packed)
    grads = joined(grad_own, grad_came)
    edge = wide + narrow
    def summed(term):
        return lax.psum_scatter(term, "dp", scatter_dimension=0, tiled=True)

    parts = []
    term = weight_terms(at, [grads], [first], [(0, 0, 0, wide)], blocks, replicas, LOAD1)
    parts.append(summed(term))
    term, input_came, first, second = barrier((term, input_came, first, second))

    firsts = [first, swap(first, "context", 1), None, None]
    seconds = [second, None, swap(second, "context", 2), None]
    ins = joined(input_own, input_came)
    ins, parts[0] = barrier((ins, parts[0]))
    jobs = [(0, 0, wide, edge), (0, 1, 0, edge)]
    term = weight_terms(at, [ins], [first, second], jobs, blocks, replicas, LOAD2)
    parts.append(summed(term))
    term, firsts[1], seconds[2], first, second = barrier(
        (term, firsts[1], seconds[2], first, second)
    )
    seconds[1] = swap(second, "context", 1)
    firsts[2] = swap(first, "context", 2)
    jobs = [(0, 0, 0, wide), (1, 0, wide, edge), (1, 1, 0, edge)]

    def terms_of(source_first, source_second):
        lins = [firsts[source_first], seconds[source_second]]
        return weight_terms(at, [grads, ins], lins, jobs, blocks, replicas)

    term = terms_of(1, 2)
    parts.append(summed(term))
    term, firsts[1], firsts[2], seconds[1], seconds[2] = barrier(
        (term, firsts[1], firsts[2], seconds[1], seconds[2])
    )
    firsts[3] = swap(firsts[1], "context", 2)
    seconds[3] = swap(seconds[2], "context", 1)
    term = terms_of(2, 1)
    parts.append(summed(term))
    term, parts[1], firsts[3], seconds[3] = barrier((term, parts[1], firsts[3], seconds[3]))
    late, term = barrier((at, term))
    mine, sent = input_terms(
        late, firsts, seconds, w_query, w_key, w_value, count, wide, narrow
    )
    came = swap(sent, "tensor", 1)
    mine, firsts[3] = barrier((mine, firsts[3]))
    term = terms_of(3, 3)
    parts.append(summed(term))
    mine, came, parts[2], parts[3] = barrier((mine, came, parts[2], parts[3]))
    input_grad = (mine + came.astype(jnp.float32)).astype(jnp.bfloat16)
    last, input_grad = barrier((at, input_grad))

    def rest(source_first, source_second):
        return [(1, source_first, narrow), (2, source_second, wide), (3, source_second, narrow)]

    layout = [[(0, 0, wide)], rest(0, 0)]
    for source_first, source_second in ((1, 2), (2, 1), (3, 3)):
        layout.append([(0, source_first, wide)] + rest(source_first, source_second))
    grad_output, grad_value, grad_query, grad_key = assemble(
        last, layout, parts, blocks, wide, narrow
    )
    return (input_grad, grad_query, grad_key, grad_value, grad_output)


def solution(mesh):
    return jax.shard_map(
        on_device,
        mesh=mesh,
        in_specs=(
            P(("dp", "context"), None),
            P(("dp", "context"), "tensor"),
            P(("dp", "context"), "tensor"),
            P(("dp", "context"), "tensor"),
            P(("dp", "context"), None),
            P(("dp", "context")),
            P(None, "tensor"),
            P(None, "tensor"),
            P(None, "tensor"),
            P(None, "tensor"),
        ),
        out_specs=(
            P(("dp", "context", "tensor"), None),
            P(("dp", "context"), "tensor"),
            P(("dp", "context"), "tensor"),
            P(("dp", "context"), "tensor"),
            P(("dp", "context"), "tensor"),
        ),
        check_vma=False,
    )
```

```python
import functools

import jax
import jax.numpy as jnp
from jax import lax
from jax.experimental import pallas as pl
from jax.experimental.pallas import tpu as pltpu
from jax.sharding import PartitionSpec as P

HD = 128
W = 1024
QSCALAR = 168


def shifted(x, axis, by):
    count = lax.axis_size(axis)
    pairs = [(i, i + by) for i in range(count) if 0 <= i + by < count]
    return lax.ppermute(x, axis, pairs)


def rotate_back(grads, places):
    count = grads.shape[0]
    half = HD // 2
    index = jnp.arange(half, dtype=jnp.float32)
    freq = jnp.power(jnp.float32(10000.0), index * (-2.0 / HD))
    angle = places.astype(jnp.float32)[:, None] * freq[None, :]
    cosine = jnp.cos(angle)[:, None, :]
    sine = jnp.sin(angle)[:, None, :]
    split = grads.reshape(count, -1, 2, half)
    first = split[:, :, 0, :]
    second = split[:, :, 1, :]
    upper = first * cosine + second * sine
    lower = second * cosine - first * sine
    return jnp.stack([upper, lower], axis=2).reshape(count, -1)


def contract_rows(left, right):
    return lax.dot_general(
        left, right, (((0,), (0,)), ((), ())), preferred_element_type=jnp.float32
    )


def contract_cols(left, right):
    return lax.dot_general(
        left, right, (((1,), (1,)), ((), ())), preferred_element_type=jnp.float32
    )


def banded(
    inputs,
    queries,
    key_states,
    value_states,
    out_grad,
    positions,
    w_query,
    w_key,
    w_value,
    w_output,
):
    count = queries.shape[0]
    head_cols = queries.shape[1]
    kv_cols = key_states.shape[1]
    kv_here = kv_cols // HD
    group = head_cols // kv_cols
    scale = QSCALAR ** (-0.5)
    block = lax.axis_index("context")
    blocks = lax.axis_size("context")
    reach = min((W + count - 2) // count, blocks - 1)
    span = (reach + 1) * count
    key_pieces = []
    value_pieces = []
    for back in range(reach, 0, -1):
        earlier_keys, earlier_values = shifted((key_states, value_states), "context", back)
        key_pieces.append(earlier_keys)
        value_pieces.append(earlier_values)
    band_keys = jnp.concatenate(key_pieces + [key_states], axis=0)
    band_values = jnp.concatenate(value_pieces + [value_states], axis=0)
    query_index = block * count + jnp.arange(count, dtype=jnp.int32)
    key_index = (block - reach) * count + jnp.arange(span, dtype=jnp.int32)
    doc_start = query_index - positions
    allowed = (key_index[None, :] <= query_index[:, None]) & (
        query_index[:, None] - key_index[None, :] < W
    )
    allowed = allowed & (key_index[None, :] >= doc_start[:, None]) & (key_index[None, :] >= 0)
    query_heads = queries.reshape(count, kv_here, group, HD)
    key_heads = band_keys.reshape(span, kv_here, HD)
    value_heads = band_values.reshape(span, kv_here, HD)
    scores = (
        jnp.einsum("qhgd,khd->hgqk", query_heads, key_heads, preferred_element_type=jnp.float32)
        * scale
    )
    scores = jnp.where(allowed, scores, -1e30)
    top = jnp.max(scores, axis=-1, keepdims=True)
    weights = jnp.exp(scores - top)
    probs = weights / jnp.sum(weights, axis=-1, keepdims=True)
    probs_half = probs.astype(jnp.bfloat16)
    attn = jnp.einsum(
        "hgqk,khd->qhgd", probs_half, value_heads, preferred_element_type=jnp.float32
    ).astype(jnp.bfloat16)
    attn_flat = attn.reshape(count, head_cols)
    dattn = jnp.dot(out_grad, w_output, preferred_element_type=jnp.float32).astype(jnp.bfloat16)
    dattn_heads = dattn.reshape(count, kv_here, group, HD)
    dprobs = jnp.einsum(
        "qhgd,khd->hgqk", dattn_heads, value_heads, preferred_element_type=jnp.float32
    )
    delta = jnp.sum(dattn_heads.astype(jnp.float32) * attn.astype(jnp.float32), axis=-1)
    delta = jnp.transpose(delta, (1, 2, 0))[..., None]
    dscores = (probs * (dprobs - delta) * scale).astype(jnp.bfloat16)
    query_grad = jnp.einsum(
        "hgqk,khd->qhgd", dscores, key_heads, preferred_element_type=jnp.float32
    ).reshape(count, head_cols)
    band_key_grad = jnp.einsum(
        "hgqk,qhgd->khd", dscores, query_heads, preferred_element_type=jnp.float32
    ).reshape(span, kv_cols)
    band_value_grad = jnp.einsum(
        "hgqk,qhgd->khd", probs_half, dattn_heads, preferred_element_type=jnp.float32
    ).reshape(span, kv_cols)
    key_grad = band_key_grad[reach * count :]
    value_grad = band_value_grad[reach * count :]
    for back in range(1, reach + 1):
        first_row = (reach - back) * count
        sent_keys, sent_values = shifted(
            (
                band_key_grad[first_row : first_row + count],
                band_value_grad[first_row : first_row + count],
            ),
            "context",
            -back,
        )
        key_grad = key_grad + sent_keys
        value_grad = value_grad + sent_values
    query_lin = rotate_back(query_grad, positions).astype(jnp.bfloat16)
    key_lin = rotate_back(key_grad, positions).astype(jnp.bfloat16)
    value_half = value_grad.astype(jnp.bfloat16)
    total = contract_cols(query_lin, w_query)
    total = total + contract_cols(key_lin, w_key)
    total = total + contract_cols(value_half, w_value)
    input_grad = lax.psum_scatter(total, "tensor", scatter_dimension=0, tiled=True).astype(
        jnp.bfloat16
    )
    terms = (
        contract_rows(inputs, query_lin),
        contract_rows(inputs, key_lin),
        contract_rows(inputs, value_half),
        contract_rows(out_grad, attn_flat),
    )
    summed = (
        lax.psum_scatter(
            terms[0].astype(jnp.bfloat16), ("dp", "context"), scatter_dimension=0, tiled=True
        ).astype(jnp.float32),
        lax.psum_scatter(
            terms[1].astype(jnp.bfloat16), ("dp", "context"), scatter_dimension=0, tiled=True
        ).astype(jnp.float32),
        lax.psum_scatter(
            terms[2].astype(jnp.bfloat16), ("dp", "context"), scatter_dimension=0, tiled=True
        ).astype(jnp.float32),
        lax.psum_scatter(
            terms[3].astype(jnp.bfloat16), ("dp", "context"), scatter_dimension=0, tiled=True
        ).astype(jnp.float32),
    )
    return (input_grad, summed[0], summed[1], summed[2], summed[3])


TILE = 256
EXTRA = 16
RADIX = 128
NEGATIVE = -1e30
LOG2E = 1.4426950408889634
VMEM_LIMIT = 48 * 1024 * 1024
LOAD = 40
LOAD1 = 12
LOAD2 = 12
COST = 80
VMEM_MOST = 60 * 1024 * 1024


def dot_nt(left, right):
    return lax.dot_general(
        left, right, (((1,), (1,)), ((), ())), preferred_element_type=jnp.float32
    )


def dot_nn(left, right):
    return lax.dot_general(
        left, right, (((1,), (0,)), ((), ())), preferred_element_type=jnp.float32
    )


def whole():
    return pl.BlockSpec(memory_space=pltpu.VMEM)


def scalars():
    return pl.BlockSpec(memory_space=pltpu.SMEM)


def params(limit=VMEM_LIMIT):
    return pltpu.CompilerParams(vmem_limit_bytes=limit)


def aligned(index, size):
    return pl.ds(pl.multiple_of(index * size, size), size)


def pack_heads_kernel(blocks, wide, narrow, at_ref, q_ref, k_ref, v_ref, extra_ref, *outs):
    me = at_ref[0]
    count = q_ref.shape[0]
    for part in range(blocks):
        there = me ^ part
        out = outs[part]
        out[:count, :wide] = q_ref[:, aligned(there, wide)]
        out[:count, wide : wide + narrow] = k_ref[:, aligned(there, narrow)]
        out[:count, wide + narrow :] = v_ref[:, aligned(there, narrow)]
        out[count:, :] = extra_ref[...]


def pack_heads(at, queries, key_states, value_states, extra, blocks, wide, narrow):
    count = queries.shape[0]
    shape = jax.ShapeDtypeStruct((count + EXTRA, wide + 2 * narrow), queries.dtype)
    return pl.pallas_call(
        functools.partial(pack_heads_kernel, blocks, wide, narrow),
        out_shape=(shape,) * blocks,
        in_specs=[scalars()] + [whole()] * 4,
        out_specs=(whole(),) * blocks,
        compiler_params=params(),
        cost_estimate=pl.CostEstimate(
            flops=0, bytes_accessed=4 * blocks * count * (wide + 2 * narrow), transcendentals=0
        ),
        name="pack_heads",
    )(at, queries, key_states, value_states, extra)


def pack_rows_kernel(blocks, replicas, rows, at_ref, x_ref, own_ref, *rest):
    outs, turned = rest[:-1], rest[-1]
    me, side = at_ref[0], at_ref[1]
    count, width = x_ref.shape
    half = count // 2

    def turn(index, carry):
        cols = aligned(index, HD)
        turned[cols, :] = x_ref[:, cols].T
        return carry

    lax.fori_loop(0, width // HD, turn, 0)
    for replica in range(replicas):
        into = pl.ds(replica * rows, rows)
        own_ref[into, :] = turned[aligned(replica * blocks + me, rows), :]
        for part in range(1, blocks):
            taken = aligned(replica * blocks + (me ^ part), rows)
            outs[part - 1][into, :] = turned[taken, aligned(side, half)]


def pack_rows(at, x, blocks, replicas):
    count, width = x.shape
    rows = width // (replicas * blocks)
    share = replicas * rows
    own = jax.ShapeDtypeStruct((share, count), x.dtype)
    sent = jax.ShapeDtypeStruct((share, count // 2), x.dtype)
    return pl.pallas_call(
        functools.partial(pack_rows_kernel, blocks, replicas, rows),
        out_shape=(own,) + (sent,) * (blocks - 1),
        in_specs=[scalars(), whole()],
        out_specs=(whole(),) * blocks,
        scratch_shapes=[pltpu.VMEM((width, count), x.dtype)],
        compiler_params=params(),
        cost_estimate=pl.CostEstimate(
            flops=0, bytes_accessed=6 * count * width, transcendentals=0
        ),
        name="pack_rows",
    )(at, x)


def attention_kernel(blocks, count, heads, group, *refs):
    at_ref = refs[0]
    packs = refs[1 : 1 + blocks]
    dpacks = refs[1 + blocks : 1 + 2 * blocks]
    low_ref, cos_ref, sin_ref = refs[1 + 2 * blocks : 4 + 2 * blocks]
    first_ref, second_ref = refs[4 + 2 * blocks : 6 + 2 * blocks]
    q_s, k_s, v_s, kt_s, vt_s, d_s, dt_s, dk_s, dv_s = refs[6 + 2 * blocks :]
    scale = QSCALAR ** (-0.5)
    factor = scale * LOG2E
    span = blocks * count
    wide = heads * group * HD
    narrow = heads * HD
    per_block = count // TILE
    reach = -(-(W - 1) // TILE)
    me = at_ref[0]
    for part in range(blocks):
        rows = aligned(me ^ part, count)
        pack = packs[part]
        q_s[rows, :] = pack[:count, :wide]
        keys = pack[:count, wide : wide + narrow]
        values = pack[:count, wide + narrow :]
        k_s[rows, :] = keys
        v_s[rows, :] = values
        kt_s[:, rows] = keys.T
        vt_s[:, rows] = values.T
        d_s[rows, :] = dpacks[part][...]
        dt_s[:, rows] = dpacks[part][...].T
    dk_s[...] = jnp.zeros_like(dk_s)
    dv_s[...] = jnp.zeros_like(dv_s)

    def stored(index):
        return aligned(((index // per_block) ^ me) * per_block + lax.rem(index, per_block), TILE)

    def rotated(grad, rows):
        return grad * cos_ref[rows, :] + pltpu.roll(grad, HD // 2, 1) * sin_ref[rows, :]

    for head in range(heads):
        kv = slice(head * HD, (head + 1) * HD)

        def tile(index, first_key, width):
            index = jnp.int32(index)
            q_rows = aligned(index, TILE)
            t_rows = stored(index)
            k_rows = pl.ds(first_key, width)
            columns = [slice(head * group * HD + g * HD, head * group * HD + (g + 1) * HD) for g in range(group)]
            query = jnp.concatenate([q_s[q_rows, c] for c in columns], axis=0)
            dattn = jnp.concatenate([d_s[q_rows, c] for c in columns], axis=0)
            dattn_t = jnp.concatenate([dt_s[c, q_rows] for c in columns], axis=1)
            scores = dot_nt(k_s[k_rows, kv], query)
            low = jnp.concatenate([low_ref[:, t_rows]] * group, axis=1)
            at = first_key + lax.broadcasted_iota(jnp.int32, (width, group * TILE), 0)
            own = index * TILE + lax.rem(
                lax.broadcasted_iota(jnp.int32, (1, group * TILE), 1), jnp.int32(TILE)
            )
            scores = jnp.where((at >= low) & (at <= own), scores, NEGATIVE)
            top = jnp.max(scores, axis=0, keepdims=True)
            weights = jnp.exp2(scores * factor - top * factor)
            inverse = 1.0 / jnp.sum(weights, axis=0, keepdims=True)
            probs = weights * inverse
            half = probs.astype(jnp.bfloat16)
            attn = dot_nn(vt_s[kv, k_rows], half).astype(jnp.bfloat16)
            dprobs = dot_nt(v_s[k_rows, kv], dattn)
            attn_wide = attn.astype(jnp.float32)
            delta = jnp.sum(dattn_t.astype(jnp.float32) * attn_wide, axis=0, keepdims=True)
            dscores = (probs * (dprobs - delta)).astype(jnp.bfloat16)
            query_grad = (dot_nn(kt_s[kv, k_rows], dscores) * scale).T
            attn_rows = attn_wide.T
            dk_s[k_rows, kv] += dot_nn(dscores, query)
            dv_s[k_rows, kv] += dot_nn(half, dattn)
            for g, c in enumerate(columns):
                part = slice(g * TILE, (g + 1) * TILE)
                first_ref[q_rows, c] = attn_rows[part].astype(jnp.bfloat16)
                second_ref[q_rows, c] = rotated(query_grad[part], t_rows).astype(jnp.bfloat16)

        tiles = span // TILE
        for index in range(min(reach, tiles)):
            tile(index, 0, (index + 1) * TILE)

        def steady(index, carry):
            tile(index, pl.multiple_of((index - reach) * TILE, TILE), (reach + 1) * TILE)
            return carry

        if tiles > reach:
            lax.fori_loop(reach, tiles, steady, 0)
        out = slice(wide + head * HD, wide + (head + 1) * HD)
        for index in range(tiles):
            rows = pl.ds(index * TILE, TILE)
            first_ref[rows, out] = dv_s[rows, kv].astype(jnp.bfloat16)
            second_ref[rows, out] = rotated(
                dk_s[rows, kv] * scale, stored(jnp.int32(index))
            ).astype(jnp.bfloat16)


def attention(at, packs, dpacks, low, cosine, sine, heads, group):
    blocks = len(packs)
    count = dpacks[0].shape[0]
    span = blocks * count
    wide = heads * group * HD
    narrow = heads * HD
    half = jnp.bfloat16
    pairs = heads * group * span * (W + TILE)
    return pl.pallas_call(
        functools.partial(attention_kernel, blocks, count, heads, group),
        out_shape=(jax.ShapeDtypeStruct((span, wide + narrow), half),) * 2,
        in_specs=[scalars()] + [whole()] * (2 * blocks + 3),
        out_specs=(whole(),) * 2,
        scratch_shapes=[
            pltpu.VMEM((span, wide), half),
            pltpu.VMEM((span, narrow), half),
            pltpu.VMEM((span, narrow), half),
            pltpu.VMEM((narrow, span), half),
            pltpu.VMEM((narrow, span), half),
            pltpu.VMEM((span, wide), half),
            pltpu.VMEM((wide, span), half),
            pltpu.VMEM((span, narrow), jnp.float32),
            pltpu.VMEM((span, narrow), jnp.float32),
        ],
        compiler_params=params(),
        cost_estimate=pl.CostEstimate(
            flops=10 * pairs * HD, bytes_accessed=span * wide * 12, transcendentals=pairs
        ),
        name="attention_backward",
    )(at, *packs, *dpacks, low, cosine, sine)


def weight_terms_kernel(blocks, jobs, at_ref, *refs):
    pieces = 1 + 2 * (blocks - 1)
    sets = 1 + max(job[0] for job in jobs)
    piece_refs = refs[: sets * pieces]
    lin_refs = refs[sets * pieces : -1]
    out_ref = refs[-1]
    me, side = at_ref[0], at_ref[1]
    count = piece_refs[0].shape[1]
    half = count // 2
    rows = [aligned(me, count)]
    for part in range(1, blocks):
        rows.append(aligned((me ^ part) * 2 + side, half))
        rows.append(aligned((me ^ part) * 2 + 1 - side, half))
    total = [None] * len(jobs)
    for piece in range(pieces):
        for index, (which, lin, low, high) in enumerate(jobs):
            left = piece_refs[which * pieces + piece][...]
            term = dot_nn(left, lin_refs[lin][rows[piece], low:high])
            total[index] = term if total[index] is None else total[index] + term
    first = 0
    for index, (which, lin, low, high) in enumerate(jobs):
        out_ref[:, first : first + high - low] = total[index].astype(out_ref.dtype)
        first += high - low


def weight_terms(at, sets, lins, jobs, blocks, replicas, load=LOAD):
    share = sets[0][0].shape[0]
    rows = share // replicas
    span = lins[0].shape[0]
    cols = sum(job[3] - job[2] for job in jobs)
    pieces = [x for one in sets for x in one]

    def piece(x):
        return pl.BlockSpec((rows, x.shape[1]), lambda i, at: (i, 0))

    def fixed(x):
        return pl.BlockSpec(x.shape, lambda i, at: (0, 0))

    return pl.pallas_call(
        functools.partial(weight_terms_kernel, blocks, jobs),
        out_shape=jax.ShapeDtypeStruct((share, cols), lins[0].dtype),
        grid_spec=pltpu.PrefetchScalarGridSpec(
            num_scalar_prefetch=1,
            grid=(replicas,),
            in_specs=[piece(x) for x in pieces] + [fixed(x) for x in lins],
            out_specs=pl.BlockSpec((rows, cols), lambda i, at: (i, 0)),
        ),
        compiler_params=params(VMEM_MOST),
        cost_estimate=pl.CostEstimate(
            flops=load * share * span * cols,
            bytes_accessed=2 * share * span * len(sets) + 2 * (span + share) * cols,
            transcendentals=0,
        ),
        name="weight_terms",
    )(at, *pieces, *lins)


def assemble_kernel(places, at_ref, *refs):
    parts, outs = refs[:-4], refs[-4:]
    me = at_ref[0]
    for part, one in zip(parts, places):
        first = 0
        for out, source, cols in one:
            outs[out][:, aligned(me ^ source, cols)] = part[:, first : first + cols].astype(
                jnp.float32
            )
            first += cols


def assemble(at, places, parts, blocks, wide, narrow):
    rows = parts[0].shape[0]
    shapes = [
        jax.ShapeDtypeStruct((rows, blocks * cols), jnp.float32)
        for cols in (wide, narrow, wide, narrow)
    ]
    return pl.pallas_call(
        functools.partial(assemble_kernel, places),
        out_shape=tuple(shapes),
        in_specs=[scalars()] + [whole()] * len(parts),
        out_specs=(whole(),) * 4,
        compiler_params=params(),
        name="assemble",
    )(at, *parts)


def input_first_kernel(blocks, wide, narrow, at_ref, *refs):
    firsts, seconds = refs[: blocks - 1], refs[blocks - 1 : 2 * (blocks - 1)]
    wq_ref, wk_ref, wv_ref, out_ref, q_s, k_s, v_s = refs[2 * (blocks - 1) :]
    me = at_ref[0]

    @pl.when(pl.program_id(0) == 0)
    def _():
        q_s[...] = jnp.zeros_like(q_s)
        k_s[...] = jnp.zeros_like(k_s)
        v_s[...] = jnp.zeros_like(v_s)
        for part in range(blocks - 1):
            there = me ^ part
            q_s[:, aligned(there, wide)] = seconds[part][:, :wide]
            k_s[:, aligned(there, narrow)] = seconds[part][:, wide:]
            v_s[:, aligned(there, narrow)] = firsts[part][:, wide:]

    total = dot_nt(q_s[...], wq_ref[...])
    total = total + dot_nt(k_s[...], wk_ref[...])
    out_ref[...] = total + dot_nt(v_s[...], wv_ref[...])


def input_last_kernel(wide, at_ref, first_ref, second_ref, wq_ref, wk_ref, wv_ref, part_ref, mine_ref, sent_ref, total_s):
    side = at_ref[1]
    half = first_ref.shape[0] // 2
    total = part_ref[...] + dot_nt(second_ref[:, :wide], wq_ref[...])
    total = total + dot_nt(second_ref[:, wide:], wk_ref[...])
    total_s[...] = total + dot_nt(first_ref[:, wide:], wv_ref[...])
    for target, which in ((sent_ref, 1 - side), (mine_ref, side)):
        target[...] = total_s[aligned(which, half), :].astype(target.dtype)


def columns_step(width):
    return next(s for s in (768, 512, 256, 128, width) if width % s == 0)


def input_first(at, firsts, seconds, w_query, w_key, w_value, count, wide, narrow):
    blocks = len(firsts) + 1
    width = w_query.shape[0]
    step = columns_step(width)
    ins = firsts + seconds
    half = jnp.bfloat16
    return pl.pallas_call(
        functools.partial(input_first_kernel, blocks, wide, narrow),
        out_shape=jax.ShapeDtypeStruct((count, width), jnp.float32),
        grid_spec=pltpu.PrefetchScalarGridSpec(
            num_scalar_prefetch=1,
            grid=(width // step,),
            in_specs=[pl.BlockSpec((count, x.shape[1]), lambda i, at: (at[0], 0)) for x in ins]
            + [
                pl.BlockSpec((step, x.shape[1]), lambda i, at: (i, 0))
                for x in (w_query, w_key, w_value)
            ],
            out_specs=pl.BlockSpec((count, step), lambda i, at: (0, i)),
            scratch_shapes=[
                pltpu.VMEM((count, blocks * wide), half),
                pltpu.VMEM((count, blocks * narrow), half),
                pltpu.VMEM((count, blocks * narrow), half),
            ],
        ),
        compiler_params=params(VMEM_MOST),
        cost_estimate=pl.CostEstimate(
            flops=count * width * blocks * (wide + 2 * narrow), bytes_accessed=0, transcendentals=0
        ),
        name="input_first",
    )(at, *ins, w_query, w_key, w_value)


def input_last(at, far, first, second, partial, w_query, w_key, w_value, wide, narrow):
    count, width = partial.shape
    step = columns_step(width)

    def own(x):
        return pl.BlockSpec((count, x.shape[1]), lambda i, at: (at[0], 0))

    def weight(cols):
        return pl.BlockSpec((step, cols), lambda i, at: (i, at[0] ^ far))

    out = pl.BlockSpec((count // 2, step), lambda i, at: (0, i))
    return pl.pallas_call(
        functools.partial(input_last_kernel, wide),
        out_shape=(
            jax.ShapeDtypeStruct((count // 2, width), jnp.float32),
            jax.ShapeDtypeStruct((count // 2, width), jnp.bfloat16),
        ),
        grid_spec=pltpu.PrefetchScalarGridSpec(
            num_scalar_prefetch=1,
            grid=(width // step,),
            in_specs=[own(first), own(second), weight(wide), weight(narrow), weight(narrow)]
            + [pl.BlockSpec((count, step), lambda i, at: (0, i))],
            out_specs=(out, out),
            scratch_shapes=[pltpu.VMEM((count, step), jnp.float32)],
        ),
        compiler_params=params(VMEM_MOST),
        cost_estimate=pl.CostEstimate(
            flops=COST * count * width * (wide + 2 * narrow), bytes_accessed=0, transcendentals=0
        ),
        name="input_last",
    )(at, first, second, w_query, w_key, w_value, partial)


def swap(x, axis, by):
    count = lax.axis_size(axis)
    return lax.ppermute(x, axis, [(i, i ^ by) for i in range(count)])


def rotation_tables(places):
    half = HD // 2
    index = jnp.arange(half, dtype=jnp.float32)
    freq = jnp.power(jnp.float32(10000.0), index * (-2.0 / HD))
    angle = places.astype(jnp.float32)[:, None] * freq[None, :]
    cosine = jnp.cos(angle)
    sine = jnp.sin(angle)
    return jnp.concatenate([cosine, cosine], axis=1), jnp.concatenate([sine, -sine], axis=1)


def on_device(
    inputs,
    queries,
    key_states,
    value_states,
    out_grad,
    positions,
    w_query,
    w_key,
    w_value,
    w_output,
):
    count = queries.shape[0]
    head_cols = queries.shape[1]
    kv_cols = key_states.shape[1]
    kv_here = kv_cols // HD
    group = head_cols // kv_cols
    blocks = lax.axis_size("context")
    replicas = lax.axis_size("dp")
    cores = lax.axis_size("tensor")
    width = inputs.shape[1]
    heads = kv_here // blocks
    wide = heads * group * HD
    narrow = heads * HD
    fits = (
        blocks == 4
        and kv_here % blocks == 0
        and cores == 2
        and count % (2 * HD) == 0
        and count % TILE == 0
        and W % TILE == 0
        and width % HD == 0
        and width % (replicas * blocks * EXTRA) == 0
        and wide + 2 * narrow >= count
    )
    if not fits:
        return banded(
            inputs, queries, key_states, value_states, out_grad, positions,
            w_query, w_key, w_value, w_output,
        )
    me = lax.axis_index("context")
    side = lax.axis_index("tensor")
    at = jnp.stack([me, side]).astype(jnp.int32)

    barrier = lax.optimization_barrier

    digits = jnp.stack([positions // RADIX, positions % RADIX]).astype(jnp.bfloat16)
    extra = jnp.pad(digits, ((0, EXTRA - 2), (0, wide + 2 * narrow - count)))
    packs = list(
        pack_heads(at, queries, key_states, value_states, extra, blocks, wide, narrow)
    )
    after, packs = barrier((out_grad, packs))
    for part in range(1, blocks):
        packs[part] = swap(packs[part], "context", part)
    dattn = jnp.dot(after, w_output, preferred_element_type=jnp.float32).astype(jnp.bfloat16)
    dpacks = [
        lax.dynamic_slice(dattn, (0, (me ^ part) * wide), (count, wide)) for part in range(blocks)
    ]
    def spread(packed):
        return [swap(x, "context", part + 1) for part, x in enumerate(packed)]

    def joined(own, came):
        pieces = [own]
        for x in came:
            pieces += [x, swap(x, "tensor", 1)]
        return pieces

    soon, dpacks = barrier((at, dpacks))
    packs, dpacks = barrier((packs, dpacks))
    grad_own, *grad_packed = pack_rows(soon, out_grad, blocks, replicas)
    dpacks = [dpacks[0]] + spread(dpacks[1:])
    places = [
        (pack[count, :count].astype(jnp.float32) * RADIX + pack[count + 1, :count].astype(jnp.float32)).astype(jnp.int32)
        for pack in packs[1:]
    ]
    places = jnp.concatenate([positions] + places)
    index = jnp.concatenate(
        [(me ^ part) * count + jnp.arange(count, dtype=jnp.int32) for part in range(blocks)]
    )
    low = jnp.maximum(index - places, index - (W - 1))[None, :]
    cosine, sine = rotation_tables(places)
    soon, grad_packed, packs = barrier((soon, grad_packed, packs))
    input_own, *input_packed = pack_rows(soon, inputs, blocks, replicas)
    dpacks, grad_packed, input_packed = barrier((dpacks, grad_packed, input_packed))

    grad_came = spread(grad_packed)
    first, second = attention(at, packs, dpacks, low, cosine, sine, heads, group)
    first, second, grad_came, input_packed = barrier((first, second, grad_came, input_packed))

    input_came = spread(input_packed)
    grads = joined(grad_own, grad_came)
    edge = wide + narrow
    def summed(term):
        return lax.psum_scatter(term, "dp", scatter_dimension=0, tiled=True)

    parts = []
    term = weight_terms(at, [grads], [first], [(0, 0, 0, wide)], blocks, replicas, LOAD1)
    parts.append(summed(term))
    term, input_came, first, second = barrier((term, input_came, first, second))

    firsts = [first, swap(first, "context", 1), None, None]
    seconds = [second, None, swap(second, "context", 2), None]
    ins = joined(input_own, input_came)
    ins, parts[0] = barrier((ins, parts[0]))
    jobs = [(0, 0, wide, edge), (0, 1, 0, edge)]
    term = weight_terms(at, [ins], [first, second], jobs, blocks, replicas, LOAD2)
    parts.append(summed(term))
    term, firsts[1], seconds[2], first, second = barrier(
        (term, firsts[1], seconds[2], first, second)
    )
    seconds[1] = swap(second, "context", 1)
    firsts[2] = swap(first, "context", 2)
    jobs = [(0, 0, 0, wide), (1, 0, wide, edge), (1, 1, 0, edge)]

    def terms_of(source_first, source_second):
        lins = [firsts[source_first], seconds[source_second]]
        return weight_terms(at, [grads, ins], lins, jobs, blocks, replicas)

    term = terms_of(1, 2)
    parts.append(summed(term))
    term, firsts[1], firsts[2], seconds[1], seconds[2] = barrier(
        (term, firsts[1], firsts[2], seconds[1], seconds[2])
    )
    firsts[3] = swap(firsts[1], "context", 2)
    seconds[3] = swap(seconds[2], "context", 1)
    term = terms_of(2, 1)
    parts.append(summed(term))
    late, term = barrier((at, term))
    partial = input_first(
        late, firsts[:3], seconds[:3], w_query, w_key, w_value, count, wide, narrow
    )
    term, partial, parts[1], firsts[3], seconds[3] = barrier(
        (term, partial, parts[1], firsts[3], seconds[3])
    )
    mine, sent = input_last(
        at, 3, firsts[3], seconds[3], partial, w_query, w_key, w_value, wide, narrow
    )
    came = swap(sent, "tensor", 1)
    mine, firsts[3] = barrier((mine, firsts[3]))
    term = terms_of(3, 3)
    parts.append(summed(term))
    mine, came, parts[2], parts[3] = barrier((mine, came, parts[2], parts[3]))
    input_grad = (mine + came.astype(jnp.float32)).astype(jnp.bfloat16)
    last, input_grad = barrier((at, input_grad))

    def rest(source_first, source_second):
        return [(1, source_first, narrow), (2, source_second, wide), (3, source_second, narrow)]

    layout = [[(0, 0, wide)], rest(0, 0)]
    for source_first, source_second in ((1, 2), (2, 1), (3, 3)):
        layout.append([(0, source_first, wide)] + rest(source_first, source_second))
    grad_output, grad_value, grad_query, grad_key = assemble(
        last, layout, parts, blocks, wide, narrow
    )
    return (input_grad, grad_query, grad_key, grad_value, grad_output)


def solution(mesh):
    return jax.shard_map(
        on_device,
        mesh=mesh,
        in_specs=(
            P(("dp", "context"), None),
            P(("dp", "context"), "tensor"),
            P(("dp", "context"), "tensor"),
            P(("dp", "context"), "tensor"),
            P(("dp", "context"), None),
            P(("dp", "context")),
            P(None, "tensor"),
            P(None, "tensor"),
            P(None, "tensor"),
            P(None, "tensor"),
        ),
        out_specs=(
            P(("dp", "context", "tensor"), None),
            P(("dp", "context"), "tensor"),
            P(("dp", "context"), "tensor"),
            P(("dp", "context"), "tensor"),
            P(("dp", "context"), "tensor"),
        ),
        check_vma=False,
    )
```

```python
import functools

import jax
import jax.numpy as jnp
from jax import lax
from jax.experimental import pallas as pl
from jax.experimental.pallas import tpu as pltpu
from jax.sharding import PartitionSpec as P

HD = 128
W = 1024
QSCALAR = 168


def shifted(x, axis, by):
    count = lax.axis_size(axis)
    pairs = [(i, i + by) for i in range(count) if 0 <= i + by < count]
    return lax.ppermute(x, axis, pairs)


def rotate_back(grads, places):
    count = grads.shape[0]
    half = HD // 2
    index = jnp.arange(half, dtype=jnp.float32)
    freq = jnp.power(jnp.float32(10000.0), index * (-2.0 / HD))
    angle = places.astype(jnp.float32)[:, None] * freq[None, :]
    cosine = jnp.cos(angle)[:, None, :]
    sine = jnp.sin(angle)[:, None, :]
    split = grads.reshape(count, -1, 2, half)
    first = split[:, :, 0, :]
    second = split[:, :, 1, :]
    upper = first * cosine + second * sine
    lower = second * cosine - first * sine
    return jnp.stack([upper, lower], axis=2).reshape(count, -1)


def contract_rows(left, right):
    return lax.dot_general(
        left, right, (((0,), (0,)), ((), ())), preferred_element_type=jnp.float32
    )


def contract_cols(left, right):
    return lax.dot_general(
        left, right, (((1,), (1,)), ((), ())), preferred_element_type=jnp.float32
    )


def banded(
    inputs,
    queries,
    key_states,
    value_states,
    out_grad,
    positions,
    w_query,
    w_key,
    w_value,
    w_output,
):
    count = queries.shape[0]
    head_cols = queries.shape[1]
    kv_cols = key_states.shape[1]
    kv_here = kv_cols // HD
    group = head_cols // kv_cols
    scale = QSCALAR ** (-0.5)
    block = lax.axis_index("context")
    blocks = lax.axis_size("context")
    reach = min((W + count - 2) // count, blocks - 1)
    span = (reach + 1) * count
    key_pieces = []
    value_pieces = []
    for back in range(reach, 0, -1):
        earlier_keys, earlier_values = shifted((key_states, value_states), "context", back)
        key_pieces.append(earlier_keys)
        value_pieces.append(earlier_values)
    band_keys = jnp.concatenate(key_pieces + [key_states], axis=0)
    band_values = jnp.concatenate(value_pieces + [value_states], axis=0)
    query_index = block * count + jnp.arange(count, dtype=jnp.int32)
    key_index = (block - reach) * count + jnp.arange(span, dtype=jnp.int32)
    doc_start = query_index - positions
    allowed = (key_index[None, :] <= query_index[:, None]) & (
        query_index[:, None] - key_index[None, :] < W
    )
    allowed = allowed & (key_index[None, :] >= doc_start[:, None]) & (key_index[None, :] >= 0)
    query_heads = queries.reshape(count, kv_here, group, HD)
    key_heads = band_keys.reshape(span, kv_here, HD)
    value_heads = band_values.reshape(span, kv_here, HD)
    scores = (
        jnp.einsum("qhgd,khd->hgqk", query_heads, key_heads, preferred_element_type=jnp.float32)
        * scale
    )
    scores = jnp.where(allowed, scores, -1e30)
    top = jnp.max(scores, axis=-1, keepdims=True)
    weights = jnp.exp(scores - top)
    probs = weights / jnp.sum(weights, axis=-1, keepdims=True)
    probs_half = probs.astype(jnp.bfloat16)
    attn = jnp.einsum(
        "hgqk,khd->qhgd", probs_half, value_heads, preferred_element_type=jnp.float32
    ).astype(jnp.bfloat16)
    attn_flat = attn.reshape(count, head_cols)
    dattn = jnp.dot(out_grad, w_output, preferred_element_type=jnp.float32).astype(jnp.bfloat16)
    dattn_heads = dattn.reshape(count, kv_here, group, HD)
    dprobs = jnp.einsum(
        "qhgd,khd->hgqk", dattn_heads, value_heads, preferred_element_type=jnp.float32
    )
    delta = jnp.sum(dattn_heads.astype(jnp.float32) * attn.astype(jnp.float32), axis=-1)
    delta = jnp.transpose(delta, (1, 2, 0))[..., None]
    dscores = (probs * (dprobs - delta) * scale).astype(jnp.bfloat16)
    query_grad = jnp.einsum(
        "hgqk,khd->qhgd", dscores, key_heads, preferred_element_type=jnp.float32
    ).reshape(count, head_cols)
    band_key_grad = jnp.einsum(
        "hgqk,qhgd->khd", dscores, query_heads, preferred_element_type=jnp.float32
    ).reshape(span, kv_cols)
    band_value_grad = jnp.einsum(
        "hgqk,qhgd->khd", probs_half, dattn_heads, preferred_element_type=jnp.float32
    ).reshape(span, kv_cols)
    key_grad = band_key_grad[reach * count :]
    value_grad = band_value_grad[reach * count :]
    for back in range(1, reach + 1):
        first_row = (reach - back) * count
        sent_keys, sent_values = shifted(
            (
                band_key_grad[first_row : first_row + count],
                band_value_grad[first_row : first_row + count],
            ),
            "context",
            -back,
        )
        key_grad = key_grad + sent_keys
        value_grad = value_grad + sent_values
    query_lin = rotate_back(query_grad, positions).astype(jnp.bfloat16)
    key_lin = rotate_back(key_grad, positions).astype(jnp.bfloat16)
    value_half = value_grad.astype(jnp.bfloat16)
    total = contract_cols(query_lin, w_query)
    total = total + contract_cols(key_lin, w_key)
    total = total + contract_cols(value_half, w_value)
    input_grad = lax.psum_scatter(total, "tensor", scatter_dimension=0, tiled=True).astype(
        jnp.bfloat16
    )
    terms = (
        contract_rows(inputs, query_lin),
        contract_rows(inputs, key_lin),
        contract_rows(inputs, value_half),
        contract_rows(out_grad, attn_flat),
    )
    summed = (
        lax.psum_scatter(
            terms[0].astype(jnp.bfloat16), ("dp", "context"), scatter_dimension=0, tiled=True
        ).astype(jnp.float32),
        lax.psum_scatter(
            terms[1].astype(jnp.bfloat16), ("dp", "context"), scatter_dimension=0, tiled=True
        ).astype(jnp.float32),
        lax.psum_scatter(
            terms[2].astype(jnp.bfloat16), ("dp", "context"), scatter_dimension=0, tiled=True
        ).astype(jnp.float32),
        lax.psum_scatter(
            terms[3].astype(jnp.bfloat16), ("dp", "context"), scatter_dimension=0, tiled=True
        ).astype(jnp.float32),
    )
    return (input_grad, summed[0], summed[1], summed[2], summed[3])


TILE = 256
EXTRA = 16
RADIX = 128
NEGATIVE = -1e30
LOG2E = 1.4426950408889634
VMEM_LIMIT = 48 * 1024 * 1024
LOAD = 40
LOAD1 = 12
LOAD2 = 12
COST = 80
VMEM_MOST = 60 * 1024 * 1024
STEPS = 2


def dot_nt(left, right):
    return lax.dot_general(
        left, right, (((1,), (1,)), ((), ())), preferred_element_type=jnp.float32
    )


def dot_nn(left, right):
    return lax.dot_general(
        left, right, (((1,), (0,)), ((), ())), preferred_element_type=jnp.float32
    )


def whole():
    return pl.BlockSpec(memory_space=pltpu.VMEM)


def scalars():
    return pl.BlockSpec(memory_space=pltpu.SMEM)


def params(limit=VMEM_LIMIT):
    return pltpu.CompilerParams(vmem_limit_bytes=limit)


def aligned(index, size):
    return pl.ds(pl.multiple_of(index * size, size), size)


def pack_heads_kernel(blocks, wide, narrow, at_ref, q_ref, k_ref, v_ref, extra_ref, *outs):
    me = at_ref[0]
    count = q_ref.shape[0]
    for part in range(blocks):
        there = me ^ part
        out = outs[part]
        out[:count, :wide] = q_ref[:, aligned(there, wide)]
        out[:count, wide : wide + narrow] = k_ref[:, aligned(there, narrow)]
        out[:count, wide + narrow :] = v_ref[:, aligned(there, narrow)]
        out[count:, :] = extra_ref[...]


def pack_heads(at, queries, key_states, value_states, extra, blocks, wide, narrow):
    count = queries.shape[0]
    shape = jax.ShapeDtypeStruct((count + EXTRA, wide + 2 * narrow), queries.dtype)
    return pl.pallas_call(
        functools.partial(pack_heads_kernel, blocks, wide, narrow),
        out_shape=(shape,) * blocks,
        in_specs=[scalars()] + [pl.BlockSpec(x.shape, lambda: (0, 0)) for x in (queries, key_states, value_states, extra)],
        out_specs=(whole(),) * blocks,
        compiler_params=params(VMEM_MOST),
        cost_estimate=pl.CostEstimate(
            flops=0, bytes_accessed=4 * blocks * count * (wide + 2 * narrow), transcendentals=0
        ),
        name="pack_heads",
    )(at, queries, key_states, value_states, extra)


def pack_rows_kernel(blocks, replicas, rows, at_ref, x_ref, own_ref, *rest):
    outs, turned = rest[:-1], rest[-1]
    me, side = at_ref[0], at_ref[1]
    count, width = x_ref.shape
    half = count // 2

    def turn(index, carry):
        cols = aligned(index, HD)
        turned[cols, :] = x_ref[:, cols].T
        return carry

    lax.fori_loop(0, width // HD, turn, 0)
    for replica in range(replicas):
        into = pl.ds(replica * rows, rows)
        own_ref[into, :] = turned[aligned(replica * blocks + me, rows), :]
        for part in range(1, blocks):
            taken = aligned(replica * blocks + (me ^ part), rows)
            outs[part - 1][into, :] = turned[taken, aligned(side, half)]


def pack_rows(at, x, blocks, replicas):
    count, width = x.shape
    rows = width // (replicas * blocks)
    share = replicas * rows
    own = jax.ShapeDtypeStruct((share, count), x.dtype)
    sent = jax.ShapeDtypeStruct((share, count // 2), x.dtype)
    return pl.pallas_call(
        functools.partial(pack_rows_kernel, blocks, replicas, rows),
        out_shape=(own,) + (sent,) * (blocks - 1),
        in_specs=[scalars(), whole()],
        out_specs=(whole(),) * blocks,
        scratch_shapes=[pltpu.VMEM((width, count), x.dtype)],
        compiler_params=params(),
        cost_estimate=pl.CostEstimate(
            flops=0, bytes_accessed=6 * count * width, transcendentals=0
        ),
        name="pack_rows",
    )(at, x)


def attention_kernel(blocks, count, heads, group, *refs):
    at_ref = refs[0]
    packs = refs[1 : 1 + blocks]
    dpacks = refs[1 + blocks : 1 + 2 * blocks]
    low_ref, cos_ref, sin_ref = refs[1 + 2 * blocks : 4 + 2 * blocks]
    first_ref, second_ref = refs[4 + 2 * blocks : 6 + 2 * blocks]
    q_s, k_s, v_s, kt_s, vt_s, d_s, dt_s, dk_s, dv_s = refs[6 + 2 * blocks :]
    scale = QSCALAR ** (-0.5)
    factor = scale * LOG2E
    span = blocks * count
    wide = heads * group * HD
    narrow = heads * HD
    per_block = count // TILE
    reach = -(-(W - 1) // TILE)
    me = at_ref[0]
    for part in range(blocks):
        rows = aligned(me ^ part, count)
        pack = packs[part]
        q_s[rows, :] = pack[:count, :wide]
        keys = pack[:count, wide : wide + narrow]
        values = pack[:count, wide + narrow :]
        k_s[rows, :] = keys
        v_s[rows, :] = values
        kt_s[:, rows] = keys.T
        vt_s[:, rows] = values.T
        d_s[rows, :] = dpacks[part][...]
        dt_s[:, rows] = dpacks[part][...].T
    dk_s[...] = jnp.zeros_like(dk_s)
    dv_s[...] = jnp.zeros_like(dv_s)

    def stored(index):
        return aligned(((index // per_block) ^ me) * per_block + lax.rem(index, per_block), TILE)

    def rotated(grad, rows):
        return grad * cos_ref[rows, :] + pltpu.roll(grad, HD // 2, 1) * sin_ref[rows, :]

    for head in range(heads):
        kv = slice(head * HD, (head + 1) * HD)

        def tile(index, first_key, width):
            index = jnp.int32(index)
            q_rows = aligned(index, TILE)
            t_rows = stored(index)
            k_rows = pl.ds(first_key, width)
            columns = [slice(head * group * HD + g * HD, head * group * HD + (g + 1) * HD) for g in range(group)]
            query = jnp.concatenate([q_s[q_rows, c] for c in columns], axis=0)
            dattn = jnp.concatenate([d_s[q_rows, c] for c in columns], axis=0)
            dattn_t = jnp.concatenate([dt_s[c, q_rows] for c in columns], axis=1)
            scores = dot_nt(k_s[k_rows, kv], query)
            low = jnp.concatenate([low_ref[:, t_rows]] * group, axis=1)
            at = first_key + lax.broadcasted_iota(jnp.int32, (width, group * TILE), 0)
            own = index * TILE + lax.rem(
                lax.broadcasted_iota(jnp.int32, (1, group * TILE), 1), jnp.int32(TILE)
            )
            scores = jnp.where((at >= low) & (at <= own), scores, NEGATIVE)
            top = jnp.max(scores, axis=0, keepdims=True)
            weights = jnp.exp2(scores * factor - top * factor)
            inverse = 1.0 / jnp.sum(weights, axis=0, keepdims=True)
            probs = weights * inverse
            half = probs.astype(jnp.bfloat16)
            attn = dot_nn(vt_s[kv, k_rows], half).astype(jnp.bfloat16)
            dprobs = dot_nt(v_s[k_rows, kv], dattn)
            attn_wide = attn.astype(jnp.float32)
            delta = jnp.sum(dattn_t.astype(jnp.float32) * attn_wide, axis=0, keepdims=True)
            dscores = (probs * (dprobs - delta)).astype(jnp.bfloat16)
            query_grad = (dot_nn(kt_s[kv, k_rows], dscores) * scale).T
            attn_rows = attn_wide.T
            dk_s[k_rows, kv] += dot_nn(dscores, query)
            dv_s[k_rows, kv] += dot_nn(half, dattn)
            for g, c in enumerate(columns):
                part = slice(g * TILE, (g + 1) * TILE)
                first_ref[q_rows, c] = attn_rows[part].astype(jnp.bfloat16)
                second_ref[q_rows, c] = rotated(query_grad[part], t_rows).astype(jnp.bfloat16)

        tiles = span // TILE
        for index in range(min(reach, tiles)):
            tile(index, 0, (index + 1) * TILE)

        def steady(index, carry):
            tile(index, pl.multiple_of((index - reach) * TILE, TILE), (reach + 1) * TILE)
            return carry

        if tiles > reach:
            lax.fori_loop(reach, tiles, steady, 0)
        out = slice(wide + head * HD, wide + (head + 1) * HD)
        for index in range(tiles):
            rows = pl.ds(index * TILE, TILE)
            first_ref[rows, out] = dv_s[rows, kv].astype(jnp.bfloat16)
            second_ref[rows, out] = rotated(
                dk_s[rows, kv] * scale, stored(jnp.int32(index))
            ).astype(jnp.bfloat16)


def attention(at, packs, dpacks, low, cosine, sine, heads, group):
    blocks = len(packs)
    count = dpacks[0].shape[0]
    span = blocks * count
    wide = heads * group * HD
    narrow = heads * HD
    half = jnp.bfloat16
    pairs = heads * group * span * (W + TILE)
    return pl.pallas_call(
        functools.partial(attention_kernel, blocks, count, heads, group),
        out_shape=(jax.ShapeDtypeStruct((span, wide + narrow), half),) * 2,
        in_specs=[scalars()] + [whole()] * (2 * blocks + 3),
        out_specs=(whole(),) * 2,
        scratch_shapes=[
            pltpu.VMEM((span, wide), half),
            pltpu.VMEM((span, narrow), half),
            pltpu.VMEM((span, narrow), half),
            pltpu.VMEM((narrow, span), half),
            pltpu.VMEM((narrow, span), half),
            pltpu.VMEM((span, wide), half),
            pltpu.VMEM((wide, span), half),
            pltpu.VMEM((span, narrow), jnp.float32),
            pltpu.VMEM((span, narrow), jnp.float32),
        ],
        compiler_params=params(),
        cost_estimate=pl.CostEstimate(
            flops=10 * pairs * HD, bytes_accessed=span * wide * 12, transcendentals=pairs
        ),
        name="attention_backward",
    )(at, *packs, *dpacks, low, cosine, sine)


def weight_terms_kernel(blocks, jobs, sets, at_ref, *refs):
    pieces = 1 + 2 * (blocks - 1)
    piece_refs = refs[: sets * pieces]
    lin_refs = refs[sets * pieces : -1 - sets]
    out_ref = refs[-1 - sets]
    joined_refs = refs[-sets:]
    me, side = at_ref[0], at_ref[1]
    count = piece_refs[0].shape[1]
    half = count // 2
    for index in range(sets):
        own, *came = piece_refs[index * pieces : (index + 1) * pieces]
        joined_refs[index][:, aligned(me, count)] = own[...]
        for part in range(1, blocks):
            there = (me ^ part) * 2
            joined_refs[index][:, aligned(there + side, half)] = came[2 * part - 2][...]
            joined_refs[index][:, aligned(there + 1 - side, half)] = came[2 * part - 1][...]
    first = 0
    for which, lin, low, high in jobs:
        term = dot_nn(joined_refs[which][...], lin_refs[lin][:, low:high])
        out_ref[:, first : first + high - low] = term.astype(out_ref.dtype)
        first += high - low


def weight_terms(at, sets, lins, jobs, blocks, replicas, load=LOAD):
    share = sets[0][0].shape[0]
    steps = STEPS if share % (STEPS * EXTRA) == 0 else 1
    rows = share // steps
    span = lins[0].shape[0]
    cols = sum(job[3] - job[2] for job in jobs)
    pieces = [x for one in sets for x in one]

    def piece(x):
        return pl.BlockSpec((rows, x.shape[1]), lambda i, at: (i, 0))

    def fixed(x):
        return pl.BlockSpec(x.shape, lambda i, at: (0, 0))

    return pl.pallas_call(
        functools.partial(weight_terms_kernel, blocks, jobs, len(sets)),
        out_shape=jax.ShapeDtypeStruct((share, cols), lins[0].dtype),
        grid_spec=pltpu.PrefetchScalarGridSpec(
            num_scalar_prefetch=1,
            grid=(steps,),
            in_specs=[piece(x) for x in pieces] + [fixed(x) for x in lins],
            out_specs=pl.BlockSpec((rows, cols), lambda i, at: (i, 0)),
            scratch_shapes=[pltpu.VMEM((rows, span), lins[0].dtype)] * len(sets),
        ),
        compiler_params=params(VMEM_MOST),
        cost_estimate=pl.CostEstimate(
            flops=load * share * span * cols,
            bytes_accessed=2 * share * span * len(sets) + 2 * (span + share) * cols,
            transcendentals=0,
        ),
        name="weight_terms",
    )(at, *pieces, *lins)


def assemble_kernel(places, at_ref, *refs):
    parts, outs = refs[:-4], refs[-4:]
    me = at_ref[0]
    for part, one in zip(parts, places):
        first = 0
        for out, source, cols in one:
            outs[out][:, aligned(me ^ source, cols)] = part[:, first : first + cols].astype(
                jnp.float32
            )
            first += cols


def assemble(at, places, parts, blocks, wide, narrow):
    rows = parts[0].shape[0]
    shapes = [
        jax.ShapeDtypeStruct((rows, blocks * cols), jnp.float32)
        for cols in (wide, narrow, wide, narrow)
    ]
    return pl.pallas_call(
        functools.partial(assemble_kernel, places),
        out_shape=tuple(shapes),
        in_specs=[scalars()] + [whole()] * len(parts),
        out_specs=(whole(),) * 4,
        compiler_params=params(),
        name="assemble",
    )(at, *parts)


def input_first_kernel(blocks, wide, narrow, at_ref, *refs):
    firsts, seconds = refs[: blocks - 1], refs[blocks - 1 : 2 * (blocks - 1)]
    wq_ref, wk_ref, wv_ref, out_ref, q_s, k_s, v_s = refs[2 * (blocks - 1) :]
    me = at_ref[0]

    @pl.when(pl.program_id(0) == 0)
    def _():
        q_s[...] = jnp.zeros_like(q_s)
        k_s[...] = jnp.zeros_like(k_s)
        v_s[...] = jnp.zeros_like(v_s)
        for part in range(blocks - 1):
            there = me ^ part
            q_s[:, aligned(there, wide)] = seconds[part][:, :wide]
            k_s[:, aligned(there, narrow)] = seconds[part][:, wide:]
            v_s[:, aligned(there, narrow)] = firsts[part][:, wide:]

    total = dot_nt(q_s[...], wq_ref[...])
    total = total + dot_nt(k_s[...], wk_ref[...])
    out_ref[...] = total + dot_nt(v_s[...], wv_ref[...])


def input_last_kernel(wide, at_ref, first_ref, second_ref, wq_ref, wk_ref, wv_ref, part_ref, mine_ref, sent_ref, total_s):
    side = at_ref[1]
    half = first_ref.shape[0] // 2
    total = part_ref[...] + dot_nt(second_ref[:, :wide], wq_ref[...])
    total = total + dot_nt(second_ref[:, wide:], wk_ref[...])
    total_s[...] = total + dot_nt(first_ref[:, wide:], wv_ref[...])
    for target, which in ((sent_ref, 1 - side), (mine_ref, side)):
        target[...] = total_s[aligned(which, half), :].astype(target.dtype)


def columns_step(width):
    return next(s for s in (768, 512, 256, 128, width) if width % s == 0)


def input_first(at, firsts, seconds, w_query, w_key, w_value, count, wide, narrow):
    blocks = len(firsts) + 1
    width = w_query.shape[0]
    step = columns_step(width)
    ins = firsts + seconds
    half = jnp.bfloat16
    return pl.pallas_call(
        functools.partial(input_first_kernel, blocks, wide, narrow),
        out_shape=jax.ShapeDtypeStruct((count, width), jnp.float32),
        grid_spec=pltpu.PrefetchScalarGridSpec(
            num_scalar_prefetch=1,
            grid=(width // step,),
            in_specs=[pl.BlockSpec((count, x.shape[1]), lambda i, at: (at[0], 0)) for x in ins]
            + [
                pl.BlockSpec((step, x.shape[1]), lambda i, at: (i, 0))
                for x in (w_query, w_key, w_value)
            ],
            out_specs=pl.BlockSpec((count, step), lambda i, at: (0, i)),
            scratch_shapes=[
                pltpu.VMEM((count, blocks * wide), half),
                pltpu.VMEM((count, blocks * narrow), half),
                pltpu.VMEM((count, blocks * narrow), half),
            ],
        ),
        compiler_params=params(VMEM_MOST),
        cost_estimate=pl.CostEstimate(
            flops=count * width * blocks * (wide + 2 * narrow), bytes_accessed=0, transcendentals=0
        ),
        name="input_first",
    )(at, *ins, w_query, w_key, w_value)


def input_last(at, far, first, second, partial, w_query, w_key, w_value, wide, narrow):
    count, width = partial.shape
    step = columns_step(width)

    def own(x):
        return pl.BlockSpec((count, x.shape[1]), lambda i, at: (at[0], 0))

    def weight(cols):
        return pl.BlockSpec((step, cols), lambda i, at: (i, at[0] ^ far))

    out = pl.BlockSpec((count // 2, step), lambda i, at: (0, i))
    return pl.pallas_call(
        functools.partial(input_last_kernel, wide),
        out_shape=(
            jax.ShapeDtypeStruct((count // 2, width), jnp.float32),
            jax.ShapeDtypeStruct((count // 2, width), jnp.bfloat16),
        ),
        grid_spec=pltpu.PrefetchScalarGridSpec(
            num_scalar_prefetch=1,
            grid=(width // step,),
            in_specs=[own(first), own(second), weight(wide), weight(narrow), weight(narrow)]
            + [pl.BlockSpec((count, step), lambda i, at: (0, i))],
            out_specs=(out, out),
            scratch_shapes=[pltpu.VMEM((count, step), jnp.float32)],
        ),
        compiler_params=params(VMEM_MOST),
        cost_estimate=pl.CostEstimate(
            flops=COST * count * width * (wide + 2 * narrow), bytes_accessed=0, transcendentals=0
        ),
        name="input_last",
    )(at, first, second, w_query, w_key, w_value, partial)


def swap(x, axis, by):
    count = lax.axis_size(axis)
    return lax.ppermute(x, axis, [(i, i ^ by) for i in range(count)])


def rotation_tables(places):
    half = HD // 2
    index = jnp.arange(half, dtype=jnp.float32)
    freq = jnp.power(jnp.float32(10000.0), index * (-2.0 / HD))
    angle = places.astype(jnp.float32)[:, None] * freq[None, :]
    cosine = jnp.cos(angle)
    sine = jnp.sin(angle)
    return jnp.concatenate([cosine, cosine], axis=1), jnp.concatenate([sine, -sine], axis=1)


def on_device(
    inputs,
    queries,
    key_states,
    value_states,
    out_grad,
    positions,
    w_query,
    w_key,
    w_value,
    w_output,
):
    count = queries.shape[0]
    head_cols = queries.shape[1]
    kv_cols = key_states.shape[1]
    kv_here = kv_cols // HD
    group = head_cols // kv_cols
    blocks = lax.axis_size("context")
    replicas = lax.axis_size("dp")
    cores = lax.axis_size("tensor")
    width = inputs.shape[1]
    heads = kv_here // blocks
    wide = heads * group * HD
    narrow = heads * HD
    fits = (
        blocks == 4
        and kv_here % blocks == 0
        and cores == 2
        and count % (2 * HD) == 0
        and count % TILE == 0
        and W % TILE == 0
        and width % HD == 0
        and width % (replicas * blocks * EXTRA) == 0
        and wide + 2 * narrow >= count
    )
    if not fits:
        return banded(
            inputs, queries, key_states, value_states, out_grad, positions,
            w_query, w_key, w_value, w_output,
        )
    me = lax.axis_index("context")
    side = lax.axis_index("tensor")
    at = jnp.stack([me, side]).astype(jnp.int32)

    barrier = lax.optimization_barrier

    digits = jnp.stack([positions // RADIX, positions % RADIX]).astype(jnp.bfloat16)
    extra = jnp.pad(digits, ((0, EXTRA - 2), (0, wide + 2 * narrow - count)))
    packs = list(
        pack_heads(at, queries, key_states, value_states, extra, blocks, wide, narrow)
    )
    after, packs = barrier((out_grad, packs))
    for part in range(1, blocks):
        packs[part] = swap(packs[part], "context", part)
    dattn = jnp.dot(after, w_output, preferred_element_type=jnp.float32).astype(jnp.bfloat16)
    dpacks = [
        lax.dynamic_slice(dattn, (0, (me ^ part) * wide), (count, wide)) for part in range(blocks)
    ]
    def spread(packed):
        return [swap(x, "context", part + 1) for part, x in enumerate(packed)]

    def joined(own, came):
        pieces = [own]
        for x in came:
            pieces += [x, swap(x, "tensor", 1)]
        return pieces

    soon, dpacks = barrier((at, dpacks))
    grad_own, *grad_packed = pack_rows(soon, out_grad, blocks, replicas)
    soon, grad_packed = barrier((soon, grad_packed))
    input_own, *input_packed = pack_rows(soon, inputs, blocks, replicas)
    packs, dpacks, grad_packed, input_packed = barrier((packs, dpacks, grad_packed, input_packed))
    dpacks = [dpacks[0]] + spread(dpacks[1:])
    places = [
        (pack[count, :count].astype(jnp.float32) * RADIX + pack[count + 1, :count].astype(jnp.float32)).astype(jnp.int32)
        for pack in packs[1:]
    ]
    places = jnp.concatenate([positions] + places)
    index = jnp.concatenate(
        [(me ^ part) * count + jnp.arange(count, dtype=jnp.int32) for part in range(blocks)]
    )
    low = jnp.maximum(index - places, index - (W - 1))[None, :]
    cosine, sine = rotation_tables(places)
    grad_came = spread(grad_packed)
    first, second = attention(at, packs, dpacks, low, cosine, sine, heads, group)
    first, second, grad_came, input_packed = barrier((first, second, grad_came, input_packed))

    input_came = spread(input_packed)
    grads = joined(grad_own, grad_came)
    edge = wide + narrow
    def summed(term):
        return lax.psum_scatter(term, "dp", scatter_dimension=0, tiled=True)

    parts = []
    term = weight_terms(at, [grads], [first], [(0, 0, 0, wide)], blocks, replicas, LOAD1)
    parts.append(summed(term))
    term, input_came, first, second = barrier((term, input_came, first, second))

    firsts = [first, swap(first, "context", 1), None, None]
    seconds = [second, None, swap(second, "context", 2), None]
    ins = joined(input_own, input_came)
    ins, parts[0] = barrier((ins, parts[0]))
    jobs = [(0, 0, wide, edge), (0, 1, 0, edge)]
    term = weight_terms(at, [ins], [first, second], jobs, blocks, replicas, LOAD2)
    parts.append(summed(term))
    term, firsts[1], seconds[2], first, second = barrier(
        (term, firsts[1], seconds[2], first, second)
    )
    seconds[1] = swap(second, "context", 1)
    firsts[2] = swap(first, "context", 2)
    jobs = [(0, 0, 0, wide), (1, 0, wide, edge), (1, 1, 0, edge)]

    def terms_of(source_first, source_second):
        lins = [firsts[source_first], seconds[source_second]]
        return weight_terms(at, [grads, ins], lins, jobs, blocks, replicas)

    term = terms_of(1, 2)
    parts.append(summed(term))
    term, firsts[1], firsts[2], seconds[1], seconds[2] = barrier(
        (term, firsts[1], firsts[2], seconds[1], seconds[2])
    )
    firsts[3] = swap(firsts[1], "context", 2)
    seconds[3] = swap(seconds[2], "context", 1)
    term = terms_of(2, 1)
    parts.append(summed(term))
    late, term = barrier((at, term))
    partial = input_first(
        late, firsts[:3], seconds[:3], w_query, w_key, w_value, count, wide, narrow
    )
    term, partial, parts[1], firsts[3], seconds[3] = barrier(
        (term, partial, parts[1], firsts[3], seconds[3])
    )
    mine, sent = input_last(
        at, 3, firsts[3], seconds[3], partial, w_query, w_key, w_value, wide, narrow
    )
    came = swap(sent, "tensor", 1)
    mine, firsts[3] = barrier((mine, firsts[3]))
    term = terms_of(3, 3)
    parts.append(summed(term))
    mine, came, parts[2], parts[3] = barrier((mine, came, parts[2], parts[3]))
    input_grad = (mine + came.astype(jnp.float32)).astype(jnp.bfloat16)
    last, input_grad = barrier((at, input_grad))

    def rest(source_first, source_second):
        return [(1, source_first, narrow), (2, source_second, wide), (3, source_second, narrow)]

    layout = [[(0, 0, wide)], rest(0, 0)]
    for source_first, source_second in ((1, 2), (2, 1), (3, 3)):
        layout.append([(0, source_first, wide)] + rest(source_first, source_second))
    grad_output, grad_value, grad_query, grad_key = assemble(
        last, layout, parts, blocks, wide, narrow
    )
    return (input_grad, grad_query, grad_key, grad_value, grad_output)


def solution(mesh):
    return jax.shard_map(
        on_device,
        mesh=mesh,
        in_specs=(
            P(("dp", "context"), None),
            P(("dp", "context"), "tensor"),
            P(("dp", "context"), "tensor"),
            P(("dp", "context"), "tensor"),
            P(("dp", "context"), None),
            P(("dp", "context")),
            P(None, "tensor"),
            P(None, "tensor"),
            P(None, "tensor"),
            P(None, "tensor"),
        ),
        out_specs=(
            P(("dp", "context", "tensor"), None),
            P(("dp", "context"), "tensor"),
            P(("dp", "context"), "tensor"),
            P(("dp", "context"), "tensor"),
            P(("dp", "context"), "tensor"),
        ),
        check_vma=False,
    )
```

```python
import functools

import jax
import jax.numpy as jnp
from jax import lax
from jax.experimental import pallas as pl
from jax.experimental.pallas import tpu as pltpu
from jax.sharding import PartitionSpec as P

HD = 128
W = 1024
QSCALAR = 168


def shifted(x, axis, by):
    count = lax.axis_size(axis)
    pairs = [(i, i + by) for i in range(count) if 0 <= i + by < count]
    return lax.ppermute(x, axis, pairs)


def rotate_back(grads, places):
    count = grads.shape[0]
    half = HD // 2
    index = jnp.arange(half, dtype=jnp.float32)
    freq = jnp.power(jnp.float32(10000.0), index * (-2.0 / HD))
    angle = places.astype(jnp.float32)[:, None] * freq[None, :]
    cosine = jnp.cos(angle)[:, None, :]
    sine = jnp.sin(angle)[:, None, :]
    split = grads.reshape(count, -1, 2, half)
    first = split[:, :, 0, :]
    second = split[:, :, 1, :]
    upper = first * cosine + second * sine
    lower = second * cosine - first * sine
    return jnp.stack([upper, lower], axis=2).reshape(count, -1)


def contract_rows(left, right):
    return lax.dot_general(
        left, right, (((0,), (0,)), ((), ())), preferred_element_type=jnp.float32
    )


def contract_cols(left, right):
    return lax.dot_general(
        left, right, (((1,), (1,)), ((), ())), preferred_element_type=jnp.float32
    )


def banded(
    inputs,
    queries,
    key_states,
    value_states,
    out_grad,
    positions,
    w_query,
    w_key,
    w_value,
    w_output,
):
    count = queries.shape[0]
    head_cols = queries.shape[1]
    kv_cols = key_states.shape[1]
    kv_here = kv_cols // HD
    group = head_cols // kv_cols
    scale = QSCALAR ** (-0.5)
    block = lax.axis_index("context")
    blocks = lax.axis_size("context")
    reach = min((W + count - 2) // count, blocks - 1)
    span = (reach + 1) * count
    key_pieces = []
    value_pieces = []
    for back in range(reach, 0, -1):
        earlier_keys, earlier_values = shifted((key_states, value_states), "context", back)
        key_pieces.append(earlier_keys)
        value_pieces.append(earlier_values)
    band_keys = jnp.concatenate(key_pieces + [key_states], axis=0)
    band_values = jnp.concatenate(value_pieces + [value_states], axis=0)
    query_index = block * count + jnp.arange(count, dtype=jnp.int32)
    key_index = (block - reach) * count + jnp.arange(span, dtype=jnp.int32)
    doc_start = query_index - positions
    allowed = (key_index[None, :] <= query_index[:, None]) & (
        query_index[:, None] - key_index[None, :] < W
    )
    allowed = allowed & (key_index[None, :] >= doc_start[:, None]) & (key_index[None, :] >= 0)
    query_heads = queries.reshape(count, kv_here, group, HD)
    key_heads = band_keys.reshape(span, kv_here, HD)
    value_heads = band_values.reshape(span, kv_here, HD)
    scores = (
        jnp.einsum("qhgd,khd->hgqk", query_heads, key_heads, preferred_element_type=jnp.float32)
        * scale
    )
    scores = jnp.where(allowed, scores, -1e30)
    top = jnp.max(scores, axis=-1, keepdims=True)
    weights = jnp.exp(scores - top)
    probs = weights / jnp.sum(weights, axis=-1, keepdims=True)
    probs_half = probs.astype(jnp.bfloat16)
    attn = jnp.einsum(
        "hgqk,khd->qhgd", probs_half, value_heads, preferred_element_type=jnp.float32
    ).astype(jnp.bfloat16)
    attn_flat = attn.reshape(count, head_cols)
    dattn = jnp.dot(out_grad, w_output, preferred_element_type=jnp.float32).astype(jnp.bfloat16)
    dattn_heads = dattn.reshape(count, kv_here, group, HD)
    dprobs = jnp.einsum(
        "qhgd,khd->hgqk", dattn_heads, value_heads, preferred_element_type=jnp.float32
    )
    delta = jnp.sum(dattn_heads.astype(jnp.float32) * attn.astype(jnp.float32), axis=-1)
    delta = jnp.transpose(delta, (1, 2, 0))[..., None]
    dscores = (probs * (dprobs - delta) * scale).astype(jnp.bfloat16)
    query_grad = jnp.einsum(
        "hgqk,khd->qhgd", dscores, key_heads, preferred_element_type=jnp.float32
    ).reshape(count, head_cols)
    band_key_grad = jnp.einsum(
        "hgqk,qhgd->khd", dscores, query_heads, preferred_element_type=jnp.float32
    ).reshape(span, kv_cols)
    band_value_grad = jnp.einsum(
        "hgqk,qhgd->khd", probs_half, dattn_heads, preferred_element_type=jnp.float32
    ).reshape(span, kv_cols)
    key_grad = band_key_grad[reach * count :]
    value_grad = band_value_grad[reach * count :]
    for back in range(1, reach + 1):
        first_row = (reach - back) * count
        sent_keys, sent_values = shifted(
            (
                band_key_grad[first_row : first_row + count],
                band_value_grad[first_row : first_row + count],
            ),
            "context",
            -back,
        )
        key_grad = key_grad + sent_keys
        value_grad = value_grad + sent_values
    query_lin = rotate_back(query_grad, positions).astype(jnp.bfloat16)
    key_lin = rotate_back(key_grad, positions).astype(jnp.bfloat16)
    value_half = value_grad.astype(jnp.bfloat16)
    total = contract_cols(query_lin, w_query)
    total = total + contract_cols(key_lin, w_key)
    total = total + contract_cols(value_half, w_value)
    input_grad = lax.psum_scatter(total, "tensor", scatter_dimension=0, tiled=True).astype(
        jnp.bfloat16
    )
    terms = (
        contract_rows(inputs, query_lin),
        contract_rows(inputs, key_lin),
        contract_rows(inputs, value_half),
        contract_rows(out_grad, attn_flat),
    )
    summed = (
        lax.psum_scatter(
            terms[0].astype(jnp.bfloat16), ("dp", "context"), scatter_dimension=0, tiled=True
        ).astype(jnp.float32),
        lax.psum_scatter(
            terms[1].astype(jnp.bfloat16), ("dp", "context"), scatter_dimension=0, tiled=True
        ).astype(jnp.float32),
        lax.psum_scatter(
            terms[2].astype(jnp.bfloat16), ("dp", "context"), scatter_dimension=0, tiled=True
        ).astype(jnp.float32),
        lax.psum_scatter(
            terms[3].astype(jnp.bfloat16), ("dp", "context"), scatter_dimension=0, tiled=True
        ).astype(jnp.float32),
    )
    return (input_grad, summed[0], summed[1], summed[2], summed[3])


TILE = 256
EXTRA = 16
RADIX = 128
NEGATIVE = -1e30
LOG2E = 1.4426950408889634
VMEM_LIMIT = 48 * 1024 * 1024
LOAD = 40
LOAD1 = 12
LOAD2 = 12
COST = 80
VMEM_MOST = 60 * 1024 * 1024


def dot_nt(left, right):
    return lax.dot_general(
        left, right, (((1,), (1,)), ((), ())), preferred_element_type=jnp.float32
    )


def dot_nn(left, right):
    return lax.dot_general(
        left, right, (((1,), (0,)), ((), ())), preferred_element_type=jnp.float32
    )


def whole():
    return pl.BlockSpec(memory_space=pltpu.VMEM)


def scalars():
    return pl.BlockSpec(memory_space=pltpu.SMEM)


def params(limit=VMEM_LIMIT):
    return pltpu.CompilerParams(vmem_limit_bytes=limit)


def aligned(index, size):
    return pl.ds(pl.multiple_of(index * size, size), size)


def pack_heads_kernel(blocks, wide, narrow, at_ref, q_ref, k_ref, v_ref, extra_ref, *outs):
    me = at_ref[0]
    count = q_ref.shape[0]
    for part in range(blocks):
        there = me ^ part
        out = outs[part]
        out[:count, :wide] = q_ref[:, aligned(there, wide)]
        out[:count, wide : wide + narrow] = k_ref[:, aligned(there, narrow)]
        out[:count, wide + narrow :] = v_ref[:, aligned(there, narrow)]
        out[count:, :] = extra_ref[...]


def pack_heads(at, queries, key_states, value_states, extra, blocks, wide, narrow):
    count = queries.shape[0]
    shape = jax.ShapeDtypeStruct((count + EXTRA, wide + 2 * narrow), queries.dtype)
    return pl.pallas_call(
        functools.partial(pack_heads_kernel, blocks, wide, narrow),
        out_shape=(shape,) * blocks,
        in_specs=[scalars()] + [pl.BlockSpec(x.shape, lambda: (0, 0)) for x in (queries, key_states, value_states, extra)],
        out_specs=(whole(),) * blocks,
        compiler_params=params(VMEM_MOST),
        cost_estimate=pl.CostEstimate(
            flops=0, bytes_accessed=4 * blocks * count * (wide + 2 * narrow), transcendentals=0
        ),
        name="pack_heads",
    )(at, queries, key_states, value_states, extra)


def pack_rows_kernel(blocks, replicas, rows, at_ref, x_ref, own_ref, *rest):
    outs, turned = rest[:-1], rest[-1]
    me, side = at_ref[0], at_ref[1]
    count, width = x_ref.shape
    half = count // 2

    step = next(n for n in (6, 3, 2, 1) if width % (n * HD) == 0) * HD

    def turn(index, carry):
        cols = aligned(index, step)
        turned[cols, :] = x_ref[:, cols].T
        return carry

    lax.fori_loop(0, width // step, turn, 0)
    for replica in range(replicas):
        into = pl.ds(replica * rows, rows)
        own_ref[into, :] = turned[aligned(replica * blocks + me, rows), :]
        for part in range(1, blocks):
            taken = aligned(replica * blocks + (me ^ part), rows)
            outs[part - 1][into, :] = turned[taken, aligned(side, half)]


def pack_rows(at, x, blocks, replicas):
    count, width = x.shape
    rows = width // (replicas * blocks)
    share = replicas * rows
    own = jax.ShapeDtypeStruct((share, count), x.dtype)
    sent = jax.ShapeDtypeStruct((share, count // 2), x.dtype)
    return pl.pallas_call(
        functools.partial(pack_rows_kernel, blocks, replicas, rows),
        out_shape=(own,) + (sent,) * (blocks - 1),
        in_specs=[scalars(), whole()],
        out_specs=(whole(),) * blocks,
        scratch_shapes=[pltpu.VMEM((width, count), x.dtype)],
        compiler_params=params(),
        cost_estimate=pl.CostEstimate(
            flops=0, bytes_accessed=6 * count * width, transcendentals=0
        ),
        name="pack_rows",
    )(at, x)


def attention_kernel(blocks, count, heads, group, *refs):
    at_ref = refs[0]
    packs = refs[1 : 1 + blocks]
    dpacks = refs[1 + blocks : 1 + 2 * blocks]
    low_ref, cos_ref, sin_ref = refs[1 + 2 * blocks : 4 + 2 * blocks]
    first_ref, second_ref = refs[4 + 2 * blocks : 6 + 2 * blocks]
    q_s, k_s, v_s, kt_s, vt_s, d_s, dt_s, dk_s, dv_s = refs[6 + 2 * blocks :]
    scale = QSCALAR ** (-0.5)
    factor = scale * LOG2E
    span = blocks * count
    wide = heads * group * HD
    narrow = heads * HD
    per_block = count // TILE
    reach = -(-(W - 1) // TILE)
    me = at_ref[0]
    for part in range(blocks):
        rows = aligned(me ^ part, count)
        pack = packs[part]
        q_s[rows, :] = pack[:count, :wide]
        keys = pack[:count, wide : wide + narrow]
        values = pack[:count, wide + narrow :]
        k_s[rows, :] = keys
        v_s[rows, :] = values
        kt_s[:, rows] = keys.T
        vt_s[:, rows] = values.T
        d_s[rows, :] = dpacks[part][...]
        dt_s[:, rows] = dpacks[part][...].T
    dk_s[...] = jnp.zeros_like(dk_s)
    dv_s[...] = jnp.zeros_like(dv_s)

    def stored(index):
        return aligned(((index // per_block) ^ me) * per_block + lax.rem(index, per_block), TILE)

    def rotated(grad, rows):
        return grad * cos_ref[rows, :] + pltpu.roll(grad, HD // 2, 1) * sin_ref[rows, :]

    for head in range(heads):
        kv = slice(head * HD, (head + 1) * HD)

        def tile(index, first_key, width):
            index = jnp.int32(index)
            q_rows = aligned(index, TILE)
            t_rows = stored(index)
            k_rows = pl.ds(first_key, width)
            columns = [slice(head * group * HD + g * HD, head * group * HD + (g + 1) * HD) for g in range(group)]
            query = jnp.concatenate([q_s[q_rows, c] for c in columns], axis=0)
            dattn = jnp.concatenate([d_s[q_rows, c] for c in columns], axis=0)
            dattn_t = jnp.concatenate([dt_s[c, q_rows] for c in columns], axis=1)
            scores = dot_nt(k_s[k_rows, kv], query)
            low = jnp.concatenate([low_ref[:, t_rows]] * group, axis=1)
            at = first_key + lax.broadcasted_iota(jnp.int32, (width, group * TILE), 0)
            own = index * TILE + lax.rem(
                lax.broadcasted_iota(jnp.int32, (1, group * TILE), 1), jnp.int32(TILE)
            )
            scores = jnp.where((at >= low) & (at <= own), scores, NEGATIVE)
            top = jnp.max(scores, axis=0, keepdims=True)
            weights = jnp.exp2(scores * factor - top * factor)
            inverse = 1.0 / jnp.sum(weights, axis=0, keepdims=True)
            probs = weights * inverse
            half = probs.astype(jnp.bfloat16)
            attn = dot_nn(vt_s[kv, k_rows], half).astype(jnp.bfloat16)
            dprobs = dot_nt(v_s[k_rows, kv], dattn)
            attn_wide = attn.astype(jnp.float32)
            delta = jnp.sum(dattn_t.astype(jnp.float32) * attn_wide, axis=0, keepdims=True)
            dscores = (probs * (dprobs - delta)).astype(jnp.bfloat16)
            query_grad = (dot_nn(kt_s[kv, k_rows], dscores) * scale).T
            attn_rows = attn_wide.T
            dk_s[k_rows, kv] += dot_nn(dscores, query)
            dv_s[k_rows, kv] += dot_nn(half, dattn)
            for g, c in enumerate(columns):
                part = slice(g * TILE, (g + 1) * TILE)
                first_ref[q_rows, c] = attn_rows[part].astype(jnp.bfloat16)
                second_ref[q_rows, c] = rotated(query_grad[part], t_rows).astype(jnp.bfloat16)

        tiles = span // TILE
        for index in range(min(reach, tiles)):
            tile(index, 0, (index + 1) * TILE)

        def steady(index, carry):
            tile(index, pl.multiple_of((index - reach) * TILE, TILE), (reach + 1) * TILE)
            return carry

        if tiles > reach:
            lax.fori_loop(reach, tiles, steady, 0)
        out = slice(wide + head * HD, wide + (head + 1) * HD)
        for index in range(tiles):
            rows = pl.ds(index * TILE, TILE)
            first_ref[rows, out] = dv_s[rows, kv].astype(jnp.bfloat16)
            second_ref[rows, out] = rotated(
                dk_s[rows, kv] * scale, stored(jnp.int32(index))
            ).astype(jnp.bfloat16)


def attention(at, packs, dpacks, low, cosine, sine, heads, group):
    blocks = len(packs)
    count = dpacks[0].shape[0]
    span = blocks * count
    wide = heads * group * HD
    narrow = heads * HD
    half = jnp.bfloat16
    pairs = heads * group * span * (W + TILE)
    return pl.pallas_call(
        functools.partial(attention_kernel, blocks, count, heads, group),
        out_shape=(jax.ShapeDtypeStruct((span, wide + narrow), half),) * 2,
        in_specs=[scalars()] + [whole()] * (2 * blocks + 3),
        out_specs=(whole(),) * 2,
        scratch_shapes=[
            pltpu.VMEM((span, wide), half),
            pltpu.VMEM((span, narrow), half),
            pltpu.VMEM((span, narrow), half),
            pltpu.VMEM((narrow, span), half),
            pltpu.VMEM((narrow, span), half),
            pltpu.VMEM((span, wide), half),
            pltpu.VMEM((wide, span), half),
            pltpu.VMEM((span, narrow), jnp.float32),
            pltpu.VMEM((span, narrow), jnp.float32),
        ],
        compiler_params=params(),
        cost_estimate=pl.CostEstimate(
            flops=10 * pairs * HD, bytes_accessed=span * wide * 12, transcendentals=pairs
        ),
        name="attention_backward",
    )(at, *packs, *dpacks, low, cosine, sine)


def weight_terms_kernel(blocks, jobs, at_ref, *refs):
    pieces = 1 + 2 * (blocks - 1)
    sets = 1 + max(job[0] for job in jobs)
    piece_refs = refs[: sets * pieces]
    lin_refs = refs[sets * pieces : -1]
    out_ref = refs[-1]
    me, side = at_ref[0], at_ref[1]
    count = piece_refs[0].shape[1]
    half = count // 2
    rows = [aligned(me, count)]
    for part in range(1, blocks):
        rows.append(aligned((me ^ part) * 2 + side, half))
        rows.append(aligned((me ^ part) * 2 + 1 - side, half))
    total = [None] * len(jobs)
    for piece in range(pieces):
        for index, (which, lin, low, high) in enumerate(jobs):
            left = piece_refs[which * pieces + piece][...]
            term = dot_nn(left, lin_refs[lin][rows[piece], low:high])
            total[index] = term if total[index] is None else total[index] + term
    first = 0
    for index, (which, lin, low, high) in enumerate(jobs):
        out_ref[:, first : first + high - low] = total[index].astype(out_ref.dtype)
        first += high - low


def weight_terms(at, sets, lins, jobs, blocks, replicas, load=LOAD):
    share = sets[0][0].shape[0]
    rows = share // replicas
    span = lins[0].shape[0]
    cols = sum(job[3] - job[2] for job in jobs)
    pieces = [x for one in sets for x in one]

    def piece(x):
        return pl.BlockSpec((rows, x.shape[1]), lambda i, at: (i, 0))

    def fixed(x):
        return pl.BlockSpec(x.shape, lambda i, at: (0, 0))

    return pl.pallas_call(
        functools.partial(weight_terms_kernel, blocks, jobs),
        out_shape=jax.ShapeDtypeStruct((share, cols), lins[0].dtype),
        grid_spec=pltpu.PrefetchScalarGridSpec(
            num_scalar_prefetch=1,
            grid=(replicas,),
            in_specs=[piece(x) for x in pieces] + [fixed(x) for x in lins],
            out_specs=pl.BlockSpec((rows, cols), lambda i, at: (i, 0)),
        ),
        compiler_params=params(VMEM_MOST),
        cost_estimate=pl.CostEstimate(
            flops=load * share * span * cols,
            bytes_accessed=2 * share * span * len(sets) + 2 * (span + share) * cols,
            transcendentals=0,
        ),
        name="weight_terms",
    )(at, *pieces, *lins)


def assemble_kernel(places, at_ref, *refs):
    parts, outs = refs[:-4], refs[-4:]
    me = at_ref[0]
    for part, one in zip(parts, places):
        first = 0
        for out, source, cols in one:
            outs[out][:, aligned(me ^ source, cols)] = part[:, first : first + cols].astype(
                jnp.float32
            )
            first += cols


def assemble(at, places, parts, blocks, wide, narrow):
    rows = parts[0].shape[0]
    shapes = [
        jax.ShapeDtypeStruct((rows, blocks * cols), jnp.float32)
        for cols in (wide, narrow, wide, narrow)
    ]
    return pl.pallas_call(
        functools.partial(assemble_kernel, places),
        out_shape=tuple(shapes),
        in_specs=[scalars()] + [whole()] * len(parts),
        out_specs=(whole(),) * 4,
        compiler_params=params(),
        name="assemble",
    )(at, *parts)


def assemble_last_kernel(places, at_ref, part_ref, *refs):
    outs, wide_s, sems = refs[4:8], refs[8], refs[9]
    me = at_ref[0]
    wide_s[...] = part_ref[...].astype(jnp.float32)
    copies = []
    first = 0
    for index, (out, source, cols) in enumerate(places):
        copies.append(
            pltpu.make_async_copy(
                wide_s.at[:, first : first + cols],
                outs[out].at[:, aligned(me ^ source, cols)],
                sems.at[index],
            )
        )
        copies[-1].start()
        first += cols
    for copy in copies:
        copy.wait()


def assemble_last(at, places, part, grads):
    anywhere = pl.BlockSpec(memory_space=pl.ANY)
    return pl.pallas_call(
        functools.partial(assemble_last_kernel, places),
        out_shape=tuple(jax.ShapeDtypeStruct(x.shape, x.dtype) for x in grads),
        in_specs=[scalars(), whole()] + [anywhere] * 4,
        out_specs=(anywhere,) * 4,
        scratch_shapes=[
            pltpu.VMEM(part.shape, jnp.float32),
            pltpu.SemaphoreType.DMA((len(places),)),
        ],
        input_output_aliases={2: 0, 3: 1, 4: 2, 5: 3},
        compiler_params=params(),
        name="assemble_last",
    )(at, part, *grads)


def input_first_kernel(blocks, wide, narrow, at_ref, *refs):
    firsts, seconds = refs[: blocks - 1], refs[blocks - 1 : 2 * (blocks - 1)]
    wq_ref, wk_ref, wv_ref, out_ref, q_s, k_s, v_s = refs[2 * (blocks - 1) :]
    me = at_ref[0]

    @pl.when(pl.program_id(0) == 0)
    def _():
        q_s[...] = jnp.zeros_like(q_s)
        k_s[...] = jnp.zeros_like(k_s)
        v_s[...] = jnp.zeros_like(v_s)
        for part in range(blocks - 1):
            there = me ^ part
            q_s[:, aligned(there, wide)] = seconds[part][:, :wide]
            k_s[:, aligned(there, narrow)] = seconds[part][:, wide:]
            v_s[:, aligned(there, narrow)] = firsts[part][:, wide:]

    total = dot_nt(q_s[...], wq_ref[...])
    total = total + dot_nt(k_s[...], wk_ref[...])
    out_ref[...] = total + dot_nt(v_s[...], wv_ref[...])


def input_last_kernel(wide, at_ref, first_ref, second_ref, wq_ref, wk_ref, wv_ref, part_ref, mine_ref, sent_ref, total_s):
    side = at_ref[1]
    half = first_ref.shape[0] // 2
    total = part_ref[...] + dot_nt(second_ref[:, :wide], wq_ref[...])
    total = total + dot_nt(second_ref[:, wide:], wk_ref[...])
    total_s[...] = total + dot_nt(first_ref[:, wide:], wv_ref[...])
    for target, which in ((sent_ref, 1 - side), (mine_ref, side)):
        target[...] = total_s[aligned(which, half), :].astype(target.dtype)


def columns_step(width):
    return next(s for s in (768, 512, 256, 128, width) if width % s == 0)


def input_first(at, firsts, seconds, w_query, w_key, w_value, count, wide, narrow):
    blocks = len(firsts) + 1
    width = w_query.shape[0]
    step = columns_step(width)
    ins = firsts + seconds
    half = jnp.bfloat16
    return pl.pallas_call(
        functools.partial(input_first_kernel, blocks, wide, narrow),
        out_shape=jax.ShapeDtypeStruct((count, width), jnp.float32),
        grid_spec=pltpu.PrefetchScalarGridSpec(
            num_scalar_prefetch=1,
            grid=(width // step,),
            in_specs=[pl.BlockSpec((count, x.shape[1]), lambda i, at: (at[0], 0)) for x in ins]
            + [
                pl.BlockSpec((step, x.shape[1]), lambda i, at: (i, 0))
                for x in (w_query, w_key, w_value)
            ],
            out_specs=pl.BlockSpec((count, step), lambda i, at: (0, i)),
            scratch_shapes=[
                pltpu.VMEM((count, blocks * wide), half),
                pltpu.VMEM((count, blocks * narrow), half),
                pltpu.VMEM((count, blocks * narrow), half),
            ],
        ),
        compiler_params=params(VMEM_MOST),
        cost_estimate=pl.CostEstimate(
            flops=count * width * blocks * (wide + 2 * narrow), bytes_accessed=0, transcendentals=0
        ),
        name="input_first",
    )(at, *ins, w_query, w_key, w_value)


def input_last(at, far, first, second, partial, w_query, w_key, w_value, wide, narrow):
    count, width = partial.shape
    step = columns_step(width)

    def own(x):
        return pl.BlockSpec((count, x.shape[1]), lambda i, at: (at[0], 0))

    def weight(cols):
        return pl.BlockSpec((step, cols), lambda i, at: (i, at[0] ^ far))

    out = pl.BlockSpec((count // 2, step), lambda i, at: (0, i))
    return pl.pallas_call(
        functools.partial(input_last_kernel, wide),
        out_shape=(
            jax.ShapeDtypeStruct((count // 2, width), jnp.float32),
            jax.ShapeDtypeStruct((count // 2, width), jnp.bfloat16),
        ),
        grid_spec=pltpu.PrefetchScalarGridSpec(
            num_scalar_prefetch=1,
            grid=(width // step,),
            in_specs=[own(first), own(second), weight(wide), weight(narrow), weight(narrow)]
            + [pl.BlockSpec((count, step), lambda i, at: (0, i))],
            out_specs=(out, out),
            scratch_shapes=[pltpu.VMEM((count, step), jnp.float32)],
        ),
        compiler_params=params(VMEM_MOST),
        cost_estimate=pl.CostEstimate(
            flops=COST * count * width * (wide + 2 * narrow), bytes_accessed=0, transcendentals=0
        ),
        name="input_last",
    )(at, first, second, w_query, w_key, w_value, partial)


def swap(x, axis, by):
    count = lax.axis_size(axis)
    return lax.ppermute(x, axis, [(i, i ^ by) for i in range(count)])


def rotation_tables(places):
    half = HD // 2
    index = jnp.arange(half, dtype=jnp.float32)
    freq = jnp.power(jnp.float32(10000.0), index * (-2.0 / HD))
    angle = places.astype(jnp.float32)[:, None] * freq[None, :]
    cosine = jnp.cos(angle)
    sine = jnp.sin(angle)
    return jnp.concatenate([cosine, cosine], axis=1), jnp.concatenate([sine, -sine], axis=1)


def on_device(
    inputs,
    queries,
    key_states,
    value_states,
    out_grad,
    positions,
    w_query,
    w_key,
    w_value,
    w_output,
):
    count = queries.shape[0]
    head_cols = queries.shape[1]
    kv_cols = key_states.shape[1]
    kv_here = kv_cols // HD
    group = head_cols // kv_cols
    blocks = lax.axis_size("context")
    replicas = lax.axis_size("dp")
    cores = lax.axis_size("tensor")
    width = inputs.shape[1]
    heads = kv_here // blocks
    wide = heads * group * HD
    narrow = heads * HD
    fits = (
        blocks == 4
        and kv_here % blocks == 0
        and cores == 2
        and count % (2 * HD) == 0
        and count % TILE == 0
        and W % TILE == 0
        and width % HD == 0
        and width % (replicas * blocks * EXTRA) == 0
        and wide + 2 * narrow >= count
    )
    if not fits:
        return banded(
            inputs, queries, key_states, value_states, out_grad, positions,
            w_query, w_key, w_value, w_output,
        )
    me = lax.axis_index("context")
    side = lax.axis_index("tensor")
    at = jnp.stack([me, side]).astype(jnp.int32)

    barrier = lax.optimization_barrier

    digits = jnp.stack([positions // RADIX, positions % RADIX]).astype(jnp.bfloat16)
    extra = jnp.pad(digits, ((0, EXTRA - 2), (0, wide + 2 * narrow - count)))
    packs = list(
        pack_heads(at, queries, key_states, value_states, extra, blocks, wide, narrow)
    )
    after, packs = barrier((out_grad, packs))
    for part in range(1, blocks):
        packs[part] = swap(packs[part], "context", part)
    dattn = jnp.dot(after, w_output, preferred_element_type=jnp.float32).astype(jnp.bfloat16)
    dpacks = [
        lax.dynamic_slice(dattn, (0, (me ^ part) * wide), (count, wide)) for part in range(blocks)
    ]
    def spread(packed):
        return [swap(x, "context", part + 1) for part, x in enumerate(packed)]

    def joined(own, came):
        pieces = [own]
        for x in came:
            pieces += [x, swap(x, "tensor", 1)]
        return pieces

    soon, dpacks = barrier((at, dpacks))
    grad_own, *grad_packed = pack_rows(soon, out_grad, blocks, replicas)
    soon, grad_packed = barrier((soon, grad_packed))
    input_own, *input_packed = pack_rows(soon, inputs, blocks, replicas)
    packs, dpacks, grad_packed, input_packed = barrier((packs, dpacks, grad_packed, input_packed))
    dpacks = [dpacks[0]] + spread(dpacks[1:])
    places = [
        (pack[count, :count].astype(jnp.float32) * RADIX + pack[count + 1, :count].astype(jnp.float32)).astype(jnp.int32)
        for pack in packs[1:]
    ]
    places = jnp.concatenate([positions] + places)
    index = jnp.concatenate(
        [(me ^ part) * count + jnp.arange(count, dtype=jnp.int32) for part in range(blocks)]
    )
    low = jnp.maximum(index - places, index - (W - 1))[None, :]
    cosine, sine = rotation_tables(places)
    grad_came = spread(grad_packed)
    first, second = attention(at, packs, dpacks, low, cosine, sine, heads, group)
    first, second, grad_came, input_packed = barrier((first, second, grad_came, input_packed))

    input_came = spread(input_packed)
    grads = joined(grad_own, grad_came)
    edge = wide + narrow
    def summed(term):
        return lax.psum_scatter(term, "dp", scatter_dimension=0, tiled=True)

    parts = []
    term = weight_terms(at, [grads], [first], [(0, 0, 0, wide)], blocks, replicas, LOAD1)
    parts.append(summed(term))
    term, input_came, first, second = barrier((term, input_came, first, second))

    firsts = [first, swap(first, "context", 1), None, None]
    seconds = [second, None, swap(second, "context", 2), None]
    ins = joined(input_own, input_came)
    ins, parts[0] = barrier((ins, parts[0]))
    jobs = [(0, 0, wide, edge), (0, 1, 0, edge)]
    term = weight_terms(at, [ins], [first, second], jobs, blocks, replicas, LOAD2)
    parts.append(summed(term))
    term, firsts[1], seconds[2], first, second = barrier(
        (term, firsts[1], seconds[2], first, second)
    )
    seconds[1] = swap(second, "context", 1)
    firsts[2] = swap(first, "context", 2)
    jobs = [(0, 0, 0, wide), (1, 0, wide, edge), (1, 1, 0, edge)]

    def terms_of(source_first, source_second):
        lins = [firsts[source_first], seconds[source_second]]
        return weight_terms(at, [grads, ins], lins, jobs, blocks, replicas)

    term = terms_of(1, 2)
    parts.append(summed(term))
    term, firsts[1], firsts[2], seconds[1], seconds[2] = barrier(
        (term, firsts[1], firsts[2], seconds[1], seconds[2])
    )
    firsts[3] = swap(firsts[1], "context", 2)
    seconds[3] = swap(seconds[2], "context", 1)
    term = terms_of(2, 1)
    parts.append(summed(term))
    late, term = barrier((at, term))
    partial = input_first(
        late, firsts[:3], seconds[:3], w_query, w_key, w_value, count, wide, narrow
    )
    term, partial, parts[1], firsts[3], seconds[3] = barrier(
        (term, partial, parts[1], firsts[3], seconds[3])
    )
    mine, sent = input_last(
        at, 3, firsts[3], seconds[3], partial, w_query, w_key, w_value, wide, narrow
    )
    came = swap(sent, "tensor", 1)
    mine, firsts[3] = barrier((mine, firsts[3]))
    term = terms_of(3, 3)
    parts.append(summed(term))
    mine, came, parts[2], parts[3] = barrier((mine, came, parts[2], parts[3]))
    input_grad = (mine + came.astype(jnp.float32)).astype(jnp.bfloat16)
    last, input_grad = barrier((at, input_grad))

    def rest(source_first, source_second):
        return [(1, source_first, narrow), (2, source_second, wide), (3, source_second, narrow)]

    layout = [[(0, 0, wide)], rest(0, 0)]
    for source_first, source_second in ((1, 2), (2, 1), (3, 3)):
        layout.append([(0, source_first, wide)] + rest(source_first, source_second))
    near = assemble(last, layout[:-1], parts[:-1], blocks, wide, narrow)
    grad_output, grad_value, grad_query, grad_key = assemble_last(at, layout[-1], parts[-1], near)
    return (input_grad, grad_query, grad_key, grad_value, grad_output)


def solution(mesh):
    return jax.shard_map(
        on_device,
        mesh=mesh,
        in_specs=(
            P(("dp", "context"), None),
            P(("dp", "context"), "tensor"),
            P(("dp", "context"), "tensor"),
            P(("dp", "context"), "tensor"),
            P(("dp", "context"), None),
            P(("dp", "context")),
            P(None, "tensor"),
            P(None, "tensor"),
            P(None, "tensor"),
            P(None, "tensor"),
        ),
        out_specs=(
            P(("dp", "context", "tensor"), None),
            P(("dp", "context"), "tensor"),
            P(("dp", "context"), "tensor"),
            P(("dp", "context"), "tensor"),
            P(("dp", "context"), "tensor"),
        ),
        check_vma=False,
    )
```

```python
import functools

import jax
import jax.numpy as jnp
from jax import lax
from jax.experimental import pallas as pl
from jax.experimental.pallas import tpu as pltpu
from jax.sharding import PartitionSpec as P

HD = 128
W = 1024
QSCALAR = 168


def shifted(x, axis, by):
    count = lax.axis_size(axis)
    pairs = [(i, i + by) for i in range(count) if 0 <= i + by < count]
    return lax.ppermute(x, axis, pairs)


def rotate_back(grads, places):
    count = grads.shape[0]
    half = HD // 2
    index = jnp.arange(half, dtype=jnp.float32)
    freq = jnp.power(jnp.float32(10000.0), index * (-2.0 / HD))
    angle = places.astype(jnp.float32)[:, None] * freq[None, :]
    cosine = jnp.cos(angle)[:, None, :]
    sine = jnp.sin(angle)[:, None, :]
    split = grads.reshape(count, -1, 2, half)
    first = split[:, :, 0, :]
    second = split[:, :, 1, :]
    upper = first * cosine + second * sine
    lower = second * cosine - first * sine
    return jnp.stack([upper, lower], axis=2).reshape(count, -1)


def contract_rows(left, right):
    return lax.dot_general(
        left, right, (((0,), (0,)), ((), ())), preferred_element_type=jnp.float32
    )


def contract_cols(left, right):
    return lax.dot_general(
        left, right, (((1,), (1,)), ((), ())), preferred_element_type=jnp.float32
    )


def banded(
    inputs,
    queries,
    key_states,
    value_states,
    out_grad,
    positions,
    w_query,
    w_key,
    w_value,
    w_output,
):
    count = queries.shape[0]
    head_cols = queries.shape[1]
    kv_cols = key_states.shape[1]
    kv_here = kv_cols // HD
    group = head_cols // kv_cols
    scale = QSCALAR ** (-0.5)
    block = lax.axis_index("context")
    blocks = lax.axis_size("context")
    reach = min((W + count - 2) // count, blocks - 1)
    span = (reach + 1) * count
    key_pieces = []
    value_pieces = []
    for back in range(reach, 0, -1):
        earlier_keys, earlier_values = shifted((key_states, value_states), "context", back)
        key_pieces.append(earlier_keys)
        value_pieces.append(earlier_values)
    band_keys = jnp.concatenate(key_pieces + [key_states], axis=0)
    band_values = jnp.concatenate(value_pieces + [value_states], axis=0)
    query_index = block * count + jnp.arange(count, dtype=jnp.int32)
    key_index = (block - reach) * count + jnp.arange(span, dtype=jnp.int32)
    doc_start = query_index - positions
    allowed = (key_index[None, :] <= query_index[:, None]) & (
        query_index[:, None] - key_index[None, :] < W
    )
    allowed = allowed & (key_index[None, :] >= doc_start[:, None]) & (key_index[None, :] >= 0)
    query_heads = queries.reshape(count, kv_here, group, HD)
    key_heads = band_keys.reshape(span, kv_here, HD)
    value_heads = band_values.reshape(span, kv_here, HD)
    scores = (
        jnp.einsum("qhgd,khd->hgqk", query_heads, key_heads, preferred_element_type=jnp.float32)
        * scale
    )
    scores = jnp.where(allowed, scores, -1e30)
    top = jnp.max(scores, axis=-1, keepdims=True)
    weights = jnp.exp(scores - top)
    probs = weights / jnp.sum(weights, axis=-1, keepdims=True)
    probs_half = probs.astype(jnp.bfloat16)
    attn = jnp.einsum(
        "hgqk,khd->qhgd", probs_half, value_heads, preferred_element_type=jnp.float32
    ).astype(jnp.bfloat16)
    attn_flat = attn.reshape(count, head_cols)
    dattn = jnp.dot(out_grad, w_output, preferred_element_type=jnp.float32).astype(jnp.bfloat16)
    dattn_heads = dattn.reshape(count, kv_here, group, HD)
    dprobs = jnp.einsum(
        "qhgd,khd->hgqk", dattn_heads, value_heads, preferred_element_type=jnp.float32
    )
    delta = jnp.sum(dattn_heads.astype(jnp.float32) * attn.astype(jnp.float32), axis=-1)
    delta = jnp.transpose(delta, (1, 2, 0))[..., None]
    dscores = (probs * (dprobs - delta) * scale).astype(jnp.bfloat16)
    query_grad = jnp.einsum(
        "hgqk,khd->qhgd", dscores, key_heads, preferred_element_type=jnp.float32
    ).reshape(count, head_cols)
    band_key_grad = jnp.einsum(
        "hgqk,qhgd->khd", dscores, query_heads, preferred_element_type=jnp.float32
    ).reshape(span, kv_cols)
    band_value_grad = jnp.einsum(
        "hgqk,qhgd->khd", probs_half, dattn_heads, preferred_element_type=jnp.float32
    ).reshape(span, kv_cols)
    key_grad = band_key_grad[reach * count :]
    value_grad = band_value_grad[reach * count :]
    for back in range(1, reach + 1):
        first_row = (reach - back) * count
        sent_keys, sent_values = shifted(
            (
                band_key_grad[first_row : first_row + count],
                band_value_grad[first_row : first_row + count],
            ),
            "context",
            -back,
        )
        key_grad = key_grad + sent_keys
        value_grad = value_grad + sent_values
    query_lin = rotate_back(query_grad, positions).astype(jnp.bfloat16)
    key_lin = rotate_back(key_grad, positions).astype(jnp.bfloat16)
    value_half = value_grad.astype(jnp.bfloat16)
    total = contract_cols(query_lin, w_query)
    total = total + contract_cols(key_lin, w_key)
    total = total + contract_cols(value_half, w_value)
    input_grad = lax.psum_scatter(total, "tensor", scatter_dimension=0, tiled=True).astype(
        jnp.bfloat16
    )
    terms = (
        contract_rows(inputs, query_lin),
        contract_rows(inputs, key_lin),
        contract_rows(inputs, value_half),
        contract_rows(out_grad, attn_flat),
    )
    summed = (
        lax.psum_scatter(
            terms[0].astype(jnp.bfloat16), ("dp", "context"), scatter_dimension=0, tiled=True
        ).astype(jnp.float32),
        lax.psum_scatter(
            terms[1].astype(jnp.bfloat16), ("dp", "context"), scatter_dimension=0, tiled=True
        ).astype(jnp.float32),
        lax.psum_scatter(
            terms[2].astype(jnp.bfloat16), ("dp", "context"), scatter_dimension=0, tiled=True
        ).astype(jnp.float32),
        lax.psum_scatter(
            terms[3].astype(jnp.bfloat16), ("dp", "context"), scatter_dimension=0, tiled=True
        ).astype(jnp.float32),
    )
    return (input_grad, summed[0], summed[1], summed[2], summed[3])


TILE = 256
EXTRA = 16
RADIX_BITS = 7
RADIX = 1 << RADIX_BITS
NEGATIVE = -1e30
LOG2E = 1.4426950408889634
VMEM_LIMIT = 48 * 1024 * 1024
LOAD = 40
LOAD1 = 12
LOAD2 = 12
COST = 80
VMEM_MOST = 60 * 1024 * 1024


def dot_nt(left, right):
    return lax.dot_general(
        left, right, (((1,), (1,)), ((), ())), preferred_element_type=jnp.float32
    )


def dot_nn(left, right):
    return lax.dot_general(
        left, right, (((1,), (0,)), ((), ())), preferred_element_type=jnp.float32
    )


def whole():
    return pl.BlockSpec(memory_space=pltpu.VMEM)


def scalars():
    return pl.BlockSpec(memory_space=pltpu.SMEM)


def params(limit=VMEM_LIMIT):
    return pltpu.CompilerParams(vmem_limit_bytes=limit)


def aligned(index, size):
    return pl.ds(pl.multiple_of(index * size, size), size)


def pack_heads_kernel(blocks, wide, narrow, at_ref, q_ref, k_ref, v_ref, places_ref, *outs):
    me = at_ref[0]
    count = q_ref.shape[0]
    places = jnp.broadcast_to(places_ref[...], (EXTRA, count))
    row = lax.broadcasted_iota(jnp.int32, (EXTRA, count), 0)
    digits = jnp.where(row == 0, places >> RADIX_BITS, jnp.where(row == 1, places & (RADIX - 1), 0))
    digits = digits.astype(jnp.float32).astype(jnp.bfloat16)
    for part in range(blocks):
        there = me ^ part
        out = outs[part]
        out[:count, :wide] = q_ref[:, aligned(there, wide)]
        out[:count, wide : wide + narrow] = k_ref[:, aligned(there, narrow)]
        out[:count, wide + narrow :] = v_ref[:, aligned(there, narrow)]
        out[count:, :count] = digits
        if out.shape[1] > count:
            out[count:, count:] = jnp.zeros((EXTRA, out.shape[1] - count), out.dtype)


def pack_heads(at, queries, key_states, value_states, places, blocks, wide, narrow):
    count = queries.shape[0]
    shape = jax.ShapeDtypeStruct((count + EXTRA, wide + 2 * narrow), queries.dtype)
    return pl.pallas_call(
        functools.partial(pack_heads_kernel, blocks, wide, narrow),
        out_shape=(shape,) * blocks,
        in_specs=[scalars()] + [pl.BlockSpec(x.shape, lambda: (0, 0)) for x in (queries, key_states, value_states, places)],
        out_specs=(whole(),) * blocks,
        compiler_params=params(VMEM_MOST),
        cost_estimate=pl.CostEstimate(
            flops=0, bytes_accessed=4 * blocks * count * (wide + 2 * narrow), transcendentals=0
        ),
        name="pack_heads",
    )(at, queries, key_states, value_states, places)


def pack_rows_kernel(blocks, replicas, rows, at_ref, x_ref, own_ref, *rest):
    outs, turned = rest[:-1], rest[-1]
    me, side = at_ref[0], at_ref[1]
    count, width = x_ref.shape
    half = count // 2

    step = next(n for n in (6, 3, 2, 1) if width % (n * HD) == 0) * HD

    def turn(index, carry):
        cols = aligned(index, step)
        turned[cols, :] = x_ref[:, cols].T
        return carry

    lax.fori_loop(0, width // step, turn, 0)
    for replica in range(replicas):
        into = pl.ds(replica * rows, rows)
        own_ref[into, :] = turned[aligned(replica * blocks + me, rows), :]
        for part in range(1, blocks):
            taken = aligned(replica * blocks + (me ^ part), rows)
            outs[part - 1][into, :] = turned[taken, aligned(side, half)]


def pack_rows(at, x, blocks, replicas):
    count, width = x.shape
    rows = width // (replicas * blocks)
    share = replicas * rows
    own = jax.ShapeDtypeStruct((share, count), x.dtype)
    sent = jax.ShapeDtypeStruct((share, count // 2), x.dtype)
    return pl.pallas_call(
        functools.partial(pack_rows_kernel, blocks, replicas, rows),
        out_shape=(own,) + (sent,) * (blocks - 1),
        in_specs=[scalars(), whole()],
        out_specs=(whole(),) * blocks,
        scratch_shapes=[pltpu.VMEM((width, count), x.dtype)],
        compiler_params=params(),
        cost_estimate=pl.CostEstimate(
            flops=0, bytes_accessed=6 * count * width, transcendentals=0
        ),
        name="pack_rows",
    )(at, x)


def attention_kernel(blocks, count, heads, group, *refs):
    at_ref = refs[0]
    packs = refs[1 : 1 + blocks]
    dpacks = refs[1 + blocks : 1 + 2 * blocks]
    low_ref, cos_ref, sin_ref = refs[1 + 2 * blocks : 4 + 2 * blocks]
    first_ref, second_ref = refs[4 + 2 * blocks : 6 + 2 * blocks]
    q_s, k_s, v_s, kt_s, vt_s, d_s, dt_s, dk_s, dv_s = refs[6 + 2 * blocks :]
    scale = QSCALAR ** (-0.5)
    factor = scale * LOG2E
    span = blocks * count
    wide = heads * group * HD
    narrow = heads * HD
    per_block = count // TILE
    reach = -(-(W - 1) // TILE)
    me = at_ref[0]
    for part in range(blocks):
        rows = aligned(me ^ part, count)
        pack = packs[part]
        q_s[rows, :] = pack[:count, :wide]
        keys = pack[:count, wide : wide + narrow]
        values = pack[:count, wide + narrow :]
        k_s[rows, :] = keys
        v_s[rows, :] = values
        kt_s[:, rows] = keys.T
        vt_s[:, rows] = values.T
        d_s[rows, :] = dpacks[part][...]
        dt_s[:, rows] = dpacks[part][...].T
    dk_s[...] = jnp.zeros_like(dk_s)
    dv_s[...] = jnp.zeros_like(dv_s)

    def stored(index):
        return aligned(((index // per_block) ^ me) * per_block + lax.rem(index, per_block), TILE)

    def rotated(grad, rows):
        return grad * cos_ref[rows, :] + pltpu.roll(grad, HD // 2, 1) * sin_ref[rows, :]

    for head in range(heads):
        kv = slice(head * HD, (head + 1) * HD)

        def tile(index, first_key, width):
            index = jnp.int32(index)
            q_rows = aligned(index, TILE)
            t_rows = stored(index)
            k_rows = pl.ds(first_key, width)
            columns = [slice(head * group * HD + g * HD, head * group * HD + (g + 1) * HD) for g in range(group)]
            query = jnp.concatenate([q_s[q_rows, c] for c in columns], axis=0)
            dattn = jnp.concatenate([d_s[q_rows, c] for c in columns], axis=0)
            dattn_t = jnp.concatenate([dt_s[c, q_rows] for c in columns], axis=1)
            scores = dot_nt(k_s[k_rows, kv], query)
            low = jnp.concatenate([low_ref[:, t_rows]] * group, axis=1)
            at = first_key + lax.broadcasted_iota(jnp.int32, (width, group * TILE), 0)
            own = index * TILE + lax.rem(
                lax.broadcasted_iota(jnp.int32, (1, group * TILE), 1), jnp.int32(TILE)
            )
            scores = jnp.where((at >= low) & (at <= own), scores, NEGATIVE)
            top = jnp.max(scores, axis=0, keepdims=True)
            weights = jnp.exp2(scores * factor - top * factor)
            inverse = 1.0 / jnp.sum(weights, axis=0, keepdims=True)
            probs = weights * inverse
            half = probs.astype(jnp.bfloat16)
            attn = dot_nn(vt_s[kv, k_rows], half).astype(jnp.bfloat16)
            dprobs = dot_nt(v_s[k_rows, kv], dattn)
            attn_wide = attn.astype(jnp.float32)
            delta = jnp.sum(dattn_t.astype(jnp.float32) * attn_wide, axis=0, keepdims=True)
            dscores = (probs * (dprobs - delta)).astype(jnp.bfloat16)
            query_grad = (dot_nn(kt_s[kv, k_rows], dscores) * scale).T
            attn_rows = attn_wide.T
            dk_s[k_rows, kv] += dot_nn(dscores, query)
            dv_s[k_rows, kv] += dot_nn(half, dattn)
            for g, c in enumerate(columns):
                part = slice(g * TILE, (g + 1) * TILE)
                first_ref[q_rows, c] = attn_rows[part].astype(jnp.bfloat16)
                second_ref[q_rows, c] = rotated(query_grad[part], t_rows).astype(jnp.bfloat16)

        tiles = span // TILE
        for index in range(min(reach, tiles)):
            tile(index, 0, (index + 1) * TILE)

        def steady(index, carry):
            tile(index, pl.multiple_of((index - reach) * TILE, TILE), (reach + 1) * TILE)
            return carry

        if tiles > reach:
            lax.fori_loop(reach, tiles, steady, 0)
        out = slice(wide + head * HD, wide + (head + 1) * HD)
        for index in range(tiles):
            rows = pl.ds(index * TILE, TILE)
            first_ref[rows, out] = dv_s[rows, kv].astype(jnp.bfloat16)
            second_ref[rows, out] = rotated(
                dk_s[rows, kv] * scale, stored(jnp.int32(index))
            ).astype(jnp.bfloat16)


def attention(at, packs, dpacks, low, cosine, sine, heads, group):
    blocks = len(packs)
    count = dpacks[0].shape[0]
    span = blocks * count
    wide = heads * group * HD
    narrow = heads * HD
    half = jnp.bfloat16
    pairs = heads * group * span * (W + TILE)
    return pl.pallas_call(
        functools.partial(attention_kernel, blocks, count, heads, group),
        out_shape=(jax.ShapeDtypeStruct((span, wide + narrow), half),) * 2,
        in_specs=[scalars()] + [whole()] * (2 * blocks + 3),
        out_specs=(whole(),) * 2,
        scratch_shapes=[
            pltpu.VMEM((span, wide), half),
            pltpu.VMEM((span, narrow), half),
            pltpu.VMEM((span, narrow), half),
            pltpu.VMEM((narrow, span), half),
            pltpu.VMEM((narrow, span), half),
            pltpu.VMEM((span, wide), half),
            pltpu.VMEM((wide, span), half),
            pltpu.VMEM((span, narrow), jnp.float32),
            pltpu.VMEM((span, narrow), jnp.float32),
        ],
        compiler_params=params(),
        cost_estimate=pl.CostEstimate(
            flops=10 * pairs * HD, bytes_accessed=span * wide * 12, transcendentals=pairs
        ),
        name="attention_backward",
    )(at, *packs, *dpacks, low, cosine, sine)


def weight_terms_kernel(blocks, jobs, at_ref, *refs):
    pieces = 1 + 2 * (blocks - 1)
    sets = 1 + max(job[0] for job in jobs)
    piece_refs = refs[: sets * pieces]
    lin_refs = refs[sets * pieces : -1]
    out_ref = refs[-1]
    me, side = at_ref[0], at_ref[1]
    count = piece_refs[0].shape[1]
    half = count // 2
    rows = [aligned(me, count)]
    for part in range(1, blocks):
        rows.append(aligned((me ^ part) * 2 + side, half))
        rows.append(aligned((me ^ part) * 2 + 1 - side, half))
    total = [None] * len(jobs)
    for piece in range(pieces):
        for index, (which, lin, low, high) in enumerate(jobs):
            left = piece_refs[which * pieces + piece][...]
            term = dot_nn(left, lin_refs[lin][rows[piece], low:high])
            total[index] = term if total[index] is None else total[index] + term
    first = 0
    for index, (which, lin, low, high) in enumerate(jobs):
        out_ref[:, first : first + high - low] = total[index].astype(out_ref.dtype)
        first += high - low


def weight_terms(at, sets, lins, jobs, blocks, replicas, load=LOAD):
    share = sets[0][0].shape[0]
    rows = share // replicas
    span = lins[0].shape[0]
    cols = sum(job[3] - job[2] for job in jobs)
    pieces = [x for one in sets for x in one]

    def piece(x):
        return pl.BlockSpec((rows, x.shape[1]), lambda i, at: (i, 0))

    def fixed(x):
        return pl.BlockSpec(x.shape, lambda i, at: (0, 0))

    return pl.pallas_call(
        functools.partial(weight_terms_kernel, blocks, jobs),
        out_shape=jax.ShapeDtypeStruct((share, cols), lins[0].dtype),
        grid_spec=pltpu.PrefetchScalarGridSpec(
            num_scalar_prefetch=1,
            grid=(replicas,),
            in_specs=[piece(x) for x in pieces] + [fixed(x) for x in lins],
            out_specs=pl.BlockSpec((rows, cols), lambda i, at: (i, 0)),
        ),
        compiler_params=params(VMEM_MOST),
        cost_estimate=pl.CostEstimate(
            flops=load * share * span * cols,
            bytes_accessed=2 * share * span * len(sets) + 2 * (span + share) * cols,
            transcendentals=0,
        ),
        name="weight_terms",
    )(at, *pieces, *lins)


def assemble_kernel(places, at_ref, *refs):
    parts, outs = refs[:-4], refs[-4:]
    me = at_ref[0]
    for part, one in zip(parts, places):
        first = 0
        for out, source, cols in one:
            outs[out][:, aligned(me ^ source, cols)] = part[:, first : first + cols].astype(
                jnp.float32
            )
            first += cols


def assemble(at, places, parts, blocks, wide, narrow):
    rows = parts[0].shape[0]
    shapes = [
        jax.ShapeDtypeStruct((rows, blocks * cols), jnp.float32)
        for cols in (wide, narrow, wide, narrow)
    ]
    return pl.pallas_call(
        functools.partial(assemble_kernel, places),
        out_shape=tuple(shapes),
        in_specs=[scalars()] + [whole()] * len(parts),
        out_specs=(whole(),) * 4,
        compiler_params=params(),
        name="assemble",
    )(at, *parts)


def assemble_last_kernel(places, at_ref, part_ref, *refs):
    outs, wide_s, sems = refs[4:8], refs[8], refs[9]
    me = at_ref[0]
    wide_s[...] = part_ref[...].astype(jnp.float32)
    copies = []
    first = 0
    for index, (out, source, cols) in enumerate(places):
        copies.append(
            pltpu.make_async_copy(
                wide_s.at[:, first : first + cols],
                outs[out].at[:, aligned(me ^ source, cols)],
                sems.at[index],
            )
        )
        copies[-1].start()
        first += cols
    for copy in copies:
        copy.wait()


def assemble_last(at, places, part, grads):
    anywhere = pl.BlockSpec(memory_space=pl.ANY)
    return pl.pallas_call(
        functools.partial(assemble_last_kernel, places),
        out_shape=tuple(jax.ShapeDtypeStruct(x.shape, x.dtype) for x in grads),
        in_specs=[scalars(), pl.BlockSpec(part.shape, lambda: (0, 0))] + [anywhere] * 4,
        out_specs=(anywhere,) * 4,
        scratch_shapes=[
            pltpu.VMEM(part.shape, jnp.float32),
            pltpu.SemaphoreType.DMA((len(places),)),
        ],
        input_output_aliases={2: 0, 3: 1, 4: 2, 5: 3},
        compiler_params=params(VMEM_MOST),
        name="assemble_last",
    )(at, part, *grads)


def input_first_kernel(blocks, wide, narrow, at_ref, *refs):
    firsts, seconds = refs[: blocks - 1], refs[blocks - 1 : 2 * (blocks - 1)]
    wq_ref, wk_ref, wv_ref, out_ref, q_s, k_s, v_s = refs[2 * (blocks - 1) :]
    me = at_ref[0]

    @pl.when(pl.program_id(0) == 0)
    def _():
        q_s[...] = jnp.zeros_like(q_s)
        k_s[...] = jnp.zeros_like(k_s)
        v_s[...] = jnp.zeros_like(v_s)
        for part in range(blocks - 1):
            there = me ^ part
            q_s[:, aligned(there, wide)] = seconds[part][:, :wide]
            k_s[:, aligned(there, narrow)] = seconds[part][:, wide:]
            v_s[:, aligned(there, narrow)] = firsts[part][:, wide:]

    total = dot_nt(q_s[...], wq_ref[...])
    total = total + dot_nt(k_s[...], wk_ref[...])
    out_ref[...] = total + dot_nt(v_s[...], wv_ref[...])


def input_last_kernel(wide, at_ref, first_ref, second_ref, wq_ref, wk_ref, wv_ref, part_ref, mine_ref, sent_ref, total_s):
    side = at_ref[1]
    half = first_ref.shape[0] // 2
    total = part_ref[...] + dot_nt(second_ref[:, :wide], wq_ref[...])
    total = total + dot_nt(second_ref[:, wide:], wk_ref[...])
    total_s[...] = total + dot_nt(first_ref[:, wide:], wv_ref[...])
    for target, which in ((sent_ref, 1 - side), (mine_ref, side)):
        target[...] = total_s[aligned(which, half), :].astype(target.dtype)


def columns_step(width):
    return next(s for s in (768, 512, 256, 128, width) if width % s == 0)


def input_first(at, firsts, seconds, w_query, w_key, w_value, count, wide, narrow):
    blocks = len(firsts) + 1
    width = w_query.shape[0]
    step = columns_step(width)
    ins = firsts + seconds
    half = jnp.bfloat16
    return pl.pallas_call(
        functools.partial(input_first_kernel, blocks, wide, narrow),
        out_shape=jax.ShapeDtypeStruct((count, width), jnp.float32),
        grid_spec=pltpu.PrefetchScalarGridSpec(
            num_scalar_prefetch=1,
            grid=(width // step,),
            in_specs=[pl.BlockSpec((count, x.shape[1]), lambda i, at: (at[0], 0)) for x in ins]
            + [
                pl.BlockSpec((step, x.shape[1]), lambda i, at: (i, 0))
                for x in (w_query, w_key, w_value)
            ],
            out_specs=pl.BlockSpec((count, step), lambda i, at: (0, i)),
            scratch_shapes=[
                pltpu.VMEM((count, blocks * wide), half),
                pltpu.VMEM((count, blocks * narrow), half),
                pltpu.VMEM((count, blocks * narrow), half),
            ],
        ),
        compiler_params=params(VMEM_MOST),
        cost_estimate=pl.CostEstimate(
            flops=count * width * blocks * (wide + 2 * narrow), bytes_accessed=0, transcendentals=0
        ),
        name="input_first",
    )(at, *ins, w_query, w_key, w_value)


def input_last(at, far, first, second, partial, w_query, w_key, w_value, wide, narrow):
    count, width = partial.shape
    step = columns_step(width)

    def own(x):
        return pl.BlockSpec((count, x.shape[1]), lambda i, at: (at[0], 0))

    def weight(cols):
        return pl.BlockSpec((step, cols), lambda i, at: (i, at[0] ^ far))

    out = pl.BlockSpec((count // 2, step), lambda i, at: (0, i))
    return pl.pallas_call(
        functools.partial(input_last_kernel, wide),
        out_shape=(
            jax.ShapeDtypeStruct((count // 2, width), jnp.float32),
            jax.ShapeDtypeStruct((count // 2, width), jnp.bfloat16),
        ),
        grid_spec=pltpu.PrefetchScalarGridSpec(
            num_scalar_prefetch=1,
            grid=(width // step,),
            in_specs=[own(first), own(second), weight(wide), weight(narrow), weight(narrow)]
            + [pl.BlockSpec((count, step), lambda i, at: (0, i))],
            out_specs=(out, out),
            scratch_shapes=[pltpu.VMEM((count, step), jnp.float32)],
        ),
        compiler_params=params(VMEM_MOST),
        cost_estimate=pl.CostEstimate(
            flops=COST * count * width * (wide + 2 * narrow), bytes_accessed=0, transcendentals=0
        ),
        name="input_last",
    )(at, first, second, w_query, w_key, w_value, partial)


def swap(x, axis, by):
    count = lax.axis_size(axis)
    return lax.ppermute(x, axis, [(i, i ^ by) for i in range(count)])


def rotation_tables(places):
    half = HD // 2
    index = jnp.arange(half, dtype=jnp.float32)
    freq = jnp.power(jnp.float32(10000.0), index * (-2.0 / HD))
    angle = places.astype(jnp.float32)[:, None] * freq[None, :]
    cosine = jnp.cos(angle)
    sine = jnp.sin(angle)
    return jnp.concatenate([cosine, cosine], axis=1), jnp.concatenate([sine, -sine], axis=1)


def on_device(
    inputs,
    queries,
    key_states,
    value_states,
    out_grad,
    positions,
    w_query,
    w_key,
    w_value,
    w_output,
):
    count = queries.shape[0]
    head_cols = queries.shape[1]
    kv_cols = key_states.shape[1]
    kv_here = kv_cols // HD
    group = head_cols // kv_cols
    blocks = lax.axis_size("context")
    replicas = lax.axis_size("dp")
    cores = lax.axis_size("tensor")
    width = inputs.shape[1]
    heads = kv_here // blocks
    wide = heads * group * HD
    narrow = heads * HD
    fits = (
        blocks == 4
        and kv_here % blocks == 0
        and cores == 2
        and count % (2 * HD) == 0
        and count % TILE == 0
        and W % TILE == 0
        and width % HD == 0
        and width % (replicas * blocks * EXTRA) == 0
        and wide + 2 * narrow >= count
    )
    if not fits:
        return banded(
            inputs, queries, key_states, value_states, out_grad, positions,
            w_query, w_key, w_value, w_output,
        )
    me = lax.axis_index("context")
    side = lax.axis_index("tensor")
    at = jnp.stack([me, side]).astype(jnp.int32)

    barrier = lax.optimization_barrier

    packs = list(
        pack_heads(at, queries, key_states, value_states, positions[None, :], blocks, wide, narrow)
    )
    after, packs = barrier((out_grad, packs))
    for part in range(1, blocks):
        packs[part] = swap(packs[part], "context", part)
    dattn = jnp.dot(after, w_output, preferred_element_type=jnp.float32).astype(jnp.bfloat16)
    dpacks = [
        lax.dynamic_slice(dattn, (0, (me ^ part) * wide), (count, wide)) for part in range(blocks)
    ]
    def spread(packed):
        return [swap(x, "context", part + 1) for part, x in enumerate(packed)]

    def joined(own, came):
        pieces = [own]
        for x in came:
            pieces += [x, swap(x, "tensor", 1)]
        return pieces

    soon, dpacks = barrier((at, dpacks))
    grad_own, *grad_packed = pack_rows(soon, out_grad, blocks, replicas)
    soon, grad_packed = barrier((soon, grad_packed))
    input_own, *input_packed = pack_rows(soon, inputs, blocks, replicas)
    packs, dpacks, grad_packed, input_packed = barrier((packs, dpacks, grad_packed, input_packed))
    dpacks = [dpacks[0]] + spread(dpacks[1:])
    places = [
        (pack[count, :count].astype(jnp.float32) * RADIX + pack[count + 1, :count].astype(jnp.float32)).astype(jnp.int32)
        for pack in packs[1:]
    ]
    places = jnp.concatenate([positions] + places)
    index = jnp.concatenate(
        [(me ^ part) * count + jnp.arange(count, dtype=jnp.int32) for part in range(blocks)]
    )
    low = jnp.maximum(index - places, index - (W - 1))[None, :]
    cosine, sine = rotation_tables(places)
    grad_came = spread(grad_packed)
    first, second = attention(at, packs, dpacks, low, cosine, sine, heads, group)
    first, second, grad_came, input_packed = barrier((first, second, grad_came, input_packed))

    input_came = spread(input_packed)
    grads = joined(grad_own, grad_came)
    edge = wide + narrow
    def summed(term):
        return lax.psum_scatter(term, "dp", scatter_dimension=0, tiled=True)

    parts = []
    term = weight_terms(at, [grads], [first], [(0, 0, 0, wide)], blocks, replicas, LOAD1)
    parts.append(summed(term))
    term, input_came, first, second = barrier((term, input_came, first, second))

    firsts = [first, swap(first, "context", 1), None, None]
    seconds = [second, None, swap(second, "context", 2), None]
    ins = joined(input_own, input_came)
    ins, parts[0] = barrier((ins, parts[0]))
    jobs = [(0, 0, wide, edge), (0, 1, 0, edge)]
    term = weight_terms(at, [ins], [first, second], jobs, blocks, replicas, LOAD2)
    parts.append(summed(term))
    term, firsts[1], seconds[2], first, second = barrier(
        (term, firsts[1], seconds[2], first, second)
    )
    seconds[1] = swap(second, "context", 1)
    firsts[2] = swap(first, "context", 2)
    jobs = [(0, 0, 0, wide), (1, 0, wide, edge), (1, 1, 0, edge)]

    def terms_of(source_first, source_second):
        lins = [firsts[source_first], seconds[source_second]]
        return weight_terms(at, [grads, ins], lins, jobs, blocks, replicas)

    term = terms_of(1, 2)
    parts.append(summed(term))
    term, firsts[1], firsts[2], seconds[1], seconds[2] = barrier(
        (term, firsts[1], firsts[2], seconds[1], seconds[2])
    )
    firsts[3] = swap(firsts[1], "context", 2)
    seconds[3] = swap(seconds[2], "context", 1)
    term = terms_of(2, 1)
    parts.append(summed(term))
    late, term = barrier((at, term))
    partial = input_first(
        late, firsts[:3], seconds[:3], w_query, w_key, w_value, count, wide, narrow
    )
    term, partial, parts[1], firsts[3], seconds[3] = barrier(
        (term, partial, parts[1], firsts[3], seconds[3])
    )
    mine, sent = input_last(
        at, 3, firsts[3], seconds[3], partial, w_query, w_key, w_value, wide, narrow
    )
    came = swap(sent, "tensor", 1)
    mine, firsts[3] = barrier((mine, firsts[3]))
    term = terms_of(3, 3)
    parts.append(summed(term))
    mine, came, parts[2], parts[3] = barrier((mine, came, parts[2], parts[3]))
    input_grad = (mine + came.astype(jnp.float32)).astype(jnp.bfloat16)
    last, input_grad = barrier((at, input_grad))

    def rest(source_first, source_second):
        return [(1, source_first, narrow), (2, source_second, wide), (3, source_second, narrow)]

    layout = [[(0, 0, wide)], rest(0, 0)]
    for source_first, source_second in ((1, 2), (2, 1), (3, 3)):
        layout.append([(0, source_first, wide)] + rest(source_first, source_second))
    near = assemble(last, layout[:-1], parts[:-1], blocks, wide, narrow)
    grad_output, grad_value, grad_query, grad_key = assemble_last(at, layout[-1], parts[-1], near)
    return (input_grad, grad_query, grad_key, grad_value, grad_output)


def solution(mesh):
    return jax.shard_map(
        on_device,
        mesh=mesh,
        in_specs=(
            P(("dp", "context"), None),
            P(("dp", "context"), "tensor"),
            P(("dp", "context"), "tensor"),
            P(("dp", "context"), "tensor"),
            P(("dp", "context"), None),
            P(("dp", "context")),
            P(None, "tensor"),
            P(None, "tensor"),
            P(None, "tensor"),
            P(None, "tensor"),
        ),
        out_specs=(
            P(("dp", "context", "tensor"), None),
            P(("dp", "context"), "tensor"),
            P(("dp", "context"), "tensor"),
            P(("dp", "context"), "tensor"),
            P(("dp", "context"), "tensor"),
        ),
        check_vma=False,
    )
```

```python
import functools

import jax
import jax.numpy as jnp
from jax import lax
from jax.experimental import pallas as pl
from jax.experimental.pallas import tpu as pltpu
from jax.sharding import PartitionSpec as P

HD = 128
W = 1024
QSCALAR = 168


def shifted(x, axis, by):
    count = lax.axis_size(axis)
    pairs = [(i, i + by) for i in range(count) if 0 <= i + by < count]
    return lax.ppermute(x, axis, pairs)


def rotate_back(grads, places):
    count = grads.shape[0]
    half = HD // 2
    index = jnp.arange(half, dtype=jnp.float32)
    freq = jnp.power(jnp.float32(10000.0), index * (-2.0 / HD))
    angle = places.astype(jnp.float32)[:, None] * freq[None, :]
    cosine = jnp.cos(angle)[:, None, :]
    sine = jnp.sin(angle)[:, None, :]
    split = grads.reshape(count, -1, 2, half)
    first = split[:, :, 0, :]
    second = split[:, :, 1, :]
    upper = first * cosine + second * sine
    lower = second * cosine - first * sine
    return jnp.stack([upper, lower], axis=2).reshape(count, -1)


def contract_rows(left, right):
    return lax.dot_general(
        left, right, (((0,), (0,)), ((), ())), preferred_element_type=jnp.float32
    )


def contract_cols(left, right):
    return lax.dot_general(
        left, right, (((1,), (1,)), ((), ())), preferred_element_type=jnp.float32
    )


def banded(
    inputs,
    queries,
    key_states,
    value_states,
    out_grad,
    positions,
    w_query,
    w_key,
    w_value,
    w_output,
):
    count = queries.shape[0]
    head_cols = queries.shape[1]
    kv_cols = key_states.shape[1]
    kv_here = kv_cols // HD
    group = head_cols // kv_cols
    scale = QSCALAR ** (-0.5)
    block = lax.axis_index("context")
    blocks = lax.axis_size("context")
    reach = min((W + count - 2) // count, blocks - 1)
    span = (reach + 1) * count
    key_pieces = []
    value_pieces = []
    for back in range(reach, 0, -1):
        earlier_keys, earlier_values = shifted((key_states, value_states), "context", back)
        key_pieces.append(earlier_keys)
        value_pieces.append(earlier_values)
    band_keys = jnp.concatenate(key_pieces + [key_states], axis=0)
    band_values = jnp.concatenate(value_pieces + [value_states], axis=0)
    query_index = block * count + jnp.arange(count, dtype=jnp.int32)
    key_index = (block - reach) * count + jnp.arange(span, dtype=jnp.int32)
    doc_start = query_index - positions
    allowed = (key_index[None, :] <= query_index[:, None]) & (
        query_index[:, None] - key_index[None, :] < W
    )
    allowed = allowed & (key_index[None, :] >= doc_start[:, None]) & (key_index[None, :] >= 0)
    query_heads = queries.reshape(count, kv_here, group, HD)
    key_heads = band_keys.reshape(span, kv_here, HD)
    value_heads = band_values.reshape(span, kv_here, HD)
    scores = (
        jnp.einsum("qhgd,khd->hgqk", query_heads, key_heads, preferred_element_type=jnp.float32)
        * scale
    )
    scores = jnp.where(allowed, scores, -1e30)
    top = jnp.max(scores, axis=-1, keepdims=True)
    weights = jnp.exp(scores - top)
    probs = weights / jnp.sum(weights, axis=-1, keepdims=True)
    probs_half = probs.astype(jnp.bfloat16)
    attn = jnp.einsum(
        "hgqk,khd->qhgd", probs_half, value_heads, preferred_element_type=jnp.float32
    ).astype(jnp.bfloat16)
    attn_flat = attn.reshape(count, head_cols)
    dattn = jnp.dot(out_grad, w_output, preferred_element_type=jnp.float32).astype(jnp.bfloat16)
    dattn_heads = dattn.reshape(count, kv_here, group, HD)
    dprobs = jnp.einsum(
        "qhgd,khd->hgqk", dattn_heads, value_heads, preferred_element_type=jnp.float32
    )
    delta = jnp.sum(dattn_heads.astype(jnp.float32) * attn.astype(jnp.float32), axis=-1)
    delta = jnp.transpose(delta, (1, 2, 0))[..., None]
    dscores = (probs * (dprobs - delta) * scale).astype(jnp.bfloat16)
    query_grad = jnp.einsum(
        "hgqk,khd->qhgd", dscores, key_heads, preferred_element_type=jnp.float32
    ).reshape(count, head_cols)
    band_key_grad = jnp.einsum(
        "hgqk,qhgd->khd", dscores, query_heads, preferred_element_type=jnp.float32
    ).reshape(span, kv_cols)
    band_value_grad = jnp.einsum(
        "hgqk,qhgd->khd", probs_half, dattn_heads, preferred_element_type=jnp.float32
    ).reshape(span, kv_cols)
    key_grad = band_key_grad[reach * count :]
    value_grad = band_value_grad[reach * count :]
    for back in range(1, reach + 1):
        first_row = (reach - back) * count
        sent_keys, sent_values = shifted(
            (
                band_key_grad[first_row : first_row + count],
                band_value_grad[first_row : first_row + count],
            ),
            "context",
            -back,
        )
        key_grad = key_grad + sent_keys
        value_grad = value_grad + sent_values
    query_lin = rotate_back(query_grad, positions).astype(jnp.bfloat16)
    key_lin = rotate_back(key_grad, positions).astype(jnp.bfloat16)
    value_half = value_grad.astype(jnp.bfloat16)
    total = contract_cols(query_lin, w_query)
    total = total + contract_cols(key_lin, w_key)
    total = total + contract_cols(value_half, w_value)
    input_grad = lax.psum_scatter(total, "tensor", scatter_dimension=0, tiled=True).astype(
        jnp.bfloat16
    )
    terms = (
        contract_rows(inputs, query_lin),
        contract_rows(inputs, key_lin),
        contract_rows(inputs, value_half),
        contract_rows(out_grad, attn_flat),
    )
    summed = (
        lax.psum_scatter(
            terms[0].astype(jnp.bfloat16), ("dp", "context"), scatter_dimension=0, tiled=True
        ).astype(jnp.float32),
        lax.psum_scatter(
            terms[1].astype(jnp.bfloat16), ("dp", "context"), scatter_dimension=0, tiled=True
        ).astype(jnp.float32),
        lax.psum_scatter(
            terms[2].astype(jnp.bfloat16), ("dp", "context"), scatter_dimension=0, tiled=True
        ).astype(jnp.float32),
        lax.psum_scatter(
            terms[3].astype(jnp.bfloat16), ("dp", "context"), scatter_dimension=0, tiled=True
        ).astype(jnp.float32),
    )
    return (input_grad, summed[0], summed[1], summed[2], summed[3])


TILE = 256
EXTRA = 16
RADIX_BITS = 7
RADIX = 1 << RADIX_BITS
NEGATIVE = -1e30
LOG2E = 1.4426950408889634
VMEM_LIMIT = 48 * 1024 * 1024
LOAD = 40
LOAD1 = 12
LOAD2 = 12
COST = 80
VMEM_MOST = 60 * 1024 * 1024


def dot_nt(left, right):
    return lax.dot_general(
        left, right, (((1,), (1,)), ((), ())), preferred_element_type=jnp.float32
    )


def dot_nn(left, right):
    return lax.dot_general(
        left, right, (((1,), (0,)), ((), ())), preferred_element_type=jnp.float32
    )


def whole():
    return pl.BlockSpec(memory_space=pltpu.VMEM)


def scalars():
    return pl.BlockSpec(memory_space=pltpu.SMEM)


def params(limit=VMEM_LIMIT):
    return pltpu.CompilerParams(vmem_limit_bytes=limit)


def aligned(index, size):
    return pl.ds(pl.multiple_of(index * size, size), size)


def pack_heads_kernel(blocks, wide, narrow, at_ref, q_ref, k_ref, v_ref, places_ref, *outs):
    me = at_ref[0]
    count = q_ref.shape[0]
    places = jnp.broadcast_to(places_ref[...], (EXTRA, count))
    row = lax.broadcasted_iota(jnp.int32, (EXTRA, count), 0)
    digits = jnp.where(row == 0, places >> RADIX_BITS, jnp.where(row == 1, places & (RADIX - 1), 0))
    digits = digits.astype(jnp.float32).astype(jnp.bfloat16)
    for part in range(blocks):
        there = me ^ part
        out = outs[part]
        out[:count, :wide] = q_ref[:, aligned(there, wide)]
        out[:count, wide : wide + narrow] = k_ref[:, aligned(there, narrow)]
        out[:count, wide + narrow :] = v_ref[:, aligned(there, narrow)]
        out[count:, :count] = digits
        if out.shape[1] > count:
            out[count:, count:] = jnp.zeros((EXTRA, out.shape[1] - count), out.dtype)


def pack_heads(at, queries, key_states, value_states, places, blocks, wide, narrow):
    count = queries.shape[0]
    shape = jax.ShapeDtypeStruct((count + EXTRA, wide + 2 * narrow), queries.dtype)
    return pl.pallas_call(
        functools.partial(pack_heads_kernel, blocks, wide, narrow),
        out_shape=(shape,) * blocks,
        in_specs=[scalars()] + [pl.BlockSpec(x.shape, lambda: (0, 0)) for x in (queries, key_states, value_states, places)],
        out_specs=(whole(),) * blocks,
        compiler_params=params(VMEM_MOST),
        cost_estimate=pl.CostEstimate(
            flops=0, bytes_accessed=4 * blocks * count * (wide + 2 * narrow), transcendentals=0
        ),
        name="pack_heads",
    )(at, queries, key_states, value_states, places)


def pack_rows_kernel(blocks, replicas, rows, at_ref, x_ref, own_ref, *rest):
    outs, turned = rest[:-1], rest[-1]
    me, side = at_ref[0], at_ref[1]
    count, width = x_ref.shape
    half = count // 2

    step = next(n for n in (6, 3, 2, 1) if width % (n * HD) == 0) * HD

    def turn(index, carry):
        cols = aligned(index, step)
        turned[cols, :] = x_ref[:, cols].T
        return carry

    lax.fori_loop(0, width // step, turn, 0)
    for replica in range(replicas):
        into = pl.ds(replica * rows, rows)
        own_ref[into, :] = turned[aligned(replica * blocks + me, rows), :]
        for part in range(1, blocks):
            taken = aligned(replica * blocks + (me ^ part), rows)
            outs[part - 1][into, :] = turned[taken, aligned(side, half)]


def pack_rows(at, x, blocks, replicas):
    count, width = x.shape
    rows = width // (replicas * blocks)
    share = replicas * rows
    own = jax.ShapeDtypeStruct((share, count), x.dtype)
    sent = jax.ShapeDtypeStruct((share, count // 2), x.dtype)
    return pl.pallas_call(
        functools.partial(pack_rows_kernel, blocks, replicas, rows),
        out_shape=(own,) + (sent,) * (blocks - 1),
        in_specs=[scalars(), whole()],
        out_specs=(whole(),) * blocks,
        scratch_shapes=[pltpu.VMEM((width, count), x.dtype)],
        compiler_params=params(),
        cost_estimate=pl.CostEstimate(
            flops=0, bytes_accessed=6 * count * width, transcendentals=0
        ),
        name="pack_rows",
    )(at, x)


def attention_kernel(blocks, count, heads, group, *refs):
    at_ref = refs[0]
    packs = refs[1 : 1 + blocks]
    dpacks = refs[1 + blocks : 1 + 2 * blocks]
    low_ref, cos_ref, sin_ref = refs[1 + 2 * blocks : 4 + 2 * blocks]
    first_ref, second_ref = refs[4 + 2 * blocks : 6 + 2 * blocks]
    q_s, k_s, v_s, kt_s, vt_s, d_s, dt_s, dk_s, dv_s = refs[6 + 2 * blocks :]
    scale = QSCALAR ** (-0.5)
    factor = scale * LOG2E
    span = blocks * count
    wide = heads * group * HD
    narrow = heads * HD
    per_block = count // TILE
    reach = -(-(W - 1) // TILE)
    me = at_ref[0]
    for part in range(blocks):
        rows = aligned(me ^ part, count)
        pack = packs[part]
        q_s[rows, :] = pack[:count, :wide]
        keys = pack[:count, wide : wide + narrow]
        values = pack[:count, wide + narrow :]
        k_s[rows, :] = keys
        v_s[rows, :] = values
        kt_s[:, rows] = keys.T
        vt_s[:, rows] = values.T
        d_s[rows, :] = dpacks[part][...]
        dt_s[:, rows] = dpacks[part][...].T
    dk_s[...] = jnp.zeros_like(dk_s)
    dv_s[...] = jnp.zeros_like(dv_s)

    def stored(index):
        return aligned(((index // per_block) ^ me) * per_block + lax.rem(index, per_block), TILE)

    def rotated(grad, rows):
        return grad * cos_ref[rows, :] + pltpu.roll(grad, HD // 2, 1) * sin_ref[rows, :]

    for head in range(heads):
        kv = slice(head * HD, (head + 1) * HD)

        def tile(index, first_key, width):
            index = jnp.int32(index)
            q_rows = aligned(index, TILE)
            t_rows = stored(index)
            k_rows = pl.ds(first_key, width)
            columns = [slice(head * group * HD + g * HD, head * group * HD + (g + 1) * HD) for g in range(group)]
            query = jnp.concatenate([q_s[q_rows, c] for c in columns], axis=0)
            dattn = jnp.concatenate([d_s[q_rows, c] for c in columns], axis=0)
            dattn_t = jnp.concatenate([dt_s[c, q_rows] for c in columns], axis=1)
            scores = dot_nt(k_s[k_rows, kv], query)
            low = jnp.concatenate([low_ref[:, t_rows]] * group, axis=1)
            at = first_key + lax.broadcasted_iota(jnp.int32, (width, group * TILE), 0)
            own = index * TILE + lax.rem(
                lax.broadcasted_iota(jnp.int32, (1, group * TILE), 1), jnp.int32(TILE)
            )
            scores = jnp.where((at >= low) & (at <= own), scores, NEGATIVE)
            top = jnp.max(scores, axis=0, keepdims=True)
            weights = jnp.exp2(scores * factor - top * factor)
            inverse = 1.0 / jnp.sum(weights, axis=0, keepdims=True)
            probs = weights * inverse
            half = probs.astype(jnp.bfloat16)
            attn = dot_nn(vt_s[kv, k_rows], half).astype(jnp.bfloat16)
            dprobs = dot_nt(v_s[k_rows, kv], dattn)
            attn_wide = attn.astype(jnp.float32)
            delta = jnp.sum(dattn_t.astype(jnp.float32) * attn_wide, axis=0, keepdims=True)
            dscores = (probs * (dprobs - delta)).astype(jnp.bfloat16)
            query_grad = (dot_nn(kt_s[kv, k_rows], dscores) * scale).T
            attn_rows = attn_wide.T
            dk_s[k_rows, kv] += dot_nn(dscores, query)
            dv_s[k_rows, kv] += dot_nn(half, dattn)
            for g, c in enumerate(columns):
                part = slice(g * TILE, (g + 1) * TILE)
                first_ref[q_rows, c] = attn_rows[part].astype(jnp.bfloat16)
                second_ref[q_rows, c] = rotated(query_grad[part], t_rows).astype(jnp.bfloat16)

        tiles = span // TILE
        for index in range(min(reach, tiles)):
            tile(index, 0, (index + 1) * TILE)

        def steady(index, carry):
            tile(index, pl.multiple_of((index - reach) * TILE, TILE), (reach + 1) * TILE)
            return carry

        if tiles > reach:
            lax.fori_loop(reach, tiles, steady, 0)
        out = slice(wide + head * HD, wide + (head + 1) * HD)
        for index in range(tiles):
            rows = pl.ds(index * TILE, TILE)
            first_ref[rows, out] = dv_s[rows, kv].astype(jnp.bfloat16)
            second_ref[rows, out] = rotated(
                dk_s[rows, kv] * scale, stored(jnp.int32(index))
            ).astype(jnp.bfloat16)


def attention(at, packs, dpacks, low, cosine, sine, heads, group):
    blocks = len(packs)
    count = dpacks[0].shape[0]
    span = blocks * count
    wide = heads * group * HD
    narrow = heads * HD
    half = jnp.bfloat16
    pairs = heads * group * span * (W + TILE)
    return pl.pallas_call(
        functools.partial(attention_kernel, blocks, count, heads, group),
        out_shape=(jax.ShapeDtypeStruct((span, wide + narrow), half),) * 2,
        in_specs=[scalars()] + [whole()] * (2 * blocks + 3),
        out_specs=(whole(),) * 2,
        scratch_shapes=[
            pltpu.VMEM((span, wide), half),
            pltpu.VMEM((span, narrow), half),
            pltpu.VMEM((span, narrow), half),
            pltpu.VMEM((narrow, span), half),
            pltpu.VMEM((narrow, span), half),
            pltpu.VMEM((span, wide), half),
            pltpu.VMEM((wide, span), half),
            pltpu.VMEM((span, narrow), jnp.float32),
            pltpu.VMEM((span, narrow), jnp.float32),
        ],
        compiler_params=params(),
        cost_estimate=pl.CostEstimate(
            flops=10 * pairs * HD, bytes_accessed=span * wide * 12, transcendentals=pairs
        ),
        name="attention_backward",
    )(at, *packs, *dpacks, low, cosine, sine)


def weight_terms_kernel(blocks, jobs, at_ref, *refs):
    pieces = 1 + 2 * (blocks - 1)
    sets = 1 + max(job[0] for job in jobs)
    piece_refs = refs[: sets * pieces]
    lin_refs = refs[sets * pieces : -1]
    out_ref = refs[-1]
    me, side = at_ref[0], at_ref[1]
    count = piece_refs[0].shape[1]
    half = count // 2
    rows = [aligned(me, count)]
    for part in range(1, blocks):
        rows.append(aligned((me ^ part) * 2 + side, half))
        rows.append(aligned((me ^ part) * 2 + 1 - side, half))
    total = [None] * len(jobs)
    for piece in range(pieces):
        for index, (which, lin, low, high) in enumerate(jobs):
            left = piece_refs[which * pieces + piece][...]
            term = dot_nn(left, lin_refs[lin][rows[piece], low:high])
            total[index] = term if total[index] is None else total[index] + term
    first = 0
    for index, (which, lin, low, high) in enumerate(jobs):
        out_ref[:, first : first + high - low] = total[index].astype(out_ref.dtype)
        first += high - low


def weight_terms(at, sets, lins, jobs, blocks, replicas, load=LOAD):
    share = sets[0][0].shape[0]
    rows = share // replicas
    span = lins[0].shape[0]
    cols = sum(job[3] - job[2] for job in jobs)
    pieces = [x for one in sets for x in one]

    def piece(x):
        return pl.BlockSpec((rows, x.shape[1]), lambda i, at: (i, 0))

    def fixed(x):
        return pl.BlockSpec(x.shape, lambda i, at: (0, 0))

    return pl.pallas_call(
        functools.partial(weight_terms_kernel, blocks, jobs),
        out_shape=jax.ShapeDtypeStruct((share, cols), lins[0].dtype),
        grid_spec=pltpu.PrefetchScalarGridSpec(
            num_scalar_prefetch=1,
            grid=(replicas,),
            in_specs=[piece(x) for x in pieces] + [fixed(x) for x in lins],
            out_specs=pl.BlockSpec((rows, cols), lambda i, at: (i, 0)),
        ),
        compiler_params=params(VMEM_MOST),
        cost_estimate=pl.CostEstimate(
            flops=load * share * span * cols,
            bytes_accessed=2 * share * span * len(sets) + 2 * (span + share) * cols,
            transcendentals=0,
        ),
        name="weight_terms",
    )(at, *pieces, *lins)


def assemble_kernel(places, at_ref, *refs):
    parts, outs = refs[:-4], refs[-4:]
    me = at_ref[0]
    for part, one in zip(parts, places):
        first = 0
        for out, source, cols in one:
            outs[out][:, aligned(me ^ source, cols)] = part[:, first : first + cols].astype(
                jnp.float32
            )
            first += cols


def assemble(at, places, parts, blocks, wide, narrow):
    rows = parts[0].shape[0]
    shapes = [
        jax.ShapeDtypeStruct((rows, blocks * cols), jnp.float32)
        for cols in (wide, narrow, wide, narrow)
    ]
    return pl.pallas_call(
        functools.partial(assemble_kernel, places),
        out_shape=tuple(shapes),
        in_specs=[scalars()] + [whole()] * len(parts),
        out_specs=(whole(),) * 4,
        compiler_params=params(),
        name="assemble",
    )(at, *parts)


def assemble_last_kernel(places, at_ref, part_ref, *refs):
    outs, wide_s, sems = refs[4:8], refs[8], refs[9]
    me = at_ref[0]
    wide_s[...] = part_ref[...].astype(jnp.float32)
    copies = []
    first = 0
    for index, (out, source, cols) in enumerate(places):
        copies.append(
            pltpu.make_async_copy(
                wide_s.at[:, first : first + cols],
                outs[out].at[:, aligned(me ^ source, cols)],
                sems.at[index],
            )
        )
        copies[-1].start()
        first += cols
    for copy in copies:
        copy.wait()


def assemble_last(at, places, part, grads):
    anywhere = pl.BlockSpec(memory_space=pl.ANY)
    return pl.pallas_call(
        functools.partial(assemble_last_kernel, places),
        out_shape=tuple(jax.ShapeDtypeStruct(x.shape, x.dtype) for x in grads),
        in_specs=[scalars(), pl.BlockSpec(part.shape, lambda: (0, 0))] + [anywhere] * 4,
        out_specs=(anywhere,) * 4,
        scratch_shapes=[
            pltpu.VMEM(part.shape, jnp.float32),
            pltpu.SemaphoreType.DMA((len(places),)),
        ],
        input_output_aliases={2: 0, 3: 1, 4: 2, 5: 3},
        compiler_params=params(VMEM_MOST),
        name="assemble_last",
    )(at, part, *grads)


def input_first_kernel(blocks, wide, narrow, at_ref, *refs):
    firsts, seconds = refs[: blocks - 1], refs[blocks - 1 : 2 * (blocks - 1)]
    wq_ref, wk_ref, wv_ref, out_ref, q_s, k_s, v_s = refs[2 * (blocks - 1) :]
    me = at_ref[0]

    @pl.when(pl.program_id(0) == 0)
    def _():
        q_s[...] = jnp.zeros_like(q_s)
        k_s[...] = jnp.zeros_like(k_s)
        v_s[...] = jnp.zeros_like(v_s)
        for part in range(blocks - 1):
            there = me ^ part
            q_s[:, aligned(there, wide)] = seconds[part][:, :wide]
            k_s[:, aligned(there, narrow)] = seconds[part][:, wide:]
            v_s[:, aligned(there, narrow)] = firsts[part][:, wide:]

    total = dot_nt(q_s[...], wq_ref[...])
    total = total + dot_nt(k_s[...], wk_ref[...])
    out_ref[...] = total + dot_nt(v_s[...], wv_ref[...])


def input_last_kernel(wide, at_ref, first_ref, second_ref, wq_ref, wk_ref, wv_ref, part_ref, mine_ref, sent_ref, total_s):
    side = at_ref[1]
    half = first_ref.shape[0] // 2
    total = part_ref[...] + dot_nt(second_ref[:, :wide], wq_ref[...])
    total = total + dot_nt(second_ref[:, wide:], wk_ref[...])
    total_s[...] = total + dot_nt(first_ref[:, wide:], wv_ref[...])
    for target, which in ((sent_ref, 1 - side), (mine_ref, side)):
        target[...] = total_s[aligned(which, half), :].astype(target.dtype)


def columns_step(width):
    return next(s for s in (768, 512, 256, 128, width) if width % s == 0)


def input_first(at, firsts, seconds, w_query, w_key, w_value, count, wide, narrow):
    blocks = len(firsts) + 1
    width = w_query.shape[0]
    step = columns_step(width)
    ins = firsts + seconds
    half = jnp.bfloat16
    return pl.pallas_call(
        functools.partial(input_first_kernel, blocks, wide, narrow),
        out_shape=jax.ShapeDtypeStruct((count, width), jnp.float32),
        grid_spec=pltpu.PrefetchScalarGridSpec(
            num_scalar_prefetch=1,
            grid=(width // step,),
            in_specs=[pl.BlockSpec((count, x.shape[1]), lambda i, at: (at[0], 0)) for x in ins]
            + [
                pl.BlockSpec((step, x.shape[1]), lambda i, at: (i, 0))
                for x in (w_query, w_key, w_value)
            ],
            out_specs=pl.BlockSpec((count, step), lambda i, at: (0, i)),
            scratch_shapes=[
                pltpu.VMEM((count, blocks * wide), half),
                pltpu.VMEM((count, blocks * narrow), half),
                pltpu.VMEM((count, blocks * narrow), half),
            ],
        ),
        compiler_params=params(VMEM_MOST),
        cost_estimate=pl.CostEstimate(
            flops=count * width * blocks * (wide + 2 * narrow), bytes_accessed=0, transcendentals=0
        ),
        name="input_first",
    )(at, *ins, w_query, w_key, w_value)


def input_last(at, far, first, second, partial, w_query, w_key, w_value, wide, narrow):
    count, width = partial.shape
    step = columns_step(width)

    def own(x):
        return pl.BlockSpec((count, x.shape[1]), lambda i, at: (at[0], 0))

    def weight(cols):
        return pl.BlockSpec((step, cols), lambda i, at: (i, at[0] ^ far))

    out = pl.BlockSpec((count // 2, step), lambda i, at: (0, i))
    return pl.pallas_call(
        functools.partial(input_last_kernel, wide),
        out_shape=(
            jax.ShapeDtypeStruct((count // 2, width), jnp.float32),
            jax.ShapeDtypeStruct((count // 2, width), jnp.bfloat16),
        ),
        grid_spec=pltpu.PrefetchScalarGridSpec(
            num_scalar_prefetch=1,
            grid=(width // step,),
            in_specs=[own(first), own(second), weight(wide), weight(narrow), weight(narrow)]
            + [pl.BlockSpec((count, step), lambda i, at: (0, i))],
            out_specs=(out, out),
            scratch_shapes=[pltpu.VMEM((count, step), jnp.float32)],
        ),
        compiler_params=params(VMEM_MOST),
        cost_estimate=pl.CostEstimate(
            flops=COST * count * width * (wide + 2 * narrow), bytes_accessed=0, transcendentals=0
        ),
        name="input_last",
    )(at, first, second, w_query, w_key, w_value, partial)


def swap(x, axis, by):
    count = lax.axis_size(axis)
    return lax.ppermute(x, axis, [(i, i ^ by) for i in range(count)])


def rotation_tables(places):
    half = HD // 2
    index = jnp.arange(half, dtype=jnp.float32)
    freq = jnp.power(jnp.float32(10000.0), index * (-2.0 / HD))
    angle = places.astype(jnp.float32)[:, None] * freq[None, :]
    cosine = jnp.cos(angle)
    sine = jnp.sin(angle)
    return jnp.concatenate([cosine, cosine], axis=1), jnp.concatenate([sine, -sine], axis=1)


def on_device(
    inputs,
    queries,
    key_states,
    value_states,
    out_grad,
    positions,
    w_query,
    w_key,
    w_value,
    w_output,
):
    count = queries.shape[0]
    head_cols = queries.shape[1]
    kv_cols = key_states.shape[1]
    kv_here = kv_cols // HD
    group = head_cols // kv_cols
    blocks = lax.axis_size("context")
    replicas = lax.axis_size("dp")
    cores = lax.axis_size("tensor")
    width = inputs.shape[1]
    heads = kv_here // blocks
    wide = heads * group * HD
    narrow = heads * HD
    fits = (
        blocks == 4
        and kv_here % blocks == 0
        and cores == 2
        and count % (2 * HD) == 0
        and count % TILE == 0
        and W % TILE == 0
        and width % HD == 0
        and width % (replicas * blocks * EXTRA) == 0
        and wide + 2 * narrow >= count
    )
    if not fits:
        return banded(
            inputs, queries, key_states, value_states, out_grad, positions,
            w_query, w_key, w_value, w_output,
        )
    me = lax.axis_index("context")
    side = lax.axis_index("tensor")
    at = jnp.stack([me, side]).astype(jnp.int32)

    barrier = lax.optimization_barrier

    packs = list(
        pack_heads(at, queries, key_states, value_states, positions[None, :], blocks, wide, narrow)
    )
    after, packs = barrier((out_grad, packs))
    for part in range(1, blocks):
        packs[part] = swap(packs[part], "context", part)
    dattn = jnp.dot(after, w_output, preferred_element_type=jnp.float32).astype(jnp.bfloat16)
    dpacks = [
        lax.dynamic_slice(dattn, (0, (me ^ part) * wide), (count, wide)) for part in range(blocks)
    ]
    def spread(packed):
        return [swap(x, "context", part + 1) for part, x in enumerate(packed)]

    def joined(own, came):
        pieces = [own]
        for x in came:
            pieces += [x, swap(x, "tensor", 1)]
        return pieces

    soon, dpacks = barrier((at, dpacks))
    grad_own, *grad_packed = pack_rows(soon, out_grad, blocks, replicas)
    soon, grad_packed = barrier((soon, grad_packed))
    input_own, *input_packed = pack_rows(soon, inputs, blocks, replicas)
    packs, dpacks, grad_packed, input_packed = barrier((packs, dpacks, grad_packed, input_packed))
    dpacks = [dpacks[0]] + spread(dpacks[1:])
    places = [
        (pack[count, :count].astype(jnp.float32) * RADIX + pack[count + 1, :count].astype(jnp.float32)).astype(jnp.int32)
        for pack in packs[1:]
    ]
    places = jnp.concatenate([positions] + places)
    index = jnp.concatenate(
        [(me ^ part) * count + jnp.arange(count, dtype=jnp.int32) for part in range(blocks)]
    )
    low = jnp.maximum(index - places, index - (W - 1))[None, :]
    cosine, sine = rotation_tables(places)
    grad_came = spread(grad_packed)
    first, second = attention(at, packs, dpacks, low, cosine, sine, heads, group)
    first, second, grad_came, input_packed = barrier((first, second, grad_came, input_packed))

    input_came = spread(input_packed)
    grads = [grad_own, grad_came[0], swap(grad_came[0], "tensor", 1)]
    grads += [grad_came[1], swap(grad_came[1], "tensor", 1)]
    grads[2], held = barrier((grads[2], grad_came[2]))
    grads += [held, swap(held, "tensor", 1)]
    edge = wide + narrow
    def summed(term):
        return lax.psum_scatter(term, "dp", scatter_dimension=0, tiled=True)

    parts = []
    term = weight_terms(at, [grads], [first], [(0, 0, 0, wide)], blocks, replicas, LOAD1)
    parts.append(summed(term))
    term, input_came, first, second = barrier((term, input_came, first, second))

    firsts = [first, swap(first, "context", 1), None, None]
    seconds = [second, None, swap(second, "context", 2), None]
    ins = joined(input_own, input_came)
    ins, parts[0] = barrier((ins, parts[0]))
    jobs = [(0, 0, wide, edge), (0, 1, 0, edge)]
    term = weight_terms(at, [ins], [first, second], jobs, blocks, replicas, LOAD2)
    parts.append(summed(term))
    term, firsts[1], seconds[2], first, second = barrier(
        (term, firsts[1], seconds[2], first, second)
    )
    seconds[1] = swap(second, "context", 1)
    firsts[2] = swap(first, "context", 2)
    jobs = [(0, 0, 0, wide), (1, 0, wide, edge), (1, 1, 0, edge)]

    def terms_of(source_first, source_second):
        lins = [firsts[source_first], seconds[source_second]]
        return weight_terms(at, [grads, ins], lins, jobs, blocks, replicas)

    term = terms_of(1, 2)
    parts.append(summed(term))
    term, firsts[1], firsts[2], seconds[1], seconds[2] = barrier(
        (term, firsts[1], firsts[2], seconds[1], seconds[2])
    )
    firsts[3] = swap(firsts[1], "context", 2)
    seconds[3] = swap(seconds[2], "context", 1)
    term = terms_of(2, 1)
    parts.append(summed(term))
    late, term = barrier((at, term))
    partial = input_first(
        late, firsts[:3], seconds[:3], w_query, w_key, w_value, count, wide, narrow
    )
    term, partial, parts[1], firsts[3], seconds[3] = barrier(
        (term, partial, parts[1], firsts[3], seconds[3])
    )
    mine, sent = input_last(
        at, 3, firsts[3], seconds[3], partial, w_query, w_key, w_value, wide, narrow
    )
    came = swap(sent, "tensor", 1)
    mine, firsts[3] = barrier((mine, firsts[3]))
    term = terms_of(3, 3)
    parts.append(summed(term))
    mine, came, parts[2], parts[3] = barrier((mine, came, parts[2], parts[3]))
    input_grad = (mine + came.astype(jnp.float32)).astype(jnp.bfloat16)
    last, input_grad = barrier((at, input_grad))

    def rest(source_first, source_second):
        return [(1, source_first, narrow), (2, source_second, wide), (3, source_second, narrow)]

    layout = [[(0, 0, wide)], rest(0, 0)]
    for source_first, source_second in ((1, 2), (2, 1), (3, 3)):
        layout.append([(0, source_first, wide)] + rest(source_first, source_second))
    near = assemble(last, layout[:-1], parts[:-1], blocks, wide, narrow)
    grad_output, grad_value, grad_query, grad_key = assemble_last(at, layout[-1], parts[-1], near)
    return (input_grad, grad_query, grad_key, grad_value, grad_output)


def solution(mesh):
    return jax.shard_map(
        on_device,
        mesh=mesh,
        in_specs=(
            P(("dp", "context"), None),
            P(("dp", "context"), "tensor"),
            P(("dp", "context"), "tensor"),
            P(("dp", "context"), "tensor"),
            P(("dp", "context"), None),
            P(("dp", "context")),
            P(None, "tensor"),
            P(None, "tensor"),
            P(None, "tensor"),
            P(None, "tensor"),
        ),
        out_specs=(
            P(("dp", "context", "tensor"), None),
            P(("dp", "context"), "tensor"),
            P(("dp", "context"), "tensor"),
            P(("dp", "context"), "tensor"),
            P(("dp", "context"), "tensor"),
        ),
        check_vma=False,
    )
```
